256 devices in a mesh: section: 2 (over core), ctx: 16 (over x, y), ch: 8 (over z).
Axes of the slice: x: 4, y: 4, z: 8, core: 2. Of those that a mesh axis runs over, the one named last changes fastest.
Arguments:
- mixer_input: bfloat16 [2, 3072, 16384], P('section', 'ctx', 'ch'), may hold values from -24 to 24
- gate_input: bfloat16 [2, 3072, 16384], P('section', 'ctx', 'ch'), may hold values from -6 to 6
- upstream_grad: bfloat16 [2, 3072, 16384], P('section', 'ctx', 'ch'), may hold values from -24 to 24
- x_weight: bfloat16 [2, 16384, 544], P('section', 'ch'), may hold values from -0.046875 to 0.046875
- step_weight: bfloat16 [2, 512, 16384], P('section', None, 'ch'), may hold values from -0.25 to 0.25
- step_bias: float32 [2, 16384], P('section', 'ch'), may hold values from -3 to 0
- decay_log: float32 [2, 16, 16384], P('section', None, 'ch'), may hold values from -9 to -2
- skip_gain: float32 [2, 16384], P('section', 'ch'), may hold values from 0.5 to 5
Outputs:
- handed_input: bfloat16 [2, 3072, 16384], P('section', 'ctx', 'ch')
- handed_gate: bfloat16 [2, 3072, 16384], P('section', 'ctx', 'ch')
- grad_x_weight: float32 [2, 16384, 544], P('section', ('ch', 'ctx'))
- grad_step_weight: float32 [2, 512, 16384], P('section', 'ctx', 'ch')
- grad_step_bias: float32 [2, 16384], P('section', 'ch')
- grad_decay_log: float32 [2, 16, 16384], P('section', None, 'ch')
- grad_skip_gain: float32 [2, 16384], P('section', 'ch')
The draws below stay inside these ranges and needn't reach their ends.
All inputs are finite; a program needn't handle non-finite values.
Results may differ from the reference program's by a relative error of at most 0.0045.
The reference program's roundings to bfloat16 on the way (of `step_low`, `pre_rounded` and `d_projected`) count: a program that leaves them out, or rounds other values in their place, can miss the bound.
Values may be sent and summed in bfloat16 or wider, within the bound.
A program may use at most 192 MiB of HBM per device.

```python
import math
import jax
import jax.numpy as jnp
from jax import lax

E = 16384
R = 512
N = 16
TOKENS = 3072
SECTIONS = 2


def ramp_field(key, spread):
    position = jnp.arange(TOKENS, dtype=jnp.float32) / TOKENS
    rising = jnp.exp(math.log(3.0) * position)[None, :, None]
    first, second = jax.random.split(key)
    scales = jnp.exp(jax.random.uniform(second, (SECTIONS, TOKENS, 1), jnp.float32, 0.0, spread))
    return (first, rising * scales)


def draw_mixer_input(key, part):
    key = jax.random.fold_in(key, 11)
    inner, factor = ramp_field(key, 0.0)
    base = jnp.clip(jax.random.normal(inner, (SECTIONS, TOKENS, E), jnp.float32), -6.0, 6.0)
    return (base * factor).astype(jnp.bfloat16)


def draw_upstream_grad(key, part):
    key = jax.random.fold_in(key, 23)
    inner, factor = ramp_field(key, 0.0)
    base = jnp.clip(jax.random.normal(inner, (SECTIONS, TOKENS, E), jnp.float32), -6.0, 6.0)
    return (base * factor).astype(jnp.bfloat16)


def level_of(rng, extent, cuts, low, high):
    def one(dim, parts):
        steps = jax.random.uniform(jax.random.fold_in(jax.random.fold_in(rng, 6), dim), (parts,), jnp.float32, low / len(cuts), high / len(cuts))
        return jnp.repeat(jnp.exp(steps), extent[dim] // parts).reshape((-1,) + (1,) * (len(extent) - dim - 1))

    level = one(*cuts[0])
    for cut in cuts[1:]:
        level = level * one(*cut)
    return level


def normal_values(own_key, extent, deviation, reach, shards=(), kind=jnp.bfloat16):
    result = deviation * jax.random.normal(own_key, extent, jnp.float32)
    if shards:
        result = result * level_of(own_key, extent, shards, -0.22, 0.18)
    return jnp.clip(result, -reach, reach).astype(kind)


def setup_inputs(seed: int = 0) -> dict:
    splits = jax.random.split(jax.random.key(seed), 9)
    return {
        "mixer_input": draw_mixer_input(jax.random.fold_in(splits[8], 71), 0),
        "gate_input": normal_values(splits[1], (SECTIONS, TOKENS, E), 1.0, 6.0, ((0, 2), (1, 16), (2, 8))),
        "upstream_grad": draw_upstream_grad(jax.random.fold_in(splits[8], 71), 0),
        "x_weight": normal_values(splits[3], (SECTIONS, E, R + 2 * N), E ** -0.5, 0.046875, ((0, 2), (1, 8))),
        "step_weight": normal_values(splits[4], (SECTIONS, R, E), R ** -0.5, 0.25, ((0, 2), (2, 8))),
        "step_bias": jnp.clip(-3.0 + 3.0 * jax.random.uniform(splits[5], (SECTIONS, E), jnp.float32) ** level_of(splits[5], (SECTIONS, E), ((0, 2), (1, 8)), -0.2, 0.2), -3.0, 0.0),
        "decay_log": jnp.clip(-9.0 + 7.0 * jax.random.uniform(splits[6], (SECTIONS, N, E), jnp.float32) ** level_of(splits[6], (SECTIONS, N, E), ((0, 2), (2, 8)), -0.2, 0.2), -9.0, -2.0),
        "skip_gain": jnp.clip(0.5 + 4.5 * jax.random.uniform(splits[7], (SECTIONS, E), jnp.float32) ** level_of(splits[7], (SECTIONS, E), ((0, 2), (1, 8)), -0.2, 0.2), 0.5, 5.0),
    }


def mixer_core(step_pre, in_mat, out_mat, signal, decay_log, skip_gain, gate):
    step_size = jax.nn.softplus(step_pre)
    rates = -jnp.exp(decay_log)
    span = math.gcd(TOKENS, 64)
    count = TOKENS // span

    def advance(hidden, inputs):
        step_row, in_row, out_row, signal_row = inputs
        hidden = jnp.exp(step_row[None, :] * rates) * hidden + (step_row * signal_row)[None, :] * in_row[:, None]
        return (hidden, lax.optimization_barrier(jnp.sum(out_row[:, None] * hidden, axis=0)))

    def run_block(hidden, inputs):
        return lax.scan(advance, hidden, inputs)
    inputs = tuple((member.reshape((count, span) + member.shape[1:]) for member in (step_size, in_mat, out_mat, signal)))
    start = jnp.zeros(rates.shape, jnp.float32)
    _, outputs = lax.scan(jax.checkpoint(run_block), start, inputs)
    scanned = outputs.reshape(TOKENS, rates.shape[1])
    mixed = scanned + skip_gain[None, :] * signal
    return mixed * jax.nn.silu(gate)

def section_grads(mixer_input, gate_input, upstream_grad, x_weight, step_weight, step_bias, decay_log, skip_gain):
    projected = jnp.dot(mixer_input, x_weight, preferred_element_type=jnp.float32)
    step_low = projected[:, :R].astype(jnp.bfloat16)
    in_mat = projected[:, R:R + N]
    out_mat = projected[:, R + N:]
    step_pre = jnp.dot(step_low, step_weight, preferred_element_type=jnp.float32) + step_bias[None, :]
    signal = mixer_input.astype(jnp.float32)
    gate = gate_input.astype(jnp.float32)
    _, pullback = jax.vjp(mixer_core, step_pre, in_mat, out_mat, signal, decay_log, skip_gain, gate)
    d_pre, d_in, d_out, d_signal, d_decay, d_skip, d_gate = pullback(upstream_grad.astype(jnp.float32))
    pre_rounded = d_pre.astype(jnp.bfloat16)
    d_low = lax.dot_general(pre_rounded, step_weight, (((1,), (1,)), ((), ())), preferred_element_type=jnp.float32)
    d_projected = jnp.concatenate([d_low, d_in, d_out], axis=1).astype(jnp.bfloat16)
    d_input = d_signal + lax.dot_general(d_projected, x_weight, (((1,), (1,)), ((), ())), preferred_element_type=jnp.float32)
    grad_x = lax.dot_general(mixer_input, d_projected, (((0,), (0,)), ((), ())), preferred_element_type=jnp.float32)
    grad_step = lax.dot_general(step_low, pre_rounded, (((0,), (0,)), ((), ())), preferred_element_type=jnp.float32)
    return (d_input.astype(jnp.bfloat16), d_gate.astype(jnp.bfloat16), grad_x, grad_step, lax.optimization_barrier(jnp.sum(d_pre, axis=0)), d_decay, d_skip)

def reference(mixer_input, gate_input, upstream_grad, x_weight, step_weight, step_bias, decay_log, skip_gain):
    results = []
    for section in range(SECTIONS):
        results.append(section_grads(mixer_input[section], gate_input[section], upstream_grad[section], x_weight[section], step_weight[section], step_bias[section], decay_log[section], skip_gain[section]))
    empty = jnp.zeros((TOKENS, E), jnp.bfloat16)
    handed_input = jnp.stack([results[section + 1][0] for section in range(SECTIONS - 1)] + [empty])
    handed_gate = jnp.stack([results[section + 1][1] for section in range(SECTIONS - 1)] + [empty])
    grad_x_weight = jnp.stack([member[2] for member in results])
    grad_step_weight = jnp.stack([member[3] for member in results])
    grad_step_bias = jnp.stack([member[4] for member in results])
    grad_decay_log = jnp.stack([member[5] for member in results])
    grad_skip_gain = jnp.stack([member[6] for member in results])
    return (handed_input, handed_gate, grad_x_weight, grad_step_weight, grad_step_bias, grad_decay_log, grad_skip_gain)
```

```python
import functools

import jax
import jax.numpy as jnp
from jax import lax
from jax.experimental import pallas as pl
from jax.experimental.pallas import tpu as pltpu
from jax.sharding import PartitionSpec as P

R = 512
N = 16
TOK = 192
STEPS = 24
ROWS = 8
TILE = 256
LANE = 128
HALVES = TILE // LANE
CHUNK = 4
LOG2E = 1.4426950408889634
VMEM_BYTES = 60 * 2**20
SIDE = 4
CTX = 16
CH = 8
PIECE = TOK // CH
WIDE = R + LANE
PACK = 40
SMALL = 24
MESH = pl.DeviceIdType.MESH
LN2 = 0.6931471805599453
F32 = jnp.float32
BF16 = jnp.bfloat16


def every(i):
    return pl.ds(i, ROWS, stride=STEPS)


def lanes(k):
    return slice(k * LANE, (k + 1) * LANE)


def by_lanes(ref, value):
    for k in range(HALVES):
        ref[k] = value[:, lanes(k)]


def joined(ref):
    return jnp.concatenate([ref[k] for k in range(HALVES)], axis=1)


def row_index():
    return lax.broadcasted_iota(jnp.int32, (ROWS, LANE), 0)


def spread_columns(io_ref, spread):
    def one(i, _):
        rows = io_ref[every(i), :]
        for n in range(2 * N):
            spread[i, n] = jnp.broadcast_to(rows[:, n : n + 1], (ROWS, LANE))
        return 0

    lax.fori_loop(0, STEPS, one, 0)


def scan_rows(decay, value, reverse):
    row = row_index()
    for k in (1, 2, 4):
        shift = ROWS - k if reverse else k
        inside = row < ROWS - k if reverse else row >= k
        value = value + decay * jnp.where(inside, pltpu.roll(value, shift, 0), 0.0)
        if k < 4:
            decay = decay * jnp.where(inside, pltpu.roll(decay, shift, 0), 1.0)
    return value


def first_pass(
    low_ref, io_ref, w_ref, bias_ref, dlog_ref, u_ref, z_ref, g_ref,
    step_ref, sig_ref, entry_ref, exit_ref, pack_ref, bsum_ref,
    spread, drive, seed, rates,
):
    @pl.when(pl.program_id(0) == 0)
    def _():
        spread_columns(io_ref, spread)

    pre = jnp.dot(low_ref[...], w_ref[...], preferred_element_type=F32) + bias_ref[...]
    step = jnp.maximum(pre, 0.0) + jnp.log1p(jnp.exp(-jnp.abs(pre)))
    sig_ref[...] = jax.nn.sigmoid(pre)
    z = z_ref[...].astype(F32)
    by_lanes(step_ref, step)
    by_lanes(drive, step * u_ref[...].astype(F32))
    by_lanes(seed, g_ref[...].astype(F32) * z * jax.nn.sigmoid(z))
    rates[...] = -LOG2E * jnp.exp(dlog_ref[...])
    row = row_index()

    total = jnp.zeros((ROWS, TILE), F32)
    for i in range(STEPS):
        total = total + jnp.concatenate([step_ref[k, every(i), :] for k in range(HALVES)], axis=1)
    bsum_ref[...] = total
    whole_sum = jnp.sum(total, axis=0, keepdims=True)
    for k in range(HALVES):
        pack_ref[k, 2 * N :, :] = jnp.broadcast_to(whole_sum[:, lanes(k)], (PACK - 2 * N, LANE))

    for c in range(N // CHUNK):
        pairs = [(n, k) for n in range(c * CHUNK, (c + 1) * CHUNK) for k in range(HALVES)]
        rate = [jnp.broadcast_to(rates[n : n + 1, lanes(k)], (ROWS, LANE)) for n, k in pairs]

        def one(i, carry):
            state, decay, start = carry
            st = [step_ref[k, every(i), :] for k in range(HALVES)]
            dr = [drive[k, every(i), :] for k in range(HALVES)]
            sd = [seed[k, every(i), :] for k in range(HALVES)]
            new_state, new_decay, new_start = [], [], []
            for p, (n, k) in enumerate(pairs):
                a = jnp.exp2(st[k] * rate[p])
                new_state.append(a * state[p] + dr[k] * spread[i, n])
                d = a * decay[p]
                new_decay.append(d)
                new_start.append(start[p] + d * (sd[k] * spread[i, N + n]))
            return tuple(new_state), tuple(new_decay), tuple(new_start)

        zero = tuple(jnp.zeros((ROWS, LANE), F32) for _ in pairs)
        ones = tuple(jnp.ones((ROWS, LANE), F32) for _ in pairs)
        state, decay, start = lax.fori_loop(0, STEPS, one, (zero, ones, zero), unroll=4)
        for p, (n, k) in enumerate(pairs):
            ends = scan_rows(decay[p], state[p], False)
            starts = scan_rows(decay[p], start[p], True)
            entry_ref[n, :, lanes(k)] = jnp.where(row >= 1, pltpu.roll(ends, 1, 0), 0.0)
            exit_ref[n, :, lanes(k)] = jnp.where(row < ROWS - 1, pltpu.roll(starts, ROWS - 1, 0), 0.0)
            pack_ref[k, n : n + 1, :] = ends[ROWS - 1 :, :]
            pack_ref[k, N + n : N + n + 1, :] = starts[:1, :]


def sum_before(value, reverse):
    row = lax.broadcasted_iota(jnp.int32, value.shape, 0)
    held = value
    for k in (1, 2, 4):
        shift = ROWS - k if reverse else k
        inside = row < ROWS - k if reverse else row >= k
        held = held + jnp.where(inside, pltpu.roll(held, shift, 0), 0.0)
    return held - value


def second_pass(
    low_ref, io_ref, w_ref, dlog_ref, skip_ref, u_ref, z_ref, g_ref, step_ref, sig_ref,
    entry_ref, exit_ref, bsum_ref, across_ref,
    dgate_ref, dsig_ref, part_ref, gstep_ref, small_ref,
    spread, sums, held, drive, seed, scanned, grad_drive, grad_decay, rates, by_token,
):
    tile = pl.program_id(0)

    @pl.when(tile == 0)
    def _():
        spread_columns(io_ref, spread)
        sums[...] = jnp.zeros_like(sums)
        part_ref[...] = jnp.zeros_like(part_ref)

    step = joined(step_ref)
    u = u_ref[...].astype(F32)
    z = z_ref[...].astype(F32)
    g = g_ref[...].astype(F32)
    gate_sig = jax.nn.sigmoid(z)
    by_lanes(drive, step * u)
    by_lanes(seed, g * z * gate_sig)
    rates[...] = -LOG2E * jnp.exp(dlog_ref[...])
    scanned[...] = jnp.zeros_like(scanned)
    grad_drive[...] = jnp.zeros_like(grad_drive)
    grad_decay[...] = jnp.zeros_like(grad_decay)
    prior = sum_before(bsum_ref[...], False)
    later = sum_before(bsum_ref[...], True)

    for c in range(N // CHUNK):
        numbers = range(c * CHUNK, (c + 1) * CHUNK)
        pairs = [(n, k) for n in numbers for k in range(HALVES)]
        rate = [jnp.broadcast_to(rates[n : n + 1, lanes(k)], (ROWS, LANE)) for n, k in pairs]

        def forward(i, state):
            st = [step_ref[k, every(i), :] for k in range(HALVES)]
            dr = [drive[k, every(i), :] for k in range(HALVES)]
            sd = [seed[k, every(i), :] for k in range(HALVES)]
            out = [scanned[k, every(i), :] for k in range(HALVES)]
            new = []
            for m, n in enumerate(numbers):
                b_in, b_out = spread[i, n], spread[i, N + n]
                d_out = sums[i, N + n]
                for k in range(HALVES):
                    p = m * HALVES + k
                    held[i, m, :, lanes(k)] = state[p]
                    now = jnp.exp2(st[k] * rate[p]) * state[p] + dr[k] * b_in
                    new.append(now)
                    out[k] = out[k] + b_out * now
                    d_out = d_out + sd[k] * now
                sums[i, N + n] = d_out
            for k in range(HALVES):
                scanned[k, every(i), :] = out[k]
            return tuple(new)

        state = tuple(
            entry_ref[n, :, lanes(k)]
            + jnp.exp2(prior[:, lanes(k)] * rate[p]) * across_ref[k, n : n + 1, :]
            for p, (n, k) in enumerate(pairs)
        )
        lax.fori_loop(0, STEPS, forward, state, unroll=4)

        def backward(j, carry):
            incoming, total = carry
            i = STEPS - 1 - j
            st = [step_ref[k, every(i), :] for k in range(HALVES)]
            dr = [drive[k, every(i), :] for k in range(HALVES)]
            sd = [seed[k, every(i), :] for k in range(HALVES)]
            g_drive = [grad_drive[k, every(i), :] for k in range(HALVES)]
            g_decay = [grad_decay[k, every(i), :] for k in range(HALVES)]
            new_in, new_total = [], []
            for m, n in enumerate(numbers):
                b_in, b_out = spread[i, n], spread[i, N + n]
                d_in = sums[i, n]
                for k in range(HALVES):
                    p = m * HALVES + k
                    adjoint = b_out * sd[k] + incoming[p]
                    passed = jnp.exp2(st[k] * rate[p]) * adjoint
                    pulled = passed * held[i, m, :, lanes(k)]
                    new_in.append(passed)
                    new_total.append(total[p] + pulled * st[k])
                    g_decay[k] = g_decay[k] + pulled * rate[p]
                    g_drive[k] = g_drive[k] + adjoint * b_in
                    d_in = d_in + adjoint * dr[k]
                sums[i, n] = d_in
            for k in range(HALVES):
                grad_drive[k, every(i), :] = g_drive[k]
                grad_decay[k, every(i), :] = g_decay[k]
            return tuple(new_in), tuple(new_total)

        incoming = tuple(
            exit_ref[n, :, lanes(k)]
            + jnp.exp2(later[:, lanes(k)] * rate[p]) * across_ref[k, N + n : N + n + 1, :]
            for p, (n, k) in enumerate(pairs)
        )
        zero = tuple(jnp.zeros((ROWS, LANE), F32) for _ in pairs)
        _, total = lax.fori_loop(0, STEPS, backward, (incoming, zero), unroll=4)
        for p, (n, k) in enumerate(pairs):
            small_ref[k, n : n + 1, :] = (
                jnp.sum(total[p], axis=0, keepdims=True) * rates[n : n + 1, lanes(k)] * LN2
            )

    skip = skip_ref[...]
    by_drive = joined(grad_drive)
    seeds = joined(seed)
    mixed = joined(scanned) + skip * u
    dgate_ref[...] = (g * mixed * gate_sig * (1.0 + z * (1.0 - gate_sig))).astype(BF16)
    dsig_ref[...] = by_drive * step + skip * seeds
    d_pre = (by_drive * u + joined(grad_decay) * LN2) * sig_ref[...]
    pre = d_pre.astype(BF16)
    bias_row = jnp.sum(d_pre, axis=0, keepdims=True)
    skip_row = jnp.sum(seeds * u, axis=0, keepdims=True)
    for k in range(HALVES):
        small_ref[k, N : N + 1, :] = bias_row[:, lanes(k)]
        small_ref[k, N + 1 : N + 2, :] = skip_row[:, lanes(k)]
        small_ref[k, N + 2 :, :] = jnp.zeros((SMALL - N - 2, LANE), F32)
    part_ref[:, :R] += lax.dot_general(
        pre, w_ref[...], (((1,), (1,)), ((), ())), preferred_element_type=F32
    )
    grad = lax.dot_general(
        low_ref[...], pre, (((0,), (0,)), ((), ())), preferred_element_type=F32
    ).astype(BF16)
    for x in range(SIDE):
        for y in range(SIDE):
            at = (x * SIDE + y) * 2 * 16
            gstep_ref[0, x, y // 2, y % 2] = grad[at : at + 16]
            gstep_ref[1, y, x // 2, x % 2] = grad[at + 16 : at + 32]

    @pl.when(tile == pl.num_programs(0) - 1)
    def _():
        column = lax.broadcasted_iota(jnp.int32, (ROWS, LANE), 1)

        def one(i, _):
            rows = jnp.zeros((ROWS, LANE), F32)
            for n in range(2 * N):
                rows = jnp.where(column == n, jnp.sum(sums[i, n], axis=1, keepdims=True), rows)
            by_token[every(i), :] = rows
            return 0

        lax.fori_loop(0, STEPS, one, 0)
        part_ref[:, R:] = by_token[...]


def whole(*shape):
    return pl.BlockSpec(shape, lambda j: (0,) * len(shape))


def tiled(*lead):
    return pl.BlockSpec(lead + (TILE,), lambda j: (0,) * len(lead) + (j,))


def stacked(rows):
    return pl.BlockSpec((HALVES, rows, LANE), lambda j: (j, 0, 0))


def run_first(low, io, weight, bias, dlog, u, z, g):
    ch = u.shape[1]
    f = lambda *s: jax.ShapeDtypeStruct(s, F32)
    return pl.pallas_call(
        first_pass,
        grid=(ch // TILE,),
        in_specs=[
            whole(TOK, R), whole(TOK, io.shape[1]), tiled(R), tiled(1), tiled(N),
            tiled(TOK), tiled(TOK), tiled(TOK),
        ],
        out_specs=[
            stacked(TOK), tiled(TOK), tiled(N, ROWS), tiled(N, ROWS), stacked(PACK), tiled(ROWS),
        ],
        out_shape=[
            f(ch // LANE, TOK, LANE), f(TOK, ch), f(N, ROWS, ch), f(N, ROWS, ch),
            f(ch // LANE, PACK, LANE), f(ROWS, ch),
        ],
        scratch_shapes=[
            pltpu.VMEM((STEPS, 2 * N, ROWS, LANE), F32),
            pltpu.VMEM((HALVES, TOK, LANE), F32),
            pltpu.VMEM((HALVES, TOK, LANE), F32),
            pltpu.VMEM((N, TILE), F32),
        ],
        compiler_params=pltpu.CompilerParams(vmem_limit_bytes=VMEM_BYTES),
        name="first_pass",
    )(low, io, weight, bias, dlog, u, z, g)


def run_second(low, io, weight, dlog, skip, u, z, g, step, sig, entry, leave, bsum, across):
    ch = u.shape[1]
    f = lambda *s: jax.ShapeDtypeStruct(s, F32)
    return pl.pallas_call(
        second_pass,
        grid=(ch // TILE,),
        in_specs=[
            whole(TOK, R), whole(TOK, io.shape[1]), tiled(R), tiled(N), tiled(1),
            tiled(TOK), tiled(TOK), tiled(TOK), stacked(TOK), tiled(TOK),
            tiled(N, ROWS), tiled(N, ROWS), tiled(ROWS), stacked(2 * N),
        ],
        out_specs=[
            tiled(TOK), tiled(TOK), whole(TOK, WIDE), tiled(2, SIDE, 2, 2, 16), stacked(SMALL),
        ],
        out_shape=[
            jax.ShapeDtypeStruct((TOK, ch), BF16), f(TOK, ch), f(TOK, WIDE),
            jax.ShapeDtypeStruct((2, SIDE, 2, 2, 16, ch), BF16), f(ch // LANE, SMALL, LANE),
        ],
        scratch_shapes=[
            pltpu.VMEM((STEPS, 2 * N, ROWS, LANE), F32),
            pltpu.VMEM((STEPS, 2 * N, ROWS, LANE), F32),
            pltpu.VMEM((STEPS, CHUNK, ROWS, TILE), F32),
        ]
        + [pltpu.VMEM((HALVES, TOK, LANE), F32)] * 5
        + [pltpu.VMEM((N, TILE), F32), pltpu.VMEM((TOK, LANE), F32)],
        compiler_params=pltpu.CompilerParams(vmem_limit_bytes=VMEM_BYTES),
        name="second_pass",
    )(low, io, weight, dlog, skip, u, z, g, step, sig, entry, leave, bsum, across)


def greet(partners):
    barrier = pltpu.get_barrier_semaphore()
    for partner in partners:
        pl.semaphore_signal(barrier, inc=1, device_id=partner, device_id_type=MESH)
    pl.semaphore_wait(barrier, len(partners))


def remote(src, dst, send, recv, to):
    return pltpu.make_async_remote_copy(
        src_ref=src, dst_ref=dst, send_sem=send, recv_sem=recv, device_id=to, device_id_type=MESH
    )


def others(axis, count):
    me = lax.axis_index(axis)
    return [{axis: lax.rem(me + d, count)} for d in range(1, count)]


def token_rows(owner):
    return pl.ds(pl.multiple_of(owner * PIECE, 8), PIECE)


def sum_start(part_ref, landed, send, recv):
    copies = []
    for d, to in enumerate(others("ch", CH)):
        copies.append(remote(part_ref.at[token_rows(to["ch"])], landed.at[d], send.at[d], recv.at[d], to))
        copies[-1].start()
    return copies


def sum_finish(copies, part_ref, landed):
    me = lax.axis_index("ch")
    for copy in copies:
        copy.wait_recv()
    total = part_ref[token_rows(me), :]
    for d in range(CH - 1):
        total = total + landed[d]
    return total


def share_start(total, low_all, io_all, send, recv):
    me = lax.axis_index("ch")
    low_all[me] = jnp.concatenate([total[:, : R // 2], total[:, R // 2 : R]], axis=0).astype(BF16)
    io_all[me] = total[:, R:]
    copies = []
    for d, to in enumerate(others("ch", CH)):
        copies.append(remote(low_all.at[me], low_all.at[me], send.at[0, d], recv.at[0, d], to))
        copies.append(remote(io_all.at[me], io_all.at[me], send.at[1, d], recv.at[1, d], to))
    for copy in copies:
        copy.start()
    return copies


def share_finish(copies, low_all, io_all, wide):
    for copy in copies:
        copy.wait_recv()
    for p in range(CH):
        both = low_all[p].astype(F32)
        rows = slice(p * PIECE, (p + 1) * PIECE)
        wide[rows, : R // 2] = both[:PIECE]
        wide[rows, R // 2 : R] = both[PIECE:]
        wide[rows, R:] = io_all[p]


SUM_SCRATCH = [
    pltpu.VMEM((CH - 1, PIECE, WIDE), F32),
    pltpu.VMEM((CH, 2 * PIECE, R // 2), BF16),
    pltpu.VMEM((CH, PIECE, LANE), F32),
    pltpu.VMEM((TOK, WIDE), F32),
    pltpu.SemaphoreType.DMA((CH - 1,)),
    pltpu.SemaphoreType.DMA((CH - 1,)),
    pltpu.SemaphoreType.DMA((2, CH - 1)),
    pltpu.SemaphoreType.DMA((2, CH - 1)),
]


def sum_projected(
    part_ref, low_ref, io_ref, landed, low_all, io_all, wide, sum_send, sum_recv, all_send, all_recv
):
    greet(others("ch", CH))
    sums = sum_start(part_ref, landed, sum_send, sum_recv)
    shares = share_start(sum_finish(sums, part_ref, landed), low_all, io_all, all_send, all_recv)
    share_finish(shares, low_all, io_all, wide)
    low_ref[...] = wide[:, :R].astype(BF16)
    io_ref[...] = wide[:, R:]
    for copy in sums + shares:
        copy.wait_send()


def in_vmem(count):
    return [pl.BlockSpec(memory_space=pltpu.VMEM)] * count


def run_sum(part):
    return pl.pallas_call(
        sum_projected,
        in_specs=in_vmem(1),
        out_specs=in_vmem(2),
        out_shape=[jax.ShapeDtypeStruct((TOK, R), BF16), jax.ShapeDtypeStruct((TOK, LANE), F32)],
        scratch_shapes=SUM_SCRATCH,
        compiler_params=pltpu.CompilerParams(
            collective_id=0, has_side_effects=True, vmem_limit_bytes=VMEM_BYTES
        ),
        name="sum_projected",
    )(part)


def spread_start(src, dst, send, recv):
    me = lax.axis_index("ctx")
    copies = []
    for d, to in enumerate(others("ctx", CTX)):
        copies.append(remote(src.at[to["ctx"]], dst.at[me], send.at[d], recv.at[d], to))
        copies[-1].start()
    dst[me] = src[me]
    return copies


def exchange(pack_ref, dlog_ref, out_ref, landed, back, result, send, recv, back_send, back_recv):
    me = lax.axis_index("ctx")
    greet(others("ctx", CTX))
    there = spread_start(pack_ref, landed, send, recv)
    rates = -jnp.exp(dlog_ref[:, pl.ds(pl.multiple_of(me * LANE, LANE), LANE)])
    for copy in there:
        copy.wait_recv()
    state = jnp.zeros((N, LANE), F32)
    adjoint = jnp.zeros((N, LANE), F32)
    for c in range(CTX):
        r = CTX - 1 - c
        back[c, :N] = state
        back[r, N:] = adjoint
        state = jnp.exp(landed[c, 2 * N : 2 * N + 1] * rates) * state + landed[c, :N]
        adjoint = jnp.exp(landed[r, 2 * N : 2 * N + 1] * rates) * adjoint + landed[r, N : 2 * N]
    home = spread_start(back, result, back_send, back_recv)
    for copy in home:
        copy.wait_recv()
    out_ref[...] = result[...]
    for copy in there + home:
        copy.wait_send()


def run_exchange(pack, dlog):
    return pl.pallas_call(
        exchange,
        in_specs=in_vmem(2),
        out_specs=pl.BlockSpec(memory_space=pltpu.VMEM),
        out_shape=jax.ShapeDtypeStruct((CTX, 2 * N, LANE), F32),
        scratch_shapes=[
            pltpu.VMEM((CTX, PACK, LANE), F32),
            pltpu.VMEM((CTX, 2 * N, LANE), F32),
            pltpu.VMEM((CTX, 2 * N, LANE), F32),
        ]
        + [pltpu.SemaphoreType.DMA((CTX - 1,))] * 4,
        compiler_params=pltpu.CompilerParams(
            collective_id=1, has_side_effects=True, vmem_limit_bytes=VMEM_BYTES
        ),
        name="exchange",
    )(pack, dlog)


def neighbour(axis, d):
    me = lax.axis_index("ctx")
    x, y = me // SIDE, lax.rem(me, SIDE)
    if axis == 0:
        return {"ctx": lax.rem(x + d + SIDE, SIDE) * SIDE + y}
    return {"ctx": x * SIDE + lax.rem(y + d + SIDE, SIDE)}


def place(axis, d=0):
    me = lax.axis_index("ctx")
    at = me // SIDE if axis == 0 else lax.rem(me, SIDE)
    return lax.rem(at + d + SIDE, SIDE)


WAYS = ((0, 1, 0), (1, -1, 1))


def ring_start(axis, src, relay, land, send, recv):
    passing, direct = [], []
    for way, d, half in WAYS:
        to = neighbour(axis, d)
        passing.append(remote(src.at[place(axis, 2), half], relay.at[way], send.at[0, way], recv.at[0, way], to))
        direct.append(
            remote(src.at[place(axis, d), 1 - half], land.at[way, 1 - half], send.at[1, way], recv.at[1, way], to)
        )
        passing[-1].start()
    for copy in direct:
        copy.start()
    return passing, direct


def ring_middle(axis, src, relay, land, send, recv, copies):
    passing, direct = copies
    last = []
    for way, d, half in WAYS:
        passing[way].wait_recv()
        mine = src[place(axis, d), half]
        relay[way] = (relay[way].astype(F32) + mine.astype(F32)).astype(BF16)
        last.append(
            remote(relay.at[way], land.at[way, half], send.at[2, way], recv.at[2, way], neighbour(axis, d))
        )
        last[-1].start()
    return passing, direct, last


def ring_finish(axis, src, land, copies):
    _, direct, last = copies
    for copy in direct + last:
        copy.wait_recv()
    mine = place(axis)
    return [
        src[mine, h].astype(F32) + land[0, h].astype(F32) + land[1, h].astype(F32) for h in range(2)
    ]


def ring_done(copies):
    for group in copies:
        for copy in group:
            copy.wait_send()


def ring_scratch(unit, second):
    return [
        pltpu.VMEM((2, 2) + unit, BF16),
        pltpu.VMEM((2, 2, 2) + unit, BF16),
        pltpu.VMEM((2, SIDE, 2) + second, BF16),
        pltpu.VMEM((2, 2) + second, BF16),
        pltpu.VMEM((2, 2, 2) + second, BF16),
        pltpu.SemaphoreType.DMA((2, 3, 2)),
        pltpu.SemaphoreType.DMA((2, 3, 2)),
        pltpu.SemaphoreType.DMA((2, 3, 2)),
        pltpu.SemaphoreType.DMA((2, 3, 2)),
    ]


STEP_UNIT, STEP_SECOND = (2, 16, 2048), (16, 1024)
X_UNIT, X_SECOND = (2, 64, R + 2 * N), (32, R + 2 * N)


def plane_start(src, scratch):
    relay, land, _, _, _, send, recv, _, _ = scratch
    return [
        ring_start(q, src.at[q], relay.at[q], land.at[q], send.at[q], recv.at[q]) for q in range(2)
    ]


def plane_middle(src, scratch, copies):
    relay, land, _, _, _, send, recv, _, _ = scratch
    return [
        ring_middle(q, src.at[q], relay.at[q], land.at[q], send.at[q], recv.at[q], copies[q]) for q in range(2)
    ]


def plane_turn(src, scratch, copies, split):
    _, land, second, relay, land2, _, _, send, recv = scratch
    started = []
    for q in range(2):
        halves = ring_finish(q, src.at[q], land.at[q], copies[q])
        for o in range(SIDE):
            for h in range(2):
                second[q, o, h] = split(halves[o // 2][o % 2], h).astype(BF16)
        started.append(
            ring_start(1 - q, second.at[q], relay.at[q], land2.at[q], send.at[q], recv.at[q])
        )
    return started


def plane_second_middle(scratch, copies):
    _, _, second, relay, land, _, _, send, recv = scratch
    return [
        ring_middle(1 - q, second.at[q], relay.at[q], land.at[q], send.at[q], recv.at[q], copies[q])
        for q in range(2)
    ]


def plane_finish(scratch, copies):
    second, land = scratch[2], scratch[4]
    return [ring_finish(1 - q, second.at[q], land.at[q], copies[q]) for q in range(2)]


def tail(
    part_ref, small_in, dgate_ref, step_grad, u_ref, xw_ref, dsig_ref,
    hin_ref, hgate_ref, gx_ref, gstep_ref, small_ref,
    landed, low_all, io_all, wide, sum_send, sum_recv, all_send, all_recv,
    small_land, small_back, small_all, s_send, s_recv, t_send, t_recv,
    gate_land, in_out, in_land, hand_send, hand_recv, proj, x_grad, *rings,
):
    step_ring, x_ring = rings[:9], rings[9:]
    section = lax.axis_index("section")
    me = lax.axis_index("ctx")
    greet(others("ctx", CTX) + others("ch", CH) + [{"section": 1 - section}])
    gate_copy = remote(dgate_ref, gate_land, hand_send.at[0], hand_recv.at[0], {"section": 1 - section})
    in_copy = remote(in_out, in_land, hand_send.at[1], hand_recv.at[1], {"section": 1 - section})

    sums = sum_start(part_ref, landed, sum_send, sum_recv)
    first = plane_start(step_grad, step_ring)

    @pl.when(section == 1)
    def _():
        gate_copy.start()

    small_there = spread_start(small_in, small_land, s_send, s_recv)
    shares = share_start(sum_finish(sums, part_ref, landed), low_all, io_all, all_send, all_recv)
    first = plane_middle(step_grad, step_ring, first)
    for copy in small_there:
        copy.wait_recv()
    total = small_land[0]
    for c in range(1, CTX):
        total = total + small_land[c]
    small_all[me] = total
    small_home = []
    for d, to in enumerate(others("ctx", CTX)):
        small_home.append(remote(small_all.at[me], small_all.at[me], t_send.at[d], t_recv.at[d], to))
        small_home[-1].start()

    share_finish(shares, low_all, io_all, wide)
    proj[...] = wide[...].astype(BF16)

    def product(c, _):
        columns = pl.ds(pl.multiple_of(c * LANE, LANE), LANE)
        grad = lax.dot_general(
            u_ref[:, columns], proj[...], (((0,), (0,)), ((), ())), preferred_element_type=F32
        )[:, : R + 2 * N].astype(BF16)
        x, y = c // SIDE, lax.rem(c, SIDE)
        x_grad[0, x, y // 2, lax.rem(y, 2)] = grad[:64]
        x_grad[1, y, x // 2, lax.rem(x, 2)] = grad[64:]
        return 0

    lax.fori_loop(0, CTX, product, 0)
    first_x = plane_start(x_grad, x_ring)

    @pl.when(section == 1)
    def _():
        def one(j, _):
            columns = pl.ds(pl.multiple_of(j * TILE, TILE), TILE)
            in_out[:, columns] = (
                dsig_ref[:, columns]
                + lax.dot_general(
                    proj[:, : R + 2 * N], xw_ref[columns, :], (((1,), (1,)), ((), ())),
                    preferred_element_type=F32,
                )
            ).astype(BF16)
            return 0

        lax.fori_loop(0, u_ref.shape[1] // TILE, one, 0)
        in_copy.start()
        hin_ref[...] = jnp.zeros_like(hin_ref)
        hgate_ref[...] = jnp.zeros_like(hgate_ref)

    turned = plane_turn(step_grad, step_ring, first, lambda v, h: v[:, h * 1024 : (h + 1) * 1024])
    first_x = plane_middle(x_grad, x_ring, first_x)
    turned = plane_second_middle(step_ring, turned)
    for copy in small_home:
        copy.wait_recv()
    for c in range(CTX):
        small_ref[:, lanes(c)] = small_all[c]
    for q, halves in enumerate(plane_finish(step_ring, turned)):
        for h in range(2):
            gstep_ref[q * 16 : (q + 1) * 16, h * 1024 : (h + 1) * 1024] = halves[h]
    turned_x = plane_turn(x_grad, x_ring, first_x, lambda v, h: v[h * 32 : (h + 1) * 32])

    @pl.when(section == 0)
    def _():
        gate_copy.wait_recv()
        in_copy.wait_recv()
        hgate_ref[...] = gate_land[...]
        hin_ref[...] = in_land[...]

    turned_x = plane_second_middle(x_ring, turned_x)
    for q, halves in enumerate(plane_finish(x_ring, turned_x)):
        for h in range(2):
            gx_ref[q * 64 + h * 32 : q * 64 + (h + 1) * 32, :] = halves[h]

    @pl.when(section == 1)
    def _():
        gate_copy.wait_send()
        in_copy.wait_send()

    for copy in sums + shares + small_there + small_home:
        copy.wait_send()
    for copies in first + turned + first_x + turned_x:
        ring_done(copies)


def run_tail(part, small, dgate, step_grad, u, xw, dsig):
    ch = u.shape[1]
    f = lambda *s: jax.ShapeDtypeStruct(s, F32)
    b = lambda *s: jax.ShapeDtypeStruct(s, BF16)
    return pl.pallas_call(
        tail,
        in_specs=in_vmem(7),
        out_specs=in_vmem(5),
        out_shape=[b(TOK, ch), b(TOK, ch), f(LANE, R + 2 * N), f(32, ch), f(SMALL, ch)],
        scratch_shapes=SUM_SCRATCH
        + [pltpu.VMEM((CTX, SMALL, LANE), F32)] * 3
        + [pltpu.SemaphoreType.DMA((CTX - 1,))] * 4
        + [pltpu.VMEM((TOK, ch), BF16)] * 3
        + [pltpu.SemaphoreType.DMA((2,))] * 2
        + [pltpu.VMEM((TOK, WIDE), BF16), pltpu.VMEM((2, SIDE, 2, 2, 64, R + 2 * N), BF16)]
        + ring_scratch(STEP_UNIT, STEP_SECOND)
        + ring_scratch(X_UNIT, X_SECOND),
        compiler_params=pltpu.CompilerParams(
            collective_id=2, has_side_effects=True, vmem_limit_bytes=VMEM_BYTES
        ),
        name="tail",
    )(part, small, dgate, step_grad, u, xw, dsig)


def body(mixer_input, gate_input, upstream_grad, x_weight, step_weight, step_bias, decay_log, skip_gain):
    u, z, g = mixer_input[0], gate_input[0], upstream_grad[0]
    weight_x, weight_step = x_weight[0], step_weight[0]
    dlog = decay_log[0]
    part = jnp.dot(u, weight_x, preferred_element_type=F32)
    low, io = run_sum(jnp.pad(part, ((0, 0), (0, LANE - 2 * N))))
    step, sig, entry, leave, pack, bsum = run_first(low, io, weight_step, step_bias, dlog, u, z, g)
    across = run_exchange(pack, dlog)
    d_gate, d_signal, d_part, grad_step, small = run_second(
        low, io, weight_step, dlog, skip_gain, u, z, g, step, sig, entry, leave, bsum, across
    )
    handed_input, handed_gate, grad_x, grad_step, small = run_tail(
        d_part, small, d_gate, grad_step, u, weight_x, d_signal
    )
    return (
        handed_input[None], handed_gate[None], grad_x[None], grad_step[None],
        small[N : N + 1], small[None, :N], small[N + 1 : N + 2],
    )


def solution(mesh):
    return jax.shard_map(
        body,
        mesh=mesh,
        in_specs=(
            P("section", "ctx", "ch"), P("section", "ctx", "ch"), P("section", "ctx", "ch"),
            P("section", "ch", None), P("section", None, "ch"), P("section", "ch"),
            P("section", None, "ch"), P("section", "ch"),
        ),
        out_specs=(
            P("section", "ctx", "ch"), P("section", "ctx", "ch"), P("section", ("ch", "ctx"), None),
            P("section", "ctx", "ch"), P("section", "ch"), P("section", None, "ch"), P("section", "ch"),
        ),
        check_vma=False,
    )
```

```python
import functools

import jax
import jax.numpy as jnp
from jax import lax
from jax.experimental import pallas as pl
from jax.experimental.pallas import tpu as pltpu
from jax.sharding import PartitionSpec as P

R = 512
N = 16
TOK = 192
STEPS = 24
ROWS = 8
TILE = 256
LANE = 128
HALVES = TILE // LANE
CHUNK = 4
LOG2E = 1.4426950408889634
VMEM_BYTES = 60 * 2**20
SIDE = 4
CTX = 16
CH = 8
PIECE = TOK // CH
WIDE = R + LANE
PACK = 40
SMALL = 24
MESH = pl.DeviceIdType.MESH
LN2 = 0.6931471805599453
F32 = jnp.float32
BF16 = jnp.bfloat16


def every(i):
    return pl.ds(i, ROWS, stride=STEPS)


def lanes(k):
    return slice(k * LANE, (k + 1) * LANE)


def by_step(ref, value, by_token):
    for k in range(HALVES):
        by_token[k] = value[:, lanes(k)]
        for i in range(STEPS):
            ref[k, i] = by_token[k, every(i), :]


def from_step(ref, by_token):
    for k in range(HALVES):
        for i in range(STEPS):
            by_token[k, every(i), :] = ref[k, i]
    return jnp.concatenate([by_token[k] for k in range(HALVES)], axis=1)


def row_index():
    return lax.broadcasted_iota(jnp.int32, (ROWS, LANE), 0)


def spread_columns(io_ref, spread):
    def one(i, _):
        rows = io_ref[every(i), :]
        for n in range(2 * N):
            spread[i, n] = jnp.broadcast_to(rows[:, n : n + 1], (ROWS, LANE))
        return 0

    lax.fori_loop(0, STEPS, one, 0)


def scan_rows(decay, value, reverse):
    row = row_index()
    for k in (1, 2, 4):
        shift = ROWS - k if reverse else k
        inside = row < ROWS - k if reverse else row >= k
        value = value + decay * jnp.where(inside, pltpu.roll(value, shift, 0), 0.0)
        if k < 4:
            decay = decay * jnp.where(inside, pltpu.roll(decay, shift, 0), 1.0)
    return value


def first_pass(
    low_ref, io_ref, w_ref, bias_ref, dlog_ref, u_ref, z_ref, g_ref,
    step_ref, token_ref, sig_ref, drive, seed, entry_ref, exit_ref, pack_ref, bsum_ref,
    spread, by_drive, by_seed, by_step_size, rates,
):
    @pl.when(pl.program_id(0) == 0)
    def _():
        spread_columns(io_ref, spread)

    pre = jnp.dot(low_ref[...], w_ref[...], preferred_element_type=F32) + bias_ref[...]
    step = jnp.maximum(pre, 0.0) + jnp.log1p(jnp.exp(-jnp.abs(pre)))
    sig_ref[...] = jax.nn.sigmoid(pre)
    z = z_ref[...].astype(F32)
    token_ref[...] = step
    by_step(step_ref, step, by_step_size)
    by_step(drive, step * u_ref[...].astype(F32), by_drive)
    by_step(seed, g_ref[...].astype(F32) * z * jax.nn.sigmoid(z), by_seed)
    rates[...] = -LOG2E * jnp.exp(dlog_ref[...])
    row = row_index()

    total = jnp.zeros((ROWS, TILE), F32)
    for i in range(STEPS):
        total = total + jnp.concatenate([step_ref[k, i] for k in range(HALVES)], axis=1)
    bsum_ref[...] = total
    whole_sum = jnp.sum(total, axis=0, keepdims=True)
    for k in range(HALVES):
        pack_ref[k, 2 * N :, :] = jnp.broadcast_to(whole_sum[:, lanes(k)], (PACK - 2 * N, LANE))

    for c in range(N // CHUNK):
        pairs = [(n, k) for n in range(c * CHUNK, (c + 1) * CHUNK) for k in range(HALVES)]
        rate = [jnp.broadcast_to(rates[n : n + 1, lanes(k)], (ROWS, LANE)) for n, k in pairs]

        def one(i, carry):
            state, decay, start = carry
            st = [step_ref[k, i] for k in range(HALVES)]
            dr = [drive[k, i] for k in range(HALVES)]
            sd = [seed[k, i] for k in range(HALVES)]
            new_state, new_decay, new_start = [], [], []
            for p, (n, k) in enumerate(pairs):
                a = jnp.exp2(st[k] * rate[p])
                new_state.append(a * state[p] + dr[k] * spread[i, n])
                d = a * decay[p]
                new_decay.append(d)
                new_start.append(start[p] + d * (sd[k] * spread[i, N + n]))
            return tuple(new_state), tuple(new_decay), tuple(new_start)

        zero = tuple(jnp.zeros((ROWS, LANE), F32) for _ in pairs)
        ones = tuple(jnp.ones((ROWS, LANE), F32) for _ in pairs)
        state, decay, start = lax.fori_loop(0, STEPS, one, (zero, ones, zero), unroll=4)
        for p, (n, k) in enumerate(pairs):
            ends = scan_rows(decay[p], state[p], False)
            starts = scan_rows(decay[p], start[p], True)
            entry_ref[n, :, lanes(k)] = jnp.where(row >= 1, pltpu.roll(ends, 1, 0), 0.0)
            exit_ref[n, :, lanes(k)] = jnp.where(row < ROWS - 1, pltpu.roll(starts, ROWS - 1, 0), 0.0)
            pack_ref[k, n : n + 1, :] = ends[ROWS - 1 :, :]
            pack_ref[k, N + n : N + n + 1, :] = starts[:1, :]


def sum_before(value, reverse):
    row = lax.broadcasted_iota(jnp.int32, value.shape, 0)
    held = value
    for k in (1, 2, 4):
        shift = ROWS - k if reverse else k
        inside = row < ROWS - k if reverse else row >= k
        held = held + jnp.where(inside, pltpu.roll(held, shift, 0), 0.0)
    return held - value


def second_pass(
    low_ref, io_ref, w_ref, dlog_ref, skip_ref, u_ref, z_ref, g_ref, step_ref, token_ref, sig_ref, drive, seed,
    entry_ref, exit_ref, bsum_ref, across_ref,
    dgate_ref, dsig_ref, part_ref, gstep_ref, small_ref,
    spread, sums, held, scanned, grad_drive, grad_decay, by_scan, by_grad, by_decay, rates, by_token,
):
    tile = pl.program_id(0)

    @pl.when(tile == 0)
    def _():
        spread_columns(io_ref, spread)
        sums[...] = jnp.zeros_like(sums)
        part_ref[...] = jnp.zeros_like(part_ref)

    rates[...] = -LOG2E * jnp.exp(dlog_ref[...])
    scanned[...] = jnp.zeros_like(scanned)
    grad_drive[...] = jnp.zeros_like(grad_drive)
    grad_decay[...] = jnp.zeros_like(grad_decay)
    prior = sum_before(bsum_ref[...], False)
    later = sum_before(bsum_ref[...], True)

    for c in range(N // CHUNK):
        numbers = range(c * CHUNK, (c + 1) * CHUNK)
        pairs = [(n, k) for n in numbers for k in range(HALVES)]
        rate = [jnp.broadcast_to(rates[n : n + 1, lanes(k)], (ROWS, LANE)) for n, k in pairs]

        def forward(i, state):
            st = [step_ref[k, i] for k in range(HALVES)]
            dr = [drive[k, i] for k in range(HALVES)]
            sd = [seed[k, i] for k in range(HALVES)]
            out = [scanned[k, i] for k in range(HALVES)]
            new = []
            for m, n in enumerate(numbers):
                b_in, b_out = spread[i, n], spread[i, N + n]
                d_out = sums[i, N + n]
                for k in range(HALVES):
                    p = m * HALVES + k
                    held[i, m, :, lanes(k)] = state[p]
                    now = jnp.exp2(st[k] * rate[p]) * state[p] + dr[k] * b_in
                    new.append(now)
                    out[k] = out[k] + b_out * now
                    d_out = d_out + sd[k] * now
                sums[i, N + n] = d_out
            for k in range(HALVES):
                scanned[k, i] = out[k]
            return tuple(new)

        state = tuple(
            entry_ref[n, :, lanes(k)]
            + jnp.exp2(prior[:, lanes(k)] * rate[p]) * across_ref[k, n : n + 1, :]
            for p, (n, k) in enumerate(pairs)
        )
        lax.fori_loop(0, STEPS, forward, state, unroll=4)

        def backward(j, carry):
            incoming, total = carry
            i = STEPS - 1 - j
            st = [step_ref[k, i] for k in range(HALVES)]
            dr = [drive[k, i] for k in range(HALVES)]
            sd = [seed[k, i] for k in range(HALVES)]
            g_drive = [grad_drive[k, i] for k in range(HALVES)]
            g_decay = [grad_decay[k, i] for k in range(HALVES)]
            new_in, new_total = [], []
            for m, n in enumerate(numbers):
                b_in, b_out = spread[i, n], spread[i, N + n]
                d_in = sums[i, n]
                for k in range(HALVES):
                    p = m * HALVES + k
                    adjoint = b_out * sd[k] + incoming[p]
                    passed = jnp.exp2(st[k] * rate[p]) * adjoint
                    pulled = passed * held[i, m, :, lanes(k)]
                    new_in.append(passed)
                    new_total.append(total[p] + pulled * st[k])
                    g_decay[k] = g_decay[k] + pulled * rate[p]
                    g_drive[k] = g_drive[k] + adjoint * b_in
                    d_in = d_in + adjoint * dr[k]
                sums[i, n] = d_in
            for k in range(HALVES):
                grad_drive[k, i] = g_drive[k]
                grad_decay[k, i] = g_decay[k]
            return tuple(new_in), tuple(new_total)

        incoming = tuple(
            exit_ref[n, :, lanes(k)]
            + jnp.exp2(later[:, lanes(k)] * rate[p]) * across_ref[k, N + n : N + n + 1, :]
            for p, (n, k) in enumerate(pairs)
        )
        zero = tuple(jnp.zeros((ROWS, LANE), F32) for _ in pairs)
        _, total = lax.fori_loop(0, STEPS, backward, (incoming, zero), unroll=4)
        for p, (n, k) in enumerate(pairs):
            small_ref[k, n : n + 1, :] = (
                jnp.sum(total[p], axis=0, keepdims=True) * rates[n : n + 1, lanes(k)] * LN2
            )

    u = u_ref[...].astype(F32)
    z = z_ref[...].astype(F32)
    g = g_ref[...].astype(F32)
    gate_sig = jax.nn.sigmoid(z)
    seeds = g * z * gate_sig
    skip = skip_ref[...]
    from_drive = from_step(grad_drive, by_grad)
    mixed = from_step(scanned, by_scan) + skip * u
    dgate_ref[...] = (g * mixed * gate_sig * (1.0 + z * (1.0 - gate_sig))).astype(BF16)
    dsig_ref[...] = from_drive * token_ref[...] + skip * seeds
    d_pre = (from_drive * u + from_step(grad_decay, by_decay) * LN2) * sig_ref[...]
    pre = d_pre.astype(BF16)
    bias_row = jnp.sum(d_pre, axis=0, keepdims=True)
    skip_row = jnp.sum(seeds * u, axis=0, keepdims=True)
    for k in range(HALVES):
        small_ref[k, N : N + 1, :] = bias_row[:, lanes(k)]
        small_ref[k, N + 1 : N + 2, :] = skip_row[:, lanes(k)]
        small_ref[k, N + 2 :, :] = jnp.zeros((SMALL - N - 2, LANE), F32)
    part_ref[:, :R] += lax.dot_general(
        pre, w_ref[...], (((1,), (1,)), ((), ())), preferred_element_type=F32
    )
    grad = lax.dot_general(
        low_ref[...], pre, (((0,), (0,)), ((), ())), preferred_element_type=F32
    ).astype(BF16)
    for x in range(SIDE):
        for y in range(SIDE):
            at = (x * SIDE + y) * 2 * 16
            gstep_ref[0, x, y // 2, y % 2] = grad[at : at + 16]
            gstep_ref[1, y, x // 2, x % 2] = grad[at + 16 : at + 32]

    @pl.when(tile == pl.num_programs(0) - 1)
    def _():
        column = lax.broadcasted_iota(jnp.int32, (ROWS, LANE), 1)

        def one(i, _):
            rows = jnp.zeros((ROWS, LANE), F32)
            for n in range(2 * N):
                rows = jnp.where(column == n, jnp.sum(sums[i, n], axis=1, keepdims=True), rows)
            by_token[every(i), :] = rows
            return 0

        lax.fori_loop(0, STEPS, one, 0)
        part_ref[:, R:] = by_token[...]


def whole(*shape):
    return pl.BlockSpec(shape, lambda j: (0,) * len(shape))


def tiled(*lead):
    return pl.BlockSpec(lead + (TILE,), lambda j: (0,) * len(lead) + (j,))


def stacked(*rows):
    return pl.BlockSpec((HALVES,) + rows + (LANE,), lambda j: (j,) + (0,) * (len(rows) + 1))


def run_first(low, io, weight, bias, dlog, u, z, g):
    ch = u.shape[1]
    f = lambda *s: jax.ShapeDtypeStruct(s, F32)
    return pl.pallas_call(
        first_pass,
        grid=(ch // TILE,),
        in_specs=[
            whole(TOK, R), whole(TOK, io.shape[1]), tiled(R), tiled(1), tiled(N),
            tiled(TOK), tiled(TOK), tiled(TOK),
        ],
        out_specs=[
            stacked(STEPS, ROWS), tiled(TOK), tiled(TOK), stacked(STEPS, ROWS), stacked(STEPS, ROWS),
            tiled(N, ROWS), tiled(N, ROWS), stacked(PACK), tiled(ROWS),
        ],
        out_shape=[
            f(ch // LANE, STEPS, ROWS, LANE), f(TOK, ch), f(TOK, ch), f(ch // LANE, STEPS, ROWS, LANE),
            f(ch // LANE, STEPS, ROWS, LANE), f(N, ROWS, ch), f(N, ROWS, ch),
            f(ch // LANE, PACK, LANE), f(ROWS, ch),
        ],
        scratch_shapes=[
            pltpu.VMEM((STEPS, 2 * N, ROWS, LANE), F32),
            pltpu.VMEM((HALVES, TOK, LANE), F32),
            pltpu.VMEM((HALVES, TOK, LANE), F32),
            pltpu.VMEM((HALVES, TOK, LANE), F32),
            pltpu.VMEM((N, TILE), F32),
        ],
        compiler_params=pltpu.CompilerParams(vmem_limit_bytes=VMEM_BYTES),
        name="first_pass",
    )(low, io, weight, bias, dlog, u, z, g)


def run_second(low, io, weight, dlog, skip, u, z, g, kept, across):
    ch = u.shape[1]
    f = lambda *s: jax.ShapeDtypeStruct(s, F32)
    return pl.pallas_call(
        second_pass,
        grid=(ch // TILE,),
        in_specs=[
            whole(TOK, R), whole(TOK, io.shape[1]), tiled(R), tiled(N), tiled(1),
            tiled(TOK), tiled(TOK), tiled(TOK), stacked(STEPS, ROWS), tiled(TOK), tiled(TOK),
            stacked(STEPS, ROWS), stacked(STEPS, ROWS), tiled(N, ROWS), tiled(N, ROWS), tiled(ROWS), stacked(2 * N),
        ],
        out_specs=[
            tiled(TOK), tiled(TOK), whole(TOK, WIDE), tiled(2, SIDE, 2, 2, 16), stacked(SMALL),
        ],
        out_shape=[
            jax.ShapeDtypeStruct((TOK, ch), BF16), f(TOK, ch), f(TOK, WIDE),
            jax.ShapeDtypeStruct((2, SIDE, 2, 2, 16, ch), BF16), f(ch // LANE, SMALL, LANE),
        ],
        scratch_shapes=[
            pltpu.VMEM((STEPS, 2 * N, ROWS, LANE), F32),
            pltpu.VMEM((STEPS, 2 * N, ROWS, LANE), F32),
            pltpu.VMEM((STEPS, CHUNK, ROWS, TILE), F32),
        ]
        + [pltpu.VMEM((HALVES, STEPS, ROWS, LANE), F32)] * 3
        + [pltpu.VMEM((HALVES, TOK, LANE), F32)] * 3
        + [pltpu.VMEM((N, TILE), F32), pltpu.VMEM((TOK, LANE), F32)],
        compiler_params=pltpu.CompilerParams(vmem_limit_bytes=VMEM_BYTES),
        name="second_pass",
    )(low, io, weight, dlog, skip, u, z, g, *kept, across)


def greet(partners):
    barrier = pltpu.get_barrier_semaphore()
    for partner in partners:
        pl.semaphore_signal(barrier, inc=1, device_id=partner, device_id_type=MESH)
    pl.semaphore_wait(barrier, len(partners))


def remote(src, dst, send, recv, to):
    return pltpu.make_async_remote_copy(
        src_ref=src, dst_ref=dst, send_sem=send, recv_sem=recv, device_id=to, device_id_type=MESH
    )


def others(axis, count):
    me = lax.axis_index(axis)
    return [{axis: lax.rem(me + d, count)} for d in range(1, count)]


def token_rows(owner):
    return pl.ds(pl.multiple_of(owner * PIECE, 8), PIECE)


def fold(rows):
    return rows[:ROWS] + pltpu.roll(rows[ROWS : 2 * ROWS], 2 * N, 1) + pltpu.roll(rows[2 * ROWS :], 4 * N, 1)


def unfold(folded):
    used = lax.broadcasted_iota(jnp.int32, (ROWS, LANE), 1) < 2 * N
    parts = [folded, pltpu.roll(folded, LANE - 2 * N, 1), pltpu.roll(folded, LANE - 4 * N, 1)]
    return jnp.concatenate([jnp.where(used, part, 0.0) for part in parts], axis=0)


def over(rows):
    return jnp.concatenate([rows[:, : R // 2], rows[:, R // 2 : R]], axis=0)


def sum_start(part_ref, low_part, io_part, low_land, io_land, send, recv):
    for p in range(CH):
        rows = part_ref[p * PIECE : (p + 1) * PIECE, :]
        low_part[p] = over(rows).astype(low_part.dtype)
        io_part[p] = fold(rows[:, R:])
    copies = []
    for d, to in enumerate(others("ch", CH)):
        copies.append(remote(low_part.at[to["ch"]], low_land.at[d], send.at[0, d], recv.at[0, d], to))
        copies.append(remote(io_part.at[to["ch"]], io_land.at[d], send.at[1, d], recv.at[1, d], to))
    for copy in copies:
        copy.start()
    return copies


def share_start(sums, part_ref, io_part, low_land, io_land, low_all, io_all, send, recv):
    me = lax.axis_index("ch")
    for copy in sums:
        copy.wait_recv()
    low = over(part_ref[token_rows(me), :])
    io = io_part[me]
    for d in range(CH - 1):
        low = low + low_land[d].astype(F32)
        io = io + io_land[d]
    low_all[me] = low.astype(BF16)
    io_all[me] = io
    copies = []
    for d, to in enumerate(others("ch", CH)):
        copies.append(remote(low_all.at[me], low_all.at[me], send.at[0, d], recv.at[0, d], to))
        copies.append(remote(io_all.at[me], io_all.at[me], send.at[1, d], recv.at[1, d], to))
    for copy in copies:
        copy.start()
    return copies


def share_finish(copies, low_all, io_all, wide):
    for copy in copies:
        copy.wait_recv()
    for p in range(CH):
        both = low_all[p].astype(F32)
        rows = slice(p * PIECE, (p + 1) * PIECE)
        wide[rows, : R // 2] = both[:PIECE]
        wide[rows, R // 2 : R] = both[PIECE:]
        wide[rows, R:] = unfold(io_all[p])


def sum_scratch(sent):
    return [
        pltpu.VMEM((CH, 2 * PIECE, R // 2), sent),
        pltpu.VMEM((CH, ROWS, LANE), F32),
        pltpu.VMEM((CH - 1, 2 * PIECE, R // 2), sent),
        pltpu.VMEM((CH - 1, ROWS, LANE), F32),
        pltpu.VMEM((CH, 2 * PIECE, R // 2), BF16),
        pltpu.VMEM((CH, ROWS, LANE), F32),
        pltpu.VMEM((TOK, WIDE), F32),
        pltpu.SemaphoreType.DMA((2, CH - 1)),
        pltpu.SemaphoreType.DMA((2, CH - 1)),
        pltpu.SemaphoreType.DMA((2, CH - 1)),
        pltpu.SemaphoreType.DMA((2, CH - 1)),
    ]


def sum_projected(u_ref, xt_ref, low_ref, io_ref, part_ref, *scratch):
    low_part, io_part, low_land, io_land, low_all, io_all, wide, sum_send, sum_recv, all_send, all_recv = scratch
    part_ref[:, R:] = jnp.zeros((TOK, LANE), F32)
    part_ref[:, : R + 2 * N] = lax.dot_general(
        u_ref[...], xt_ref[...], (((1,), (1,)), ((), ())), preferred_element_type=F32
    )
    greet(others("ch", CH))
    sums = sum_start(part_ref, low_part, io_part, low_land, io_land, sum_send, sum_recv)
    shares = share_start(sums, part_ref, io_part, low_land, io_land, low_all, io_all, all_send, all_recv)
    share_finish(shares, low_all, io_all, wide)
    low_ref[...] = wide[:, :R].astype(BF16)
    io_ref[...] = wide[:, R:]
    for copy in sums + shares:
        copy.wait_send()


def in_vmem(count):
    return [pl.BlockSpec(memory_space=pltpu.VMEM)] * count


def run_sum(u, xt):
    return pl.pallas_call(
        sum_projected,
        in_specs=in_vmem(2),
        out_specs=in_vmem(2),
        out_shape=[jax.ShapeDtypeStruct((TOK, R), BF16), jax.ShapeDtypeStruct((TOK, LANE), F32)],
        scratch_shapes=[pltpu.VMEM((TOK, WIDE), F32)] + sum_scratch(F32),
        compiler_params=pltpu.CompilerParams(
            collective_id=0, has_side_effects=True, vmem_limit_bytes=VMEM_BYTES
        ),
        name="sum_projected",
    )(u, xt)


def spread_start(src, dst, send, recv):
    me = lax.axis_index("ctx")
    copies = []
    for d, to in enumerate(others("ctx", CTX)):
        copies.append(remote(src.at[to["ctx"]], dst.at[me], send.at[d], recv.at[d], to))
        copies[-1].start()
    dst[me] = src[me]
    return copies


def exchange(pack_ref, dlog_ref, out_ref, landed, back, result, send, recv, back_send, back_recv):
    me = lax.axis_index("ctx")
    greet(others("ctx", CTX))
    there = spread_start(pack_ref, landed, send, recv)
    rates = -jnp.exp(dlog_ref[:, pl.ds(pl.multiple_of(me * LANE, LANE), LANE)])
    for copy in there:
        copy.wait_recv()
    state = jnp.zeros((N, LANE), F32)
    adjoint = jnp.zeros((N, LANE), F32)
    for c in range(CTX):
        r = CTX - 1 - c
        back[c, :N] = state
        back[r, N:] = adjoint
        state = jnp.exp(landed[c, 2 * N : 2 * N + 1] * rates) * state + landed[c, :N]
        adjoint = jnp.exp(landed[r, 2 * N : 2 * N + 1] * rates) * adjoint + landed[r, N : 2 * N]
    home = spread_start(back, result, back_send, back_recv)
    for copy in home:
        copy.wait_recv()
    out_ref[...] = result[...]
    for copy in there + home:
        copy.wait_send()


def run_exchange(pack, dlog):
    return pl.pallas_call(
        exchange,
        in_specs=in_vmem(2),
        out_specs=pl.BlockSpec(memory_space=pltpu.VMEM),
        out_shape=jax.ShapeDtypeStruct((CTX, 2 * N, LANE), F32),
        scratch_shapes=[
            pltpu.VMEM((CTX, PACK, LANE), F32),
            pltpu.VMEM((CTX, 2 * N, LANE), F32),
            pltpu.VMEM((CTX, 2 * N, LANE), F32),
        ]
        + [pltpu.SemaphoreType.DMA((CTX - 1,))] * 4,
        compiler_params=pltpu.CompilerParams(
            collective_id=1, has_side_effects=True, vmem_limit_bytes=VMEM_BYTES
        ),
        name="exchange",
    )(pack, dlog)


def neighbour(axis, d):
    me = lax.axis_index("ctx")
    x, y = me // SIDE, lax.rem(me, SIDE)
    if axis == 0:
        return {"ctx": lax.rem(x + d + SIDE, SIDE) * SIDE + y}
    return {"ctx": x * SIDE + lax.rem(y + d + SIDE, SIDE)}


def place(axis, d=0):
    me = lax.axis_index("ctx")
    at = me // SIDE if axis == 0 else lax.rem(me, SIDE)
    return lax.rem(at + d + SIDE, SIDE)


WAYS = ((0, 1, 0), (1, -1, 1))


def ring_start(axis, src, relay, land, send, recv):
    passing, direct = [], []
    for way, d, half in WAYS:
        to = neighbour(axis, d)
        passing.append(remote(src.at[place(axis, 2), half], relay.at[way], send.at[0, way], recv.at[0, way], to))
        direct.append(
            remote(src.at[place(axis, d), 1 - half], land.at[way, 1 - half], send.at[1, way], recv.at[1, way], to)
        )
        passing[-1].start()
    for copy in direct:
        copy.start()
    return passing, direct


def ring_middle(axis, src, relay, land, send, recv, copies):
    passing, direct = copies
    last = []
    for way, d, half in WAYS:
        passing[way].wait_recv()
        mine = src[place(axis, d), half]
        relay[way] = (relay[way].astype(F32) + mine.astype(F32)).astype(BF16)
        last.append(
            remote(relay.at[way], land.at[way, half], send.at[2, way], recv.at[2, way], neighbour(axis, d))
        )
        last[-1].start()
    return passing, direct, last


def ring_finish(axis, src, land, copies):
    _, direct, last = copies
    for copy in direct + last:
        copy.wait_recv()
    mine = place(axis)
    return [
        src[mine, h].astype(F32) + land[0, h].astype(F32) + land[1, h].astype(F32) for h in range(2)
    ]


def ring_done(copies):
    for group in copies:
        for copy in group:
            copy.wait_send()


RING = 9


def ring_scratch(unit, second):
    return [
        pltpu.VMEM((2,) + unit, BF16),
        pltpu.VMEM((2, 2) + unit, BF16),
        pltpu.VMEM((SIDE, 2) + second, BF16),
        pltpu.VMEM((2,) + second, BF16),
        pltpu.VMEM((2, 2) + second, BF16),
        pltpu.SemaphoreType.DMA((3, 2)),
        pltpu.SemaphoreType.DMA((3, 2)),
        pltpu.SemaphoreType.DMA((3, 2)),
        pltpu.SemaphoreType.DMA((3, 2)),
    ]


def plane_start(src, rings):
    started = []
    for q, (relay, land, _, _, _, send, recv, _, _) in enumerate(rings):
        started.append(ring_start(q, src[q], relay, land, send, recv))
    return started


def plane_middle(src, rings, copies):
    passed = []
    for q, (relay, land, _, _, _, send, recv, _, _) in enumerate(rings):
        passed.append(ring_middle(q, src[q], relay, land, send, recv, copies[q]))
    return passed


def plane_turn(src, rings, copies, split):
    started = []
    for q, (_, land, second, relay, land2, _, _, send, recv) in enumerate(rings):
        halves = ring_finish(q, src[q], land, copies[q])
        for o in range(SIDE):
            for h in range(2):
                second[o, h] = split(halves[o // 2][o % 2], h).astype(BF16)
        started.append(ring_start(1 - q, second, relay, land2, send, recv))
    return started


def plane_second_middle(rings, copies):
    passed = []
    for q, (_, _, second, relay, land2, _, _, send, recv) in enumerate(rings):
        passed.append(ring_middle(1 - q, second, relay, land2, send, recv, copies[q]))
    return passed


def plane_finish(rings, copies):
    return [ring_finish(1 - q, rings[q][2], rings[q][4], copies[q]) for q in range(2)]


def left_half(value, h):
    columns = value.shape[1] // 2
    return value[:, h * columns : (h + 1) * columns]


def top_half(value, h):
    rows = value.shape[0] // 2
    return value[h * rows : (h + 1) * rows]


X_ROWS = (288, 256)


def tail(
    part_ref, small_in, dgate_ref, step_grad, u_ref, xw_ref, dsig_ref,
    hin_ref, hgate_ref, gx_ref, gstep_ref, gdecay_ref, gbias_ref, gskip_ref,
    low_part, io_part, low_land, io_land, low_all, io_all, wide, sum_send, sum_recv, all_send, all_recv,
    small_land, small_back, small_all, s_send, s_recv, t_send, t_recv,
    gate_land, in_out, in_land, hand_send, hand_recv, proj, proj_t, x_grad0, x_grad1, *scratch,
):
    rings = [scratch[k * RING : (k + 1) * RING] for k in range(4)]
    step_ring, x_ring = rings[:2], rings[2:]
    step_grad = [step_grad.at[q] for q in range(2)]
    x_grad = [x_grad0, x_grad1]
    section = lax.axis_index("section")
    me = lax.axis_index("ctx")
    greet(others("ctx", CTX) + others("ch", CH) + [{"section": 1 - section}])
    gate_copy = remote(dgate_ref, gate_land, hand_send.at[0], hand_recv.at[0], {"section": 1 - section})
    in_copy = remote(in_out, in_land, hand_send.at[1], hand_recv.at[1], {"section": 1 - section})

    sums = sum_start(part_ref, low_part, io_part, low_land, io_land, sum_send, sum_recv)
    first = plane_start(step_grad, step_ring)

    @pl.when(section == 1)
    def _():
        gate_copy.start()

    small_there = spread_start(small_in, small_land, s_send, s_recv)
    shares = share_start(sums, part_ref, io_part, low_land, io_land, low_all, io_all, all_send, all_recv)
    first = plane_middle(step_grad, step_ring, first)
    for copy in small_there:
        copy.wait_recv()
    total = small_land[0]
    for c in range(1, CTX):
        total = total + small_land[c]
    small_all[me] = total
    small_home = []
    for d, to in enumerate(others("ctx", CTX)):
        small_home.append(remote(small_all.at[me], small_all.at[me], t_send.at[d], t_recv.at[d], to))
        small_home[-1].start()

    share_finish(shares, low_all, io_all, wide)
    proj[...] = wide[...].astype(BF16)
    proj_t[...] = wide[...].T.astype(BF16)

    def product(c, _):
        columns = pl.ds(pl.multiple_of(c * TILE, TILE), TILE)
        grad = jnp.dot(
            proj_t[: R + 2 * N, :], u_ref[:, columns], preferred_element_type=F32
        ).astype(BF16)
        x, y_high = c // 2, lax.rem(c, 2)
        for e in range(2):
            x_grad0[x, y_high, e] = grad[: X_ROWS[0], lanes(e)]
            x_grad1[2 * y_high + e, x // 2, lax.rem(x, 2)] = grad[X_ROWS[0] :, lanes(e)]
        return 0

    lax.fori_loop(0, CTX // 2, product, 0)
    first_x = plane_start(x_grad, x_ring)

    @pl.when(section == 1)
    def _():
        def one(j, _):
            columns = pl.ds(pl.multiple_of(j * TILE, TILE), TILE)
            in_out[:, columns] = (
                dsig_ref[:, columns]
                + lax.dot_general(
                    proj[:, : R + 2 * N], xw_ref[:, columns], (((1,), (0,)), ((), ())),
                    preferred_element_type=F32,
                )
            ).astype(BF16)
            return 0

        lax.fori_loop(0, u_ref.shape[1] // TILE, one, 0)
        in_copy.start()
        hin_ref[...] = jnp.zeros_like(hin_ref)
        hgate_ref[...] = jnp.zeros_like(hgate_ref)

    turned = plane_turn(step_grad, step_ring, first, left_half)
    first_x = plane_middle(x_grad, x_ring, first_x)
    turned = plane_second_middle(step_ring, turned)
    for copy in small_home:
        copy.wait_recv()
    for c in range(CTX):
        gdecay_ref[:, lanes(c)] = small_all[c, :N]
        gbias_ref[:, lanes(c)] = small_all[c, N : N + 1]
        gskip_ref[:, lanes(c)] = small_all[c, N + 1 : N + 2]
    for q, halves in enumerate(plane_finish(step_ring, turned)):
        for h in range(2):
            gstep_ref[q * 16 : (q + 1) * 16, h * 1024 : (h + 1) * 1024] = halves[h]
    turned_x = plane_turn(x_grad, x_ring, first_x, top_half)

    @pl.when(section == 0)
    def _():
        gate_copy.wait_recv()
        in_copy.wait_recv()
        hgate_ref[...] = gate_land[...]
        hin_ref[...] = in_land[...]

    turned_x = plane_second_middle(x_ring, turned_x)
    for q, halves in enumerate(plane_finish(x_ring, turned_x)):
        for h in range(2):
            rows = X_ROWS[q] // 2
            gx_ref[q * X_ROWS[0] + h * rows : q * X_ROWS[0] + (h + 1) * rows, :] = halves[h]

    @pl.when(section == 1)
    def _():
        gate_copy.wait_send()
        in_copy.wait_send()

    for copy in sums + shares + small_there + small_home:
        copy.wait_send()
    for copies in first + turned + first_x + turned_x:
        ring_done(copies)


def run_tail(part, small, dgate, step_grad, u, xw, dsig):
    ch = u.shape[1]
    f = lambda *s: jax.ShapeDtypeStruct(s, F32)
    b = lambda *s: jax.ShapeDtypeStruct(s, BF16)
    return pl.pallas_call(
        tail,
        in_specs=in_vmem(7),
        out_specs=in_vmem(7),
        out_shape=[
            b(TOK, ch), b(TOK, ch), f(R + 2 * N, LANE), f(32, ch), f(N, ch), f(1, ch), f(1, ch),
        ],
        scratch_shapes=sum_scratch(BF16)
        + [pltpu.VMEM((CTX, SMALL, LANE), F32)] * 3
        + [pltpu.SemaphoreType.DMA((CTX - 1,))] * 4
        + [pltpu.VMEM((TOK, ch), BF16)] * 3
        + [pltpu.SemaphoreType.DMA((2,))] * 2
        + [pltpu.VMEM((TOK, WIDE), BF16), pltpu.VMEM((WIDE, TOK), BF16)]
        + [pltpu.VMEM((SIDE, 2, 2, rows, LANE), BF16) for rows in X_ROWS]
        + ring_scratch((2, 16, 2048), (16, 1024)) * 2
        + ring_scratch((2, X_ROWS[0], LANE), (X_ROWS[0] // 2, LANE))
        + ring_scratch((2, X_ROWS[1], LANE), (X_ROWS[1] // 2, LANE)),
        compiler_params=pltpu.CompilerParams(
            collective_id=2, has_side_effects=True, vmem_limit_bytes=VMEM_BYTES
        ),
        name="tail",
    )(part, small, dgate, step_grad, u, xw, dsig)


def finish(*refs):
    count = len(refs) // 2
    sem = refs[-1]
    copies = [pltpu.make_async_copy(refs[k], refs[count + k], sem.at[k]) for k in range(count)]
    for copy in copies:
        copy.start()
    for copy in copies:
        copy.wait()


def run_finish(*results):
    anywhere = [pl.BlockSpec(memory_space=pl.ANY)] * len(results)
    return pl.pallas_call(
        finish,
        in_specs=anywhere,
        out_specs=anywhere,
        out_shape=[jax.ShapeDtypeStruct(r.shape, r.dtype) for r in results],
        scratch_shapes=[pltpu.SemaphoreType.DMA((len(results),))],
        compiler_params=pltpu.CompilerParams(vmem_limit_bytes=VMEM_BYTES),
        name="finish",
    )(*results)


def body(mixer_input, gate_input, upstream_grad, x_weight, step_weight, step_bias, decay_log, skip_gain):
    u, z, g = mixer_input[0], gate_input[0], upstream_grad[0]
    weight_x, weight_step = jnp.swapaxes(x_weight[0], 0, 1), step_weight[0]
    dlog = decay_log[0]
    low, io = run_sum(u, weight_x)
    *kept, pack, bsum = run_first(low, io, weight_step, step_bias, dlog, u, z, g)
    across = run_exchange(pack, dlog)
    d_gate, d_signal, d_part, grad_step, small = run_second(
        low, io, weight_step, dlog, skip_gain, u, z, g, [*kept, bsum], across
    )
    handed_input, handed_gate, grad_x, grad_step, g_decay, g_bias, g_skip = run_finish(
        *run_tail(d_part, small, d_gate, grad_step, u, weight_x, d_signal)
    )
    return (
        handed_input[None], handed_gate[None], jnp.swapaxes(grad_x, 0, 1)[None], grad_step[None],
        g_bias, g_decay[None], g_skip,
    )


def solution(mesh):
    return jax.shard_map(
        body,
        mesh=mesh,
        in_specs=(
            P("section", "ctx", "ch"), P("section", "ctx", "ch"), P("section", "ctx", "ch"),
            P("section", "ch", None), P("section", None, "ch"), P("section", "ch"),
            P("section", None, "ch"), P("section", "ch"),
        ),
        out_specs=(
            P("section", "ctx", "ch"), P("section", "ctx", "ch"), P("section", ("ch", "ctx"), None),
            P("section", "ctx", "ch"), P("section", "ch"), P("section", None, "ch"), P("section", "ch"),
        ),
        check_vma=False,
    )
```

```python
import functools

import jax
import jax.numpy as jnp
from jax import lax
from jax.experimental import pallas as pl
from jax.experimental.pallas import tpu as pltpu
from jax.sharding import PartitionSpec as P

R = 512
N = 16
TOK = 192
STEPS = 24
ROWS = 8
TILE = 256
LANE = 128
HALVES = TILE // LANE
CHUNK = 4
LOG2E = 1.4426950408889634
VMEM_BYTES = 60 * 2**20
SIDE = 4
CTX = 16
CH = 8
PIECE = TOK // CH
WIDE = R + LANE
PACK = 40
SMALL = 24
MESH = pl.DeviceIdType.MESH
LN2 = 0.6931471805599453
F32 = jnp.float32
BF16 = jnp.bfloat16


def every(i):
    return pl.ds(i, ROWS, stride=STEPS)


def lanes(k):
    return slice(k * LANE, (k + 1) * LANE)


def by_step(ref, value, by_token):
    for k in range(HALVES):
        by_token[k] = value[:, lanes(k)]
        for i in range(STEPS):
            ref[k, i] = by_token[k, every(i), :]


def from_step(ref, by_token):
    for k in range(HALVES):
        for i in range(STEPS):
            by_token[k, every(i), :] = ref[k, i]
    return jnp.concatenate([by_token[k] for k in range(HALVES)], axis=1)


def row_index():
    return lax.broadcasted_iota(jnp.int32, (ROWS, LANE), 0)


def spread_columns(io_ref, spread):
    def one(i, _):
        rows = io_ref[every(i), :]
        for n in range(2 * N):
            spread[i, n] = jnp.broadcast_to(rows[:, n : n + 1], (ROWS, LANE))
        return 0

    lax.fori_loop(0, STEPS, one, 0)


def inverse(value):
    rough = pl.reciprocal(value, approx=True)
    return rough * (2.0 - value * rough)


def scan_rows(decay, value, reverse):
    row = row_index()
    for k in (1, 2, 4):
        shift = ROWS - k if reverse else k
        inside = row < ROWS - k if reverse else row >= k
        value = value + decay * jnp.where(inside, pltpu.roll(value, shift, 0), 0.0)
        if k < 4:
            decay = decay * jnp.where(inside, pltpu.roll(decay, shift, 0), 1.0)
    return value


def first_pass(
    low_ref, io_ref, w_ref, bias_ref, dlog_ref, u_ref, z_ref, g_ref,
    step_ref, token_ref, sig_ref, drive, seed, entry_ref, exit_ref, pack_ref, bsum_ref,
    spread, by_drive, by_seed, by_step_size, rates,
):
    @pl.when(pl.program_id(0) == 0)
    def _():
        spread_columns(io_ref, spread)

    pre = jnp.dot(low_ref[...], w_ref[...], preferred_element_type=F32) + bias_ref[...]
    small = jnp.exp(-jnp.abs(pre))
    above = inverse(1.0 + small)
    series = small * (1.0 - small * (0.5 - small * (1.0 / 3.0)))
    step = jnp.maximum(pre, 0.0) + jnp.where(small < 1e-3, series, jnp.log(1.0 + small))
    sig_ref[...] = jnp.where(pre >= 0.0, above, small * above)
    z = z_ref[...].astype(F32)
    token_ref[...] = step
    by_step(step_ref, step, by_step_size)
    by_step(drive, step * u_ref[...].astype(F32), by_drive)
    by_step(seed, g_ref[...].astype(F32) * z * inverse(1.0 + jnp.exp(-z)), by_seed)
    rates[...] = -LOG2E * jnp.exp(dlog_ref[...])
    row = row_index()

    total = jnp.zeros((ROWS, TILE), F32)
    for i in range(STEPS):
        total = total + jnp.concatenate([step_ref[k, i] for k in range(HALVES)], axis=1)
    bsum_ref[...] = total
    whole_sum = jnp.sum(total, axis=0, keepdims=True)
    for k in range(HALVES):
        pack_ref[k, 2 * N :, :] = jnp.broadcast_to(whole_sum[:, lanes(k)], (PACK - 2 * N, LANE))

    for c in range(N // CHUNK):
        pairs = [(n, k) for n in range(c * CHUNK, (c + 1) * CHUNK) for k in range(HALVES)]
        rate = [jnp.broadcast_to(rates[n : n + 1, lanes(k)], (ROWS, LANE)) for n, k in pairs]

        def one(i, carry):
            state, decay, start = carry
            st = [step_ref[k, i] for k in range(HALVES)]
            dr = [drive[k, i] for k in range(HALVES)]
            sd = [seed[k, i] for k in range(HALVES)]
            new_state, new_decay, new_start = [], [], []
            for p, (n, k) in enumerate(pairs):
                a = jnp.exp2(st[k] * rate[p])
                new_state.append(a * state[p] + dr[k] * spread[i, n])
                d = a * decay[p]
                new_decay.append(d)
                new_start.append(start[p] + d * (sd[k] * spread[i, N + n]))
            return tuple(new_state), tuple(new_decay), tuple(new_start)

        zero = tuple(jnp.zeros((ROWS, LANE), F32) for _ in pairs)
        ones = tuple(jnp.ones((ROWS, LANE), F32) for _ in pairs)
        state, decay, start = lax.fori_loop(0, STEPS, one, (zero, ones, zero), unroll=12)
        for p, (n, k) in enumerate(pairs):
            ends = scan_rows(decay[p], state[p], False)
            starts = scan_rows(decay[p], start[p], True)
            entry_ref[n, :, lanes(k)] = jnp.where(row >= 1, pltpu.roll(ends, 1, 0), 0.0)
            exit_ref[n, :, lanes(k)] = jnp.where(row < ROWS - 1, pltpu.roll(starts, ROWS - 1, 0), 0.0)
            pack_ref[k, n : n + 1, :] = ends[ROWS - 1 :, :]
            pack_ref[k, N + n : N + n + 1, :] = starts[:1, :]


def sum_before(value, reverse):
    row = lax.broadcasted_iota(jnp.int32, value.shape, 0)
    held = value
    for k in (1, 2, 4):
        shift = ROWS - k if reverse else k
        inside = row < ROWS - k if reverse else row >= k
        held = held + jnp.where(inside, pltpu.roll(held, shift, 0), 0.0)
    return held - value


def second_pass(
    low_ref, io_ref, w_ref, dlog_ref, skip_ref, u_ref, z_ref, g_ref, step_ref, token_ref, sig_ref, drive, seed,
    entry_ref, exit_ref, bsum_ref, across_ref,
    dgate_ref, dsig_ref, part_ref, gstep_ref, small_ref,
    spread, sums, held, scanned, grad_drive, grad_decay, by_scan, by_grad, by_decay, rates, by_token, low_t,
):
    tile = pl.program_id(0)

    @pl.when(tile == 0)
    def _():
        spread_columns(io_ref, spread)
        sums[...] = jnp.zeros_like(sums)
        part_ref[...] = jnp.zeros_like(part_ref)
        low_t[...] = low_ref[...].astype(F32).T.astype(BF16)

    rates[...] = -LOG2E * jnp.exp(dlog_ref[...])
    prior = sum_before(bsum_ref[...], False)
    later = sum_before(bsum_ref[...], True)

    def so_far(ref, c, i):
        if c == 0:
            return [jnp.zeros((ROWS, LANE), F32) for k in range(HALVES)]
        return [ref[k, i] for k in range(HALVES)]

    for c in range(N // CHUNK):
        numbers = range(c * CHUNK, (c + 1) * CHUNK)
        pairs = [(n, k) for n in numbers for k in range(HALVES)]
        rate = [jnp.broadcast_to(rates[n : n + 1, lanes(k)], (ROWS, LANE)) for n, k in pairs]

        def forward(i, state, c=c, numbers=numbers, rate=rate):
            st = [step_ref[k, i] for k in range(HALVES)]
            dr = [drive[k, i] for k in range(HALVES)]
            sd = [seed[k, i] for k in range(HALVES)]
            out = so_far(scanned, c, i)
            new = []
            for m, n in enumerate(numbers):
                b_in, b_out = spread[i, n], spread[i, N + n]
                d_out = sums[i, N + n]
                for k in range(HALVES):
                    p = m * HALVES + k
                    held[i, m, :, lanes(k)] = state[p]
                    now = jnp.exp2(st[k] * rate[p]) * state[p] + dr[k] * b_in
                    new.append(now)
                    out[k] = out[k] + b_out * now
                    d_out = d_out + sd[k] * now
                sums[i, N + n] = d_out
            for k in range(HALVES):
                scanned[k, i] = out[k]
            return tuple(new)

        state = tuple(
            entry_ref[n, :, lanes(k)]
            + jnp.exp2(prior[:, lanes(k)] * rate[p]) * across_ref[k, n : n + 1, :]
            for p, (n, k) in enumerate(pairs)
        )
        lax.fori_loop(0, STEPS, forward, state, unroll=8)

        def backward(j, carry, c=c, numbers=numbers, rate=rate):
            incoming, total = carry
            i = STEPS - 1 - j
            st = [step_ref[k, i] for k in range(HALVES)]
            dr = [drive[k, i] for k in range(HALVES)]
            sd = [seed[k, i] for k in range(HALVES)]
            g_drive = so_far(grad_drive, c, i)
            g_decay = so_far(grad_decay, c, i)
            new_in, new_total = [], []
            for m, n in enumerate(numbers):
                b_in, b_out = spread[i, n], spread[i, N + n]
                d_in = sums[i, n]
                for k in range(HALVES):
                    p = m * HALVES + k
                    adjoint = b_out * sd[k] + incoming[p]
                    passed = jnp.exp2(st[k] * rate[p]) * adjoint
                    pulled = passed * held[i, m, :, lanes(k)]
                    new_in.append(passed)
                    new_total.append(total[p] + pulled * st[k])
                    g_decay[k] = g_decay[k] + pulled * rate[p]
                    g_drive[k] = g_drive[k] + adjoint * b_in
                    d_in = d_in + adjoint * dr[k]
                sums[i, n] = d_in
            for k in range(HALVES):
                grad_drive[k, i] = g_drive[k]
                grad_decay[k, i] = g_decay[k]
            return tuple(new_in), tuple(new_total)

        incoming = tuple(
            exit_ref[n, :, lanes(k)]
            + jnp.exp2(later[:, lanes(k)] * rate[p]) * across_ref[k, N + n : N + n + 1, :]
            for p, (n, k) in enumerate(pairs)
        )
        zero = tuple(jnp.zeros((ROWS, LANE), F32) for _ in pairs)
        _, total = lax.fori_loop(0, STEPS, backward, (incoming, zero), unroll=8)
        for p, (n, k) in enumerate(pairs):
            small_ref[k, n : n + 1, :] = (
                jnp.sum(total[p], axis=0, keepdims=True) * rates[n : n + 1, lanes(k)] * LN2
            )

    u = u_ref[...].astype(F32)
    z = z_ref[...].astype(F32)
    g = g_ref[...].astype(F32)
    gate_sig = inverse(1.0 + jnp.exp(-z))
    seeds = g * z * gate_sig
    skip = skip_ref[...]
    from_drive = from_step(grad_drive, by_grad)
    mixed = from_step(scanned, by_scan) + skip * u
    dgate_ref[...] = (g * mixed * gate_sig * (1.0 + z * (1.0 - gate_sig))).astype(BF16)
    dsig_ref[...] = from_drive * token_ref[...] + skip * seeds
    d_pre = (from_drive * u + from_step(grad_decay, by_decay) * LN2) * sig_ref[...]
    pre = d_pre.astype(BF16)
    bias_row = jnp.sum(d_pre, axis=0, keepdims=True)
    skip_row = jnp.sum(seeds * u, axis=0, keepdims=True)
    for k in range(HALVES):
        small_ref[k, N : N + 1, :] = bias_row[:, lanes(k)]
        small_ref[k, N + 1 : N + 2, :] = skip_row[:, lanes(k)]
        small_ref[k, N + 2 :, :] = jnp.zeros((SMALL - N - 2, LANE), F32)
    part_ref[:, :R] += lax.dot_general(
        pre, w_ref[...], (((1,), (1,)), ((), ())), preferred_element_type=F32
    )
    grad = jnp.dot(low_t[...], pre, preferred_element_type=F32).astype(BF16)
    for x in range(SIDE):
        for y in range(SIDE):
            at = (x * SIDE + y) * 2 * 16
            gstep_ref[0, x, y // 2, y % 2] = grad[at : at + 16]
            gstep_ref[1, y, x // 2, x % 2] = grad[at + 16 : at + 32]

    @pl.when(tile == pl.num_programs(0) - 1)
    def _():
        column = lax.broadcasted_iota(jnp.int32, (ROWS, LANE), 1)

        def one(i, _):
            rows = jnp.zeros((ROWS, LANE), F32)
            for n in range(2 * N):
                rows = jnp.where(column == n, jnp.sum(sums[i, n], axis=1, keepdims=True), rows)
            by_token[every(i), :] = rows
            return 0

        lax.fori_loop(0, STEPS, one, 0)
        part_ref[:, R:] = by_token[...]


def whole(*shape):
    return pl.BlockSpec(shape, lambda j: (0,) * len(shape))


def tiled(*lead):
    return pl.BlockSpec(lead + (TILE,), lambda j: (0,) * len(lead) + (j,))


def stacked(*rows):
    return pl.BlockSpec((HALVES,) + rows + (LANE,), lambda j: (j,) + (0,) * (len(rows) + 1))


def run_first(low, io, weight, bias, dlog, u, z, g):
    ch = u.shape[1]
    f = lambda *s: jax.ShapeDtypeStruct(s, F32)
    return pl.pallas_call(
        first_pass,
        grid=(ch // TILE,),
        in_specs=[
            whole(TOK, R), whole(TOK, io.shape[1]), tiled(R), tiled(1), tiled(N),
            tiled(TOK), tiled(TOK), tiled(TOK),
        ],
        out_specs=[
            stacked(STEPS, ROWS), tiled(TOK), tiled(TOK), stacked(STEPS, ROWS), stacked(STEPS, ROWS),
            tiled(N, ROWS), tiled(N, ROWS), stacked(PACK), tiled(ROWS),
        ],
        out_shape=[
            f(ch // LANE, STEPS, ROWS, LANE), f(TOK, ch), f(TOK, ch), f(ch // LANE, STEPS, ROWS, LANE),
            f(ch // LANE, STEPS, ROWS, LANE), f(N, ROWS, ch), f(N, ROWS, ch),
            f(ch // LANE, PACK, LANE), f(ROWS, ch),
        ],
        scratch_shapes=[
            pltpu.VMEM((STEPS, 2 * N, ROWS, LANE), F32),
            pltpu.VMEM((HALVES, TOK, LANE), F32),
            pltpu.VMEM((HALVES, TOK, LANE), F32),
            pltpu.VMEM((HALVES, TOK, LANE), F32),
            pltpu.VMEM((N, TILE), F32),
        ],
        compiler_params=pltpu.CompilerParams(vmem_limit_bytes=VMEM_BYTES),
        name="first_pass",
    )(low, io, weight, bias, dlog, u, z, g)


def run_second(low, io, weight, dlog, skip, u, z, g, kept, across):
    ch = u.shape[1]
    f = lambda *s: jax.ShapeDtypeStruct(s, F32)
    return pl.pallas_call(
        second_pass,
        grid=(ch // TILE,),
        in_specs=[
            whole(TOK, R), whole(TOK, io.shape[1]), tiled(R), tiled(N), tiled(1),
            tiled(TOK), tiled(TOK), tiled(TOK), stacked(STEPS, ROWS), tiled(TOK), tiled(TOK),
            stacked(STEPS, ROWS), stacked(STEPS, ROWS), tiled(N, ROWS), tiled(N, ROWS), tiled(ROWS), stacked(2 * N),
        ],
        out_specs=[
            tiled(TOK), tiled(TOK), whole(TOK, WIDE), tiled(2, SIDE, 2, 2, 16), stacked(SMALL),
        ],
        out_shape=[
            jax.ShapeDtypeStruct((TOK, ch), BF16), f(TOK, ch), f(TOK, WIDE),
            jax.ShapeDtypeStruct((2, SIDE, 2, 2, 16, ch), BF16), f(ch // LANE, SMALL, LANE),
        ],
        scratch_shapes=[
            pltpu.VMEM((STEPS, 2 * N, ROWS, LANE), F32),
            pltpu.VMEM((STEPS, 2 * N, ROWS, LANE), F32),
            pltpu.VMEM((STEPS, CHUNK, ROWS, TILE), F32),
        ]
        + [pltpu.VMEM((HALVES, STEPS, ROWS, LANE), F32)] * 3
        + [pltpu.VMEM((HALVES, TOK, LANE), F32)] * 3
        + [pltpu.VMEM((N, TILE), F32), pltpu.VMEM((TOK, LANE), F32), pltpu.VMEM((R, TOK), BF16)],
        compiler_params=pltpu.CompilerParams(vmem_limit_bytes=VMEM_BYTES),
        name="second_pass",
    )(low, io, weight, dlog, skip, u, z, g, *kept, across)


def greet(partners):
    for partner in partners:
        pl.semaphore_signal(
            pltpu.get_barrier_semaphore(), inc=1, device_id=partner, device_id_type=MESH
        )


def met(partners):
    pl.semaphore_wait(pltpu.get_barrier_semaphore(), len(partners))


def remote(src, dst, send, recv, to):
    return pltpu.make_async_remote_copy(
        src_ref=src, dst_ref=dst, send_sem=send, recv_sem=recv, device_id=to, device_id_type=MESH
    )


def others(axis, count):
    me = lax.axis_index(axis)
    return [{axis: lax.rem(me + d, count)} for d in range(1, count)]


def token_rows(owner):
    return pl.ds(pl.multiple_of(owner * PIECE, 8), PIECE)


def fold(rows):
    return rows[:ROWS] + pltpu.roll(rows[ROWS : 2 * ROWS], 2 * N, 1) + pltpu.roll(rows[2 * ROWS :], 4 * N, 1)


def unfold(folded):
    used = lax.broadcasted_iota(jnp.int32, (ROWS, LANE), 1) < 2 * N
    parts = [folded, pltpu.roll(folded, LANE - 2 * N, 1), pltpu.roll(folded, LANE - 4 * N, 1)]
    return jnp.concatenate([jnp.where(used, part, 0.0) for part in parts], axis=0)


def over(rows):
    return jnp.concatenate([rows[:, : R // 2], rows[:, R // 2 : R]], axis=0)


def prepare(part_ref, low_part, io_part):
    for p in range(CH):
        rows = part_ref[p * PIECE : (p + 1) * PIECE, :]
        low_part[p] = over(rows).astype(low_part.dtype)
        io_part[p] = fold(rows[:, R:])


def sum_start(low_part, io_part, low_land, io_land, send, recv):
    copies = []
    for d, to in enumerate(others("ch", CH)):
        copies.append(remote(low_part.at[to["ch"]], low_land.at[d], send.at[0, d], recv.at[0, d], to))
        copies.append(remote(io_part.at[to["ch"]], io_land.at[d], send.at[1, d], recv.at[1, d], to))
    for copy in copies:
        copy.start()
    return copies


def share_start(sums, part_ref, io_part, low_land, io_land, low_all, io_all, send, recv):
    me = lax.axis_index("ch")
    for copy in sums:
        copy.wait_recv()
    low = over(part_ref[token_rows(me), :])
    io = io_part[me]
    for d in range(CH - 1):
        low = low + low_land[d].astype(F32)
        io = io + io_land[d]
    low_all[me] = low.astype(BF16)
    io_all[me] = io
    copies = []
    for d, to in enumerate(others("ch", CH)):
        copies.append(remote(low_all.at[me], low_all.at[me], send.at[0, d], recv.at[0, d], to))
        copies.append(remote(io_all.at[me], io_all.at[me], send.at[1, d], recv.at[1, d], to))
    for copy in copies:
        copy.start()
    return copies


def share_finish(copies, low_all, io_all, wide):
    for copy in copies:
        copy.wait_recv()
    for p in range(CH):
        both = low_all[p].astype(F32)
        rows = slice(p * PIECE, (p + 1) * PIECE)
        wide[rows, : R // 2] = both[:PIECE]
        wide[rows, R // 2 : R] = both[PIECE:]
        wide[rows, R:] = unfold(io_all[p])


def sum_scratch(sent):
    return [
        pltpu.VMEM((CH, 2 * PIECE, R // 2), sent),
        pltpu.VMEM((CH, ROWS, LANE), F32),
        pltpu.VMEM((CH - 1, 2 * PIECE, R // 2), sent),
        pltpu.VMEM((CH - 1, ROWS, LANE), F32),
        pltpu.VMEM((CH, 2 * PIECE, R // 2), BF16),
        pltpu.VMEM((CH, ROWS, LANE), F32),
        pltpu.VMEM((TOK, WIDE), F32),
        pltpu.SemaphoreType.DMA((2, CH - 1)),
        pltpu.SemaphoreType.DMA((2, CH - 1)),
        pltpu.SemaphoreType.DMA((2, CH - 1)),
        pltpu.SemaphoreType.DMA((2, CH - 1)),
    ]


def sum_projected(u_ref, xt_ref, low_ref, io_ref, part_ref, *scratch):
    low_part, io_part, low_land, io_land, low_all, io_all, wide, sum_send, sum_recv, all_send, all_recv = scratch
    greet(others("ch", CH))
    part_ref[:, R:] = jnp.zeros((TOK, LANE), F32)
    part_ref[:, : R + 2 * N] = lax.dot_general(
        u_ref[...], xt_ref[...], (((1,), (1,)), ((), ())), preferred_element_type=F32
    )
    prepare(part_ref, low_part, io_part)
    met(others("ch", CH))
    sums = sum_start(low_part, io_part, low_land, io_land, sum_send, sum_recv)
    shares = share_start(sums, part_ref, io_part, low_land, io_land, low_all, io_all, all_send, all_recv)
    share_finish(shares, low_all, io_all, wide)
    low_ref[...] = wide[:, :R].astype(BF16)
    io_ref[...] = wide[:, R:]
    for copy in sums + shares:
        copy.wait_send()


def in_vmem(count):
    return [pl.BlockSpec(memory_space=pltpu.VMEM)] * count


def run_sum(u, xt):
    return pl.pallas_call(
        sum_projected,
        in_specs=in_vmem(2),
        out_specs=in_vmem(2),
        out_shape=[jax.ShapeDtypeStruct((TOK, R), BF16), jax.ShapeDtypeStruct((TOK, LANE), F32)],
        scratch_shapes=[pltpu.VMEM((TOK, WIDE), F32)] + sum_scratch(F32),
        compiler_params=pltpu.CompilerParams(
            collective_id=0, has_side_effects=True, vmem_limit_bytes=VMEM_BYTES
        ),
        name="sum_projected",
    )(u, xt)


def spread_start(src, dst, send, recv):
    me = lax.axis_index("ctx")
    copies = []
    for d, to in enumerate(others("ctx", CTX)):
        copies.append(remote(src.at[to["ctx"]], dst.at[me], send.at[d], recv.at[d], to))
        copies[-1].start()
    dst[me] = src[me]
    return copies


def exchange(pack_ref, dlog_ref, out_ref, landed, back, result, send, recv, back_send, back_recv):
    me = lax.axis_index("ctx")
    greet(others("ctx", CTX))
    met(others("ctx", CTX))
    there = spread_start(pack_ref, landed, send, recv)
    rates = -jnp.exp(dlog_ref[:, pl.ds(pl.multiple_of(me * LANE, LANE), LANE)])
    for copy in there:
        copy.wait_recv()
    state = jnp.zeros((N, LANE), F32)
    adjoint = jnp.zeros((N, LANE), F32)
    for c in range(CTX):
        r = CTX - 1 - c
        back[c, :N] = state
        back[r, N:] = adjoint
        state = jnp.exp(landed[c, 2 * N : 2 * N + 1] * rates) * state + landed[c, :N]
        adjoint = jnp.exp(landed[r, 2 * N : 2 * N + 1] * rates) * adjoint + landed[r, N : 2 * N]
    home = spread_start(back, result, back_send, back_recv)
    for copy in home:
        copy.wait_recv()
    out_ref[...] = result[...]
    for copy in there + home:
        copy.wait_send()


def run_exchange(pack, dlog):
    return pl.pallas_call(
        exchange,
        in_specs=in_vmem(2),
        out_specs=pl.BlockSpec(memory_space=pltpu.VMEM),
        out_shape=jax.ShapeDtypeStruct((CTX, 2 * N, LANE), F32),
        scratch_shapes=[
            pltpu.VMEM((CTX, PACK, LANE), F32),
            pltpu.VMEM((CTX, 2 * N, LANE), F32),
            pltpu.VMEM((CTX, 2 * N, LANE), F32),
        ]
        + [pltpu.SemaphoreType.DMA((CTX - 1,))] * 4,
        compiler_params=pltpu.CompilerParams(
            collective_id=1, has_side_effects=True, vmem_limit_bytes=VMEM_BYTES
        ),
        name="exchange",
    )(pack, dlog)


def neighbour(axis, d):
    me = lax.axis_index("ctx")
    x, y = me // SIDE, lax.rem(me, SIDE)
    if axis == 0:
        return {"ctx": lax.rem(x + d + SIDE, SIDE) * SIDE + y}
    return {"ctx": x * SIDE + lax.rem(y + d + SIDE, SIDE)}


def place(axis, d=0):
    me = lax.axis_index("ctx")
    at = me // SIDE if axis == 0 else lax.rem(me, SIDE)
    return lax.rem(at + d + SIDE, SIDE)


WAYS = ((0, 1, 0), (1, -1, 1))


def ring_start(axis, src, relay, land, send, recv):
    passing, direct = [], []
    for way, d, half in WAYS:
        to = neighbour(axis, d)
        passing.append(remote(src.at[place(axis, 2), half], relay.at[way], send.at[0, way], recv.at[0, way], to))
        direct.append(
            remote(src.at[place(axis, d), 1 - half], land.at[way, 1 - half], send.at[1, way], recv.at[1, way], to)
        )
        passing[-1].start()
    for copy in direct:
        copy.start()
    return passing, direct


def ring_middle(axis, src, relay, land, send, recv, copies):
    passing, direct = copies
    last = []
    for way, d, half in WAYS:
        passing[way].wait_recv()
        mine = src[place(axis, d), half]
        relay[way] = (relay[way].astype(F32) + mine.astype(F32)).astype(BF16)
        last.append(
            remote(relay.at[way], land.at[way, half], send.at[2, way], recv.at[2, way], neighbour(axis, d))
        )
        last[-1].start()
    return passing, direct, last


def ring_finish(axis, src, land, copies):
    _, direct, last = copies
    for copy in direct + last:
        copy.wait_recv()
    mine = place(axis)
    return [
        src[mine, h].astype(F32) + land[0, h].astype(F32) + land[1, h].astype(F32) for h in range(2)
    ]


def ring_done(copies):
    for group in copies:
        for copy in group:
            copy.wait_send()


RING = 9


def ring_scratch(unit, second):
    return [
        pltpu.VMEM((2,) + unit, BF16),
        pltpu.VMEM((2, 2) + unit, BF16),
        pltpu.VMEM((SIDE, 2) + second, BF16),
        pltpu.VMEM((2,) + second, BF16),
        pltpu.VMEM((2, 2) + second, BF16),
        pltpu.SemaphoreType.DMA((3, 2)),
        pltpu.SemaphoreType.DMA((3, 2)),
        pltpu.SemaphoreType.DMA((3, 2)),
        pltpu.SemaphoreType.DMA((3, 2)),
    ]


def plane_start(src, rings):
    started = []
    for q, (relay, land, _, _, _, send, recv, _, _) in enumerate(rings):
        started.append(ring_start(q, src[q], relay, land, send, recv))
    return started


def plane_middle(src, rings, copies):
    passed = []
    for q, (relay, land, _, _, _, send, recv, _, _) in enumerate(rings):
        passed.append(ring_middle(q, src[q], relay, land, send, recv, copies[q]))
    return passed


def plane_turn(src, rings, copies, split):
    started = []
    for q, (_, land, second, relay, land2, _, _, send, recv) in enumerate(rings):
        halves = ring_finish(q, src[q], land, copies[q])
        for o in range(SIDE):
            for h in range(2):
                second[o, h] = split(halves[o // 2][o % 2], h).astype(BF16)
        started.append(ring_start(1 - q, second, relay, land2, send, recv))
    return started


def plane_second_middle(rings, copies):
    passed = []
    for q, (_, _, second, relay, land2, _, _, send, recv) in enumerate(rings):
        passed.append(ring_middle(1 - q, second, relay, land2, send, recv, copies[q]))
    return passed


def plane_finish(rings, copies):
    return [ring_finish(1 - q, rings[q][2], rings[q][4], copies[q]) for q in range(2)]


def left_half(value, h):
    columns = value.shape[1] // 2
    return value[:, h * columns : (h + 1) * columns]


def top_half(value, h):
    rows = value.shape[0] // 2
    return value[h * rows : (h + 1) * rows]


X_ROWS = (288, 256)


def tail(
    part_ref, small_in, dgate_ref, step_grad, u_hbm, xw_hbm, dsig_hbm,
    hin_ref, hgate_ref, gx_ref, gstep_ref, gdecay_ref, gbias_ref, gskip_ref,
    low_part, io_part, low_land, io_land, low_all, io_all, wide, sum_send, sum_recv, all_send, all_recv,
    small_land, small_back, small_all, s_send, s_recv, t_send, t_recv,
    gate_land, in_out, in_land, hand_send, hand_recv, proj, proj_t, x_grad0, x_grad1,
    u_ref, xw_ref, dsig_ref, load_sem, *scratch,
):
    rings = [scratch[k * RING : (k + 1) * RING] for k in range(4)]
    step_ring, x_ring = rings[:2], rings[2:]
    step_grad = [step_grad.at[q] for q in range(2)]
    x_grad = [x_grad0, x_grad1]
    section = lax.axis_index("section")
    me = lax.axis_index("ctx")
    partners = others("ctx", CTX) + others("ch", CH) + [{"section": 1 - section}]
    greet(partners)
    loads = [
        pltpu.make_async_copy(src, dst, load_sem.at[k])
        for k, (src, dst) in enumerate(((u_hbm, u_ref), (xw_hbm, xw_ref), (dsig_hbm, dsig_ref)))
    ]
    for load in loads:
        load.start()
    prepare(part_ref, low_part, io_part)
    met(partners)
    gate_copy = remote(dgate_ref, gate_land, hand_send.at[0], hand_recv.at[0], {"section": 1 - section})
    in_copy = remote(in_out, in_land, hand_send.at[1], hand_recv.at[1], {"section": 1 - section})

    sums = sum_start(low_part, io_part, low_land, io_land, sum_send, sum_recv)
    first = plane_start(step_grad, step_ring)

    @pl.when(section == 1)
    def _():
        gate_copy.start()

    small_there = spread_start(small_in, small_land, s_send, s_recv)
    shares = share_start(sums, part_ref, io_part, low_land, io_land, low_all, io_all, all_send, all_recv)
    first = plane_middle(step_grad, step_ring, first)
    for copy in small_there:
        copy.wait_recv()
    total = small_land[0]
    for c in range(1, CTX):
        total = total + small_land[c]
    small_all[me] = total
    small_home = []
    for d, to in enumerate(others("ctx", CTX)):
        small_home.append(remote(small_all.at[me], small_all.at[me], t_send.at[d], t_recv.at[d], to))
        small_home[-1].start()

    share_finish(shares, low_all, io_all, wide)
    proj[...] = wide[...].astype(BF16)
    proj_t[...] = wide[...].T.astype(BF16)

    for load in loads:
        load.wait()

    def product(c, _):
        columns = pl.ds(pl.multiple_of(c * TILE, TILE), TILE)
        grad = jnp.dot(
            proj_t[: R + 2 * N, :], u_ref[:, columns], preferred_element_type=F32
        ).astype(BF16)
        x, y_high = c // 2, lax.rem(c, 2)
        for e in range(2):
            x_grad0[x, y_high, e] = grad[: X_ROWS[0], lanes(e)]
            x_grad1[2 * y_high + e, x // 2, lax.rem(x, 2)] = grad[X_ROWS[0] :, lanes(e)]
        return 0

    lax.fori_loop(0, CTX // 2, product, 0)
    first_x = plane_start(x_grad, x_ring)

    @pl.when(section == 1)
    def _():
        def one(j, _):
            columns = pl.ds(pl.multiple_of(j * TILE, TILE), TILE)
            in_out[:, columns] = (
                dsig_ref[:, columns]
                + lax.dot_general(
                    proj[:, : R + 2 * N], xw_ref[:, columns], (((1,), (0,)), ((), ())),
                    preferred_element_type=F32,
                )
            ).astype(BF16)
            return 0

        lax.fori_loop(0, u_ref.shape[1] // TILE, one, 0)
        in_copy.start()
        hin_ref[...] = jnp.zeros_like(hin_ref)
        hgate_ref[...] = jnp.zeros_like(hgate_ref)

    turned = plane_turn(step_grad, step_ring, first, left_half)
    first_x = plane_middle(x_grad, x_ring, first_x)
    turned = plane_second_middle(step_ring, turned)
    for copy in small_home:
        copy.wait_recv()
    for c in range(CTX):
        gdecay_ref[:, lanes(c)] = small_all[c, :N]
        gbias_ref[:, lanes(c)] = small_all[c, N : N + 1]
        gskip_ref[:, lanes(c)] = small_all[c, N + 1 : N + 2]
    for q, halves in enumerate(plane_finish(step_ring, turned)):
        for h in range(2):
            gstep_ref[q * 16 : (q + 1) * 16, h * 1024 : (h + 1) * 1024] = halves[h]
    turned_x = plane_turn(x_grad, x_ring, first_x, top_half)

    @pl.when(section == 0)
    def _():
        gate_copy.wait_recv()
        in_copy.wait_recv()
        hgate_ref[...] = gate_land[...]
        hin_ref[...] = in_land[...]

    turned_x = plane_second_middle(x_ring, turned_x)
    for q, halves in enumerate(plane_finish(x_ring, turned_x)):
        for h in range(2):
            rows = X_ROWS[q] // 2
            gx_ref[q * X_ROWS[0] + h * rows : q * X_ROWS[0] + (h + 1) * rows, :] = halves[h]

    @pl.when(section == 1)
    def _():
        gate_copy.wait_send()
        in_copy.wait_send()

    for copy in sums + shares + small_there + small_home:
        copy.wait_send()
    for copies in first + turned + first_x + turned_x:
        ring_done(copies)


def run_tail(part, small, dgate, step_grad, u, xw, dsig):
    ch = u.shape[1]
    f = lambda *s: jax.ShapeDtypeStruct(s, F32)
    b = lambda *s: jax.ShapeDtypeStruct(s, BF16)
    return pl.pallas_call(
        tail,
        in_specs=in_vmem(4) + [pl.BlockSpec(memory_space=pl.ANY)] * 3,
        out_specs=in_vmem(7),
        out_shape=[
            b(TOK, ch), b(TOK, ch), f(R + 2 * N, LANE), f(32, ch), f(N, ch), f(1, ch), f(1, ch),
        ],
        scratch_shapes=sum_scratch(BF16)
        + [pltpu.VMEM((CTX, SMALL, LANE), F32)] * 3
        + [pltpu.SemaphoreType.DMA((CTX - 1,))] * 4
        + [pltpu.VMEM((TOK, ch), BF16)] * 3
        + [pltpu.SemaphoreType.DMA((2,))] * 2
        + [pltpu.VMEM((TOK, WIDE), BF16), pltpu.VMEM((WIDE, TOK), BF16)]
        + [pltpu.VMEM((SIDE, 2, 2, rows, LANE), BF16) for rows in X_ROWS]
        + [pltpu.VMEM(u.shape, BF16), pltpu.VMEM(xw.shape, BF16), pltpu.VMEM(dsig.shape, F32)]
        + [pltpu.SemaphoreType.DMA((3,))]
        + ring_scratch((2, 16, 2048), (16, 1024)) * 2
        + ring_scratch((2, X_ROWS[0], LANE), (X_ROWS[0] // 2, LANE))
        + ring_scratch((2, X_ROWS[1], LANE), (X_ROWS[1] // 2, LANE)),
        compiler_params=pltpu.CompilerParams(
            collective_id=2, has_side_effects=True, vmem_limit_bytes=VMEM_BYTES
        ),
        name="tail",
    )(part, small, dgate, step_grad, u, xw, dsig)


def finish(*refs):
    count = len(refs) // 2
    for k in range(count):
        refs[count + k][...] = refs[k][...]


def run_finish(*results):
    return pl.pallas_call(
        finish,
        in_specs=in_vmem(len(results)),
        out_specs=in_vmem(len(results)),
        out_shape=[jax.ShapeDtypeStruct(r.shape, r.dtype) for r in results],
        compiler_params=pltpu.CompilerParams(vmem_limit_bytes=VMEM_BYTES),
        name="finish",
    )(*results)


def body(mixer_input, gate_input, upstream_grad, x_weight, step_weight, step_bias, decay_log, skip_gain):
    u, z, g = mixer_input[0], gate_input[0], upstream_grad[0]
    weight_x, weight_step = jnp.swapaxes(x_weight[0], 0, 1), step_weight[0]
    dlog = decay_log[0]
    low, io = run_sum(u, weight_x)
    *kept, pack, bsum = run_first(low, io, weight_step, step_bias, dlog, u, z, g)
    across = run_exchange(pack, dlog)
    d_gate, d_signal, d_part, grad_step, small = run_second(
        low, io, weight_step, dlog, skip_gain, u, z, g, [*kept, bsum], across
    )
    handed_input, handed_gate, grad_x, grad_step, g_decay, g_bias, g_skip = run_finish(
        *run_tail(d_part, small, d_gate, grad_step, u, weight_x, d_signal)
    )
    return (
        handed_input[None], handed_gate[None], jnp.swapaxes(grad_x, 0, 1)[None], grad_step[None],
        g_bias, g_decay[None], g_skip,
    )


def solution(mesh):
    return jax.shard_map(
        body,
        mesh=mesh,
        in_specs=(
            P("section", "ctx", "ch"), P("section", "ctx", "ch"), P("section", "ctx", "ch"),
            P("section", "ch", None), P("section", None, "ch"), P("section", "ch"),
            P("section", None, "ch"), P("section", "ch"),
        ),
        out_specs=(
            P("section", "ctx", "ch"), P("section", "ctx", "ch"), P("section", ("ch", "ctx"), None),
            P("section", "ctx", "ch"), P("section", "ch"), P("section", None, "ch"), P("section", "ch"),
        ),
        check_vma=False,
    )
```

```python
import functools

import jax
import jax.numpy as jnp
from jax import lax
from jax.experimental import pallas as pl
from jax.experimental.pallas import tpu as pltpu
from jax.sharding import PartitionSpec as P

R = 512
N = 16
TOK = 192
STEPS = 24
ROWS = 8
TILE = 256
LANE = 128
HALVES = TILE // LANE
CHUNK = 4
VMEM_BYTES = 60 * 2**20
SIDE = 4
CTX = 16
CH = 8
PIECE = TOK // CH
WIDE = R + LANE
PACK = 40
SMALL = 24
MESH = pl.DeviceIdType.MESH
F32 = jnp.float32
BF16 = jnp.bfloat16


def every(i):
    return pl.ds(i, ROWS, stride=STEPS)


def lanes(k):
    return slice(k * LANE, (k + 1) * LANE)


def by_step(ref, value, by_token):
    for k in range(HALVES):
        by_token[k] = value[:, lanes(k)]
        for i in range(STEPS):
            ref[k, i] = by_token[k, every(i), :]


def from_step(ref, by_token):
    for k in range(HALVES):
        for i in range(STEPS):
            by_token[k, every(i), :] = ref[k, i]
    return jnp.concatenate([by_token[k] for k in range(HALVES)], axis=1)


def row_index():
    return lax.broadcasted_iota(jnp.int32, (ROWS, LANE), 0)


def spread_columns(io_ref, spread):
    def one(i, _):
        rows = io_ref[every(i), :]
        for n in range(2 * N):
            spread[i, n] = jnp.broadcast_to(rows[:, n : n + 1], (ROWS, LANE))
        return 0

    lax.fori_loop(0, STEPS, one, 0)


def inverse(value):
    rough = pl.reciprocal(value, approx=True)
    return rough * (2.0 - value * rough)


def scan_rows(decay, value, reverse):
    row = row_index()
    for k in (1, 2, 4):
        shift = ROWS - k if reverse else k
        inside = row < ROWS - k if reverse else row >= k
        value = value + decay * jnp.where(inside, pltpu.roll(value, shift, 0), 0.0)
        if k < 4:
            decay = decay * jnp.where(inside, pltpu.roll(decay, shift, 0), 1.0)
    return value


def first_pass(
    low_ref, io_ref, w_ref, bias_ref, dlog_ref, all_dlog_ref, u_ref, z_ref, g_ref,
    step_ref, token_ref, sig_ref, drive, seed, decay_ref, entry_ref, exit_ref, bsum_ref, across_ref,
    spread, by_drive, by_seed, by_step_size, rates,
    pack, landed, back, result, send, recv, back_send, back_recv,
):
    tile = pl.program_id(0)
    last = pl.num_programs(0) - 1
    me = lax.axis_index("ctx")
    @pl.when(tile == 0)
    def _():
        greet(others("ctx", CTX))
        spread_columns(io_ref, spread)

    pre = jnp.dot(low_ref[...], w_ref[...], preferred_element_type=F32) + bias_ref[...]
    small = jnp.exp(-jnp.abs(pre))
    above = inverse(1.0 + small)
    series = small * (1.0 - small * (0.5 - small * (1.0 / 3.0)))
    step = jnp.maximum(pre, 0.0) + jnp.where(small < 1e-3, series, jnp.log(1.0 + small))
    sig_ref[...] = jnp.where(pre >= 0.0, above, small * above)
    z = z_ref[...].astype(F32)
    token_ref[...] = step
    by_step(step_ref, step, by_step_size)
    by_step(drive, step * u_ref[...].astype(F32), by_drive)
    by_step(seed, g_ref[...].astype(F32) * z * inverse(1.0 + jnp.exp(-z)), by_seed)
    rates[...] = -jnp.exp(dlog_ref[...])
    row = row_index()

    total = jnp.zeros((ROWS, TILE), F32)
    for i in range(STEPS):
        total = total + jnp.concatenate([step_ref[k, i] for k in range(HALVES)], axis=1)
    bsum_ref[...] = total
    whole_sum = jnp.sum(total, axis=0, keepdims=True)
    for k in range(HALVES):
        pack[HALVES * tile + k, 2 * N :, :] = jnp.broadcast_to(whole_sum[:, lanes(k)], (PACK - 2 * N, LANE))

    for c in range(N // CHUNK):
        pairs = [(n, k) for n in range(c * CHUNK, (c + 1) * CHUNK) for k in range(HALVES)]
        rate = [jnp.broadcast_to(rates[n : n + 1, lanes(k)], (ROWS, LANE)) for n, k in pairs]

        def one(i, carry):
            state, decay, start = carry
            st = [step_ref[k, i] for k in range(HALVES)]
            dr = [drive[k, i] for k in range(HALVES)]
            sd = [seed[k, i] for k in range(HALVES)]
            new_state, new_decay, new_start = [], [], []
            for p, (n, k) in enumerate(pairs):
                a = jnp.exp(st[k] * rate[p])
                decay_ref[k, i, n] = a
                new_state.append(a * state[p] + dr[k] * spread[i, n])
                d = a * decay[p]
                new_decay.append(d)
                new_start.append(start[p] + d * (sd[k] * spread[i, N + n]))
            return tuple(new_state), tuple(new_decay), tuple(new_start)

        zero = tuple(jnp.zeros((ROWS, LANE), F32) for _ in pairs)
        ones = tuple(jnp.ones((ROWS, LANE), F32) for _ in pairs)
        state, decay, start = lax.fori_loop(0, STEPS, one, (zero, ones, zero), unroll=12)
        for p, (n, k) in enumerate(pairs):
            ends = scan_rows(decay[p], state[p], False)
            starts = scan_rows(decay[p], start[p], True)
            entry_ref[n, :, lanes(k)] = jnp.where(row >= 1, pltpu.roll(ends, 1, 0), 0.0)
            exit_ref[n, :, lanes(k)] = jnp.where(row < ROWS - 1, pltpu.roll(starts, ROWS - 1, 0), 0.0)
            pack[HALVES * tile + k, n : n + 1, :] = ends[ROWS - 1 :, :]
            pack[HALVES * tile + k, N + n : N + n + 1, :] = starts[:1, :]

    @pl.when(tile == 0)
    def _():
        met(others("ctx", CTX))

    def chunk_to(c):
        return remote(pack.at[c], landed.at[me], send.at[c], recv.at[me], {"ctx": c})

    def chunk_from(c):
        return remote(pack.at[c], landed.at[c], send.at[c], recv.at[c], {"ctx": c})

    def answers():
        return [
            remote(back.at[to["ctx"]], result.at[me], back_send.at[d], back_recv.at[d], to)
            for d, to in enumerate(others("ctx", CTX))
        ]

    for k in range(HALVES):
        c = HALVES * tile + k

        @pl.when(c != me)
        def _():
            chunk_to(c).start()

        @pl.when(c == me)
        def _():
            landed[me] = pack[me]

    @pl.when(tile == jnp.minimum(me // HALVES + 1, last))
    def _():
        for c in range(CTX):
            @pl.when(c != me)
            def _():
                chunk_from(c).wait_recv()

        mine = -jnp.exp(all_dlog_ref[:, pl.ds(pl.multiple_of(me * LANE, LANE), LANE)])
        state = jnp.zeros((N, LANE), F32)
        adjoint = jnp.zeros((N, LANE), F32)
        for c in range(CTX):
            r = CTX - 1 - c
            back[c, :N] = state
            back[r, N:] = adjoint
            state = jnp.exp(landed[c, 2 * N : 2 * N + 1] * mine) * state + landed[c, :N]
            adjoint = jnp.exp(landed[r, 2 * N : 2 * N + 1] * mine) * adjoint + landed[r, N : 2 * N]
        result[me] = back[me]
        for copy in answers():
            copy.start()

    @pl.when(tile == last)
    def _():
        for copy in answers():
            copy.wait_recv()
        across_ref[...] = result[...]
        for copy in answers():
            copy.wait_send()
        for c in range(CTX):
            @pl.when(c != me)
            def _():
                chunk_to(c).wait_send()


def sum_before(value, reverse):
    row = lax.broadcasted_iota(jnp.int32, value.shape, 0)
    held = value
    for k in (1, 2, 4):
        shift = ROWS - k if reverse else k
        inside = row < ROWS - k if reverse else row >= k
        held = held + jnp.where(inside, pltpu.roll(held, shift, 0), 0.0)
    return held - value


def second_pass(
    low_ref, io_ref, w_ref, dlog_ref, skip_ref, u_ref, z_ref, g_ref, step_ref, token_ref, sig_ref, drive, seed, decay_ref,
    entry_ref, exit_ref, bsum_ref, across_ref,
    dgate_ref, dsig_ref, part_ref, gstep_ref, small_ref,
    spread, sums, held, scanned, grad_drive, grad_decay, by_scan, by_grad, by_decay, rates, by_token, low_t,
):
    tile = pl.program_id(0)

    @pl.when(tile == 0)
    def _():
        spread_columns(io_ref, spread)
        sums[...] = jnp.zeros_like(sums)
        part_ref[...] = jnp.zeros_like(part_ref)
        low_t[...] = low_ref[...].astype(F32).T.astype(BF16)

    rates[...] = -jnp.exp(dlog_ref[...])
    prior = sum_before(bsum_ref[...], False)
    later = sum_before(bsum_ref[...], True)

    def so_far(ref, c, i):
        if c == 0:
            return [jnp.zeros((ROWS, LANE), F32) for k in range(HALVES)]
        return [ref[k, i] for k in range(HALVES)]

    for c in range(N // CHUNK):
        numbers = range(c * CHUNK, (c + 1) * CHUNK)
        pairs = [(n, k) for n in numbers for k in range(HALVES)]
        rate = [jnp.broadcast_to(rates[n : n + 1, lanes(k)], (ROWS, LANE)) for n, k in pairs]

        def forward(i, state, c=c, numbers=numbers, rate=rate):
            dr = [drive[k, i] for k in range(HALVES)]
            sd = [seed[k, i] for k in range(HALVES)]
            out = so_far(scanned, c, i)
            new = []
            for m, n in enumerate(numbers):
                b_in, b_out = spread[i, n], spread[i, N + n]
                d_out = sums[i, N + n]
                for k in range(HALVES):
                    p = m * HALVES + k
                    held[i, m, :, lanes(k)] = state[p]
                    now = decay_ref[k, i, n] * state[p] + dr[k] * b_in
                    new.append(now)
                    out[k] = out[k] + b_out * now
                    d_out = d_out + sd[k] * now
                sums[i, N + n] = d_out
            for k in range(HALVES):
                scanned[k, i] = out[k]
            return tuple(new)

        state = tuple(
            entry_ref[n, :, lanes(k)]
            + jnp.exp(prior[:, lanes(k)] * rate[p]) * across_ref[k, n : n + 1, :]
            for p, (n, k) in enumerate(pairs)
        )
        lax.fori_loop(0, STEPS, forward, state, unroll=8)

        def backward(j, carry, c=c, numbers=numbers, rate=rate):
            incoming, total = carry
            i = STEPS - 1 - j
            st = [step_ref[k, i] for k in range(HALVES)]
            dr = [drive[k, i] for k in range(HALVES)]
            sd = [seed[k, i] for k in range(HALVES)]
            g_drive = so_far(grad_drive, c, i)
            g_decay = so_far(grad_decay, c, i)
            new_in, new_total = [], []
            for m, n in enumerate(numbers):
                b_in, b_out = spread[i, n], spread[i, N + n]
                d_in = sums[i, n]
                for k in range(HALVES):
                    p = m * HALVES + k
                    adjoint = b_out * sd[k] + incoming[p]
                    passed = decay_ref[k, i, n] * adjoint
                    pulled = passed * held[i, m, :, lanes(k)]
                    new_in.append(passed)
                    new_total.append(total[p] + pulled * st[k])
                    g_decay[k] = g_decay[k] + pulled * rate[p]
                    g_drive[k] = g_drive[k] + adjoint * b_in
                    d_in = d_in + adjoint * dr[k]
                sums[i, n] = d_in
            for k in range(HALVES):
                grad_drive[k, i] = g_drive[k]
                grad_decay[k, i] = g_decay[k]
            return tuple(new_in), tuple(new_total)

        incoming = tuple(
            exit_ref[n, :, lanes(k)]
            + jnp.exp(later[:, lanes(k)] * rate[p]) * across_ref[k, N + n : N + n + 1, :]
            for p, (n, k) in enumerate(pairs)
        )
        zero = tuple(jnp.zeros((ROWS, LANE), F32) for _ in pairs)
        _, total = lax.fori_loop(0, STEPS, backward, (incoming, zero), unroll=8)
        for p, (n, k) in enumerate(pairs):
            small_ref[k, n : n + 1, :] = (
                jnp.sum(total[p], axis=0, keepdims=True) * rates[n : n + 1, lanes(k)]
            )

    u = u_ref[...].astype(F32)
    z = z_ref[...].astype(F32)
    g = g_ref[...].astype(F32)
    gate_sig = inverse(1.0 + jnp.exp(-z))
    seeds = g * z * gate_sig
    skip = skip_ref[...]
    from_drive = from_step(grad_drive, by_grad)
    mixed = from_step(scanned, by_scan) + skip * u
    dgate_ref[...] = (g * mixed * gate_sig * (1.0 + z * (1.0 - gate_sig))).astype(BF16)
    dsig_ref[...] = from_drive * token_ref[...] + skip * seeds
    d_pre = (from_drive * u + from_step(grad_decay, by_decay)) * sig_ref[...]
    pre = d_pre.astype(BF16)
    bias_row = jnp.sum(d_pre, axis=0, keepdims=True)
    skip_row = jnp.sum(seeds * u, axis=0, keepdims=True)
    for k in range(HALVES):
        small_ref[k, N : N + 1, :] = bias_row[:, lanes(k)]
        small_ref[k, N + 1 : N + 2, :] = skip_row[:, lanes(k)]
        small_ref[k, N + 2 :, :] = jnp.zeros((SMALL - N - 2, LANE), F32)
    part_ref[:, :R] += lax.dot_general(
        pre, w_ref[...], (((1,), (1,)), ((), ())), preferred_element_type=F32
    )
    grad = jnp.dot(low_t[...], pre, preferred_element_type=F32).astype(BF16)
    for x in range(SIDE):
        for y in range(SIDE):
            at = (x * SIDE + y) * 2 * 16
            gstep_ref[0, x, y // 2, y % 2] = grad[at : at + 16]
            gstep_ref[1, y, x // 2, x % 2] = grad[at + 16 : at + 32]

    @pl.when(tile == pl.num_programs(0) - 1)
    def _():
        column = lax.broadcasted_iota(jnp.int32, (ROWS, LANE), 1)

        def one(i, _):
            rows = jnp.zeros((ROWS, LANE), F32)
            for n in range(2 * N):
                rows = jnp.where(column == n, jnp.sum(sums[i, n], axis=1, keepdims=True), rows)
            by_token[every(i), :] = rows
            return 0

        lax.fori_loop(0, STEPS, one, 0)
        part_ref[:, R:] = by_token[...]


def whole(*shape):
    return pl.BlockSpec(shape, lambda j: (0,) * len(shape))


def tiled(*lead):
    return pl.BlockSpec(lead + (TILE,), lambda j: (0,) * len(lead) + (j,))


def stacked(*rows):
    return pl.BlockSpec((HALVES,) + rows + (LANE,), lambda j: (j,) + (0,) * (len(rows) + 1))


def run_first(low, io, weight, bias, dlog, u, z, g):
    ch = u.shape[1]
    f = lambda *s: jax.ShapeDtypeStruct(s, F32)
    return pl.pallas_call(
        first_pass,
        grid=(ch // TILE,),
        in_specs=[
            whole(TOK, R), whole(TOK, io.shape[1]), tiled(R), tiled(1), tiled(N), whole(N, ch),
            tiled(TOK), tiled(TOK), tiled(TOK),
        ],
        out_specs=[
            stacked(STEPS, ROWS), tiled(TOK), tiled(TOK), stacked(STEPS, ROWS), stacked(STEPS, ROWS),
            stacked(STEPS, N, ROWS), tiled(N, ROWS), tiled(N, ROWS), tiled(ROWS), whole(CTX, 2 * N, LANE),
        ],
        out_shape=[
            f(ch // LANE, STEPS, ROWS, LANE), f(TOK, ch), f(TOK, ch), f(ch // LANE, STEPS, ROWS, LANE),
            f(ch // LANE, STEPS, ROWS, LANE), f(ch // LANE, STEPS, N, ROWS, LANE),
            f(N, ROWS, ch), f(N, ROWS, ch),
            f(ROWS, ch), f(CTX, 2 * N, LANE),
        ],
        scratch_shapes=[
            pltpu.VMEM((STEPS, 2 * N, ROWS, LANE), F32),
            pltpu.VMEM((HALVES, TOK, LANE), F32),
            pltpu.VMEM((HALVES, TOK, LANE), F32),
            pltpu.VMEM((HALVES, TOK, LANE), F32),
            pltpu.VMEM((N, TILE), F32),
            pltpu.VMEM((CTX, PACK, LANE), F32),
            pltpu.VMEM((CTX, PACK, LANE), F32),
            pltpu.VMEM((CTX, 2 * N, LANE), F32),
            pltpu.VMEM((CTX, 2 * N, LANE), F32),
            pltpu.SemaphoreType.DMA((CTX,)),
            pltpu.SemaphoreType.DMA((CTX,)),
            pltpu.SemaphoreType.DMA((CTX - 1,)),
            pltpu.SemaphoreType.DMA((CTX - 1,)),
        ],
        compiler_params=pltpu.CompilerParams(
            collective_id=1, has_side_effects=True, vmem_limit_bytes=VMEM_BYTES
        ),
        name="first_pass",
    )(low, io, weight, bias, dlog, dlog, u, z, g)


def run_second(low, io, weight, dlog, skip, u, z, g, kept, across):
    ch = u.shape[1]
    f = lambda *s: jax.ShapeDtypeStruct(s, F32)
    return pl.pallas_call(
        second_pass,
        grid=(ch // TILE,),
        in_specs=[
            whole(TOK, R), whole(TOK, io.shape[1]), tiled(R), tiled(N), tiled(1),
            tiled(TOK), tiled(TOK), tiled(TOK), stacked(STEPS, ROWS), tiled(TOK), tiled(TOK),
            stacked(STEPS, ROWS), stacked(STEPS, ROWS), stacked(STEPS, N, ROWS), tiled(N, ROWS), tiled(N, ROWS), tiled(ROWS), stacked(2 * N),
        ],
        out_specs=[
            tiled(TOK), tiled(TOK), whole(TOK, WIDE), tiled(2, SIDE, 2, 2, 16), stacked(SMALL),
        ],
        out_shape=[
            jax.ShapeDtypeStruct((TOK, ch), BF16), f(TOK, ch), f(TOK, WIDE),
            jax.ShapeDtypeStruct((2, SIDE, 2, 2, 16, ch), BF16), f(ch // LANE, SMALL, LANE),
        ],
        scratch_shapes=[
            pltpu.VMEM((STEPS, 2 * N, ROWS, LANE), F32),
            pltpu.VMEM((STEPS, 2 * N, ROWS, LANE), F32),
            pltpu.VMEM((STEPS, CHUNK, ROWS, TILE), F32),
        ]
        + [pltpu.VMEM((HALVES, STEPS, ROWS, LANE), F32)] * 3
        + [pltpu.VMEM((HALVES, TOK, LANE), F32)] * 3
        + [pltpu.VMEM((N, TILE), F32), pltpu.VMEM((TOK, LANE), F32), pltpu.VMEM((R, TOK), BF16)],
        compiler_params=pltpu.CompilerParams(vmem_limit_bytes=VMEM_BYTES),
        name="second_pass",
    )(low, io, weight, dlog, skip, u, z, g, *kept, across)


def greet(partners):
    for partner in partners:
        pl.semaphore_signal(
            pltpu.get_barrier_semaphore(), inc=1, device_id=partner, device_id_type=MESH
        )


def met(partners):
    pl.semaphore_wait(pltpu.get_barrier_semaphore(), len(partners))


def remote(src, dst, send, recv, to):
    return pltpu.make_async_remote_copy(
        src_ref=src, dst_ref=dst, send_sem=send, recv_sem=recv, device_id=to, device_id_type=MESH
    )


def others(axis, count):
    me = lax.axis_index(axis)
    return [{axis: lax.rem(me + d, count)} for d in range(1, count)]


def token_rows(owner):
    return pl.ds(pl.multiple_of(owner * PIECE, 8), PIECE)


def fold(rows):
    return rows[:ROWS] + pltpu.roll(rows[ROWS : 2 * ROWS], 2 * N, 1) + pltpu.roll(rows[2 * ROWS :], 4 * N, 1)


def unfold(folded):
    used = lax.broadcasted_iota(jnp.int32, (ROWS, LANE), 1) < 2 * N
    parts = [folded, pltpu.roll(folded, LANE - 2 * N, 1), pltpu.roll(folded, LANE - 4 * N, 1)]
    return jnp.concatenate([jnp.where(used, part, 0.0) for part in parts], axis=0)


def over(rows):
    return jnp.concatenate([rows[:, : R // 2], rows[:, R // 2 : R]], axis=0)


def prepare(part_ref, low_part, io_part):
    for p in range(CH):
        rows = part_ref[p * PIECE : (p + 1) * PIECE, :]
        low_part[p] = over(rows).astype(low_part.dtype)
        io_part[p] = fold(rows[:, R:])


def sum_start(low_part, io_part, low_land, io_land, send, recv):
    copies = []
    for d, to in enumerate(others("ch", CH)):
        copies.append(remote(low_part.at[to["ch"]], low_land.at[d], send.at[0, d], recv.at[0, d], to))
        copies.append(remote(io_part.at[to["ch"]], io_land.at[d], send.at[1, d], recv.at[1, d], to))
    for copy in copies:
        copy.start()
    return copies


def share_start(sums, part_ref, io_part, low_land, io_land, low_all, io_all, send, recv):
    me = lax.axis_index("ch")
    for copy in sums:
        copy.wait_recv()
    low = over(part_ref[token_rows(me), :])
    io = io_part[me]
    for d in range(CH - 1):
        low = low + low_land[d].astype(F32)
        io = io + io_land[d]
    low_all[me] = low.astype(BF16)
    io_all[me] = io
    copies = []
    for d, to in enumerate(others("ch", CH)):
        copies.append(remote(low_all.at[me], low_all.at[me], send.at[0, d], recv.at[0, d], to))
        copies.append(remote(io_all.at[me], io_all.at[me], send.at[1, d], recv.at[1, d], to))
    for copy in copies:
        copy.start()
    return copies


def share_finish(copies, low_all, io_all, wide):
    for copy in copies:
        copy.wait_recv()
    for p in range(CH):
        both = low_all[p].astype(F32)
        rows = slice(p * PIECE, (p + 1) * PIECE)
        wide[rows, : R // 2] = both[:PIECE]
        wide[rows, R // 2 : R] = both[PIECE:]
        wide[rows, R:] = unfold(io_all[p])


def sum_scratch(sent):
    return [
        pltpu.VMEM((CH, 2 * PIECE, R // 2), sent),
        pltpu.VMEM((CH, ROWS, LANE), F32),
        pltpu.VMEM((CH - 1, 2 * PIECE, R // 2), sent),
        pltpu.VMEM((CH - 1, ROWS, LANE), F32),
        pltpu.VMEM((CH, 2 * PIECE, R // 2), BF16),
        pltpu.VMEM((CH, ROWS, LANE), F32),
        pltpu.VMEM((TOK, WIDE), F32),
        pltpu.SemaphoreType.DMA((2, CH - 1)),
        pltpu.SemaphoreType.DMA((2, CH - 1)),
        pltpu.SemaphoreType.DMA((2, CH - 1)),
        pltpu.SemaphoreType.DMA((2, CH - 1)),
    ]


def sum_projected(u_ref, xt_ref, low_ref, io_ref, part_ref, *scratch):
    low_part, io_part, low_land, io_land, low_all, io_all, wide, sum_send, sum_recv, all_send, all_recv = scratch
    greet(others("ch", CH))
    part_ref[:, R:] = jnp.zeros((TOK, LANE), F32)
    part_ref[:, : R + 2 * N] = lax.dot_general(
        u_ref[...], xt_ref[...], (((1,), (1,)), ((), ())), preferred_element_type=F32
    )
    prepare(part_ref, low_part, io_part)
    met(others("ch", CH))
    sums = sum_start(low_part, io_part, low_land, io_land, sum_send, sum_recv)
    shares = share_start(sums, part_ref, io_part, low_land, io_land, low_all, io_all, all_send, all_recv)
    share_finish(shares, low_all, io_all, wide)
    low_ref[...] = wide[:, :R].astype(BF16)
    io_ref[...] = wide[:, R:]
    for copy in sums + shares:
        copy.wait_send()


def in_vmem(count):
    return [pl.BlockSpec(memory_space=pltpu.VMEM)] * count


def run_sum(u, xt):
    return pl.pallas_call(
        sum_projected,
        in_specs=in_vmem(2),
        out_specs=in_vmem(2),
        out_shape=[jax.ShapeDtypeStruct((TOK, R), BF16), jax.ShapeDtypeStruct((TOK, LANE), F32)],
        scratch_shapes=[pltpu.VMEM((TOK, WIDE), F32)] + sum_scratch(F32),
        compiler_params=pltpu.CompilerParams(
            collective_id=0, has_side_effects=True, vmem_limit_bytes=VMEM_BYTES
        ),
        name="sum_projected",
    )(u, xt)


def spread_start(src, dst, send, recv):
    me = lax.axis_index("ctx")
    copies = []
    for d, to in enumerate(others("ctx", CTX)):
        copies.append(remote(src.at[to["ctx"]], dst.at[me], send.at[d], recv.at[d], to))
        copies[-1].start()
    dst[me] = src[me]
    return copies


def neighbour(axis, d):
    me = lax.axis_index("ctx")
    x, y = me // SIDE, lax.rem(me, SIDE)
    if axis == 0:
        return {"ctx": lax.rem(x + d + SIDE, SIDE) * SIDE + y}
    return {"ctx": x * SIDE + lax.rem(y + d + SIDE, SIDE)}


def place(axis, d=0):
    me = lax.axis_index("ctx")
    at = me // SIDE if axis == 0 else lax.rem(me, SIDE)
    return lax.rem(at + d + SIDE, SIDE)


WAYS = ((0, 1, 0), (1, -1, 1))


def ring_start(axis, src, relay, land, send, recv):
    passing, direct = [], []
    for way, d, half in WAYS:
        to = neighbour(axis, d)
        passing.append(remote(src.at[place(axis, 2), half], relay.at[way], send.at[0, way], recv.at[0, way], to))
        direct.append(
            remote(src.at[place(axis, d), 1 - half], land.at[way, 1 - half], send.at[1, way], recv.at[1, way], to)
        )
        passing[-1].start()
    for copy in direct:
        copy.start()
    return passing, direct


def ring_middle(axis, src, relay, land, send, recv, copies):
    passing, direct = copies
    last = []
    for way, d, half in WAYS:
        passing[way].wait_recv()
        mine = src[place(axis, d), half]
        relay[way] = (relay[way].astype(F32) + mine.astype(F32)).astype(BF16)
        last.append(
            remote(relay.at[way], land.at[way, half], send.at[2, way], recv.at[2, way], neighbour(axis, d))
        )
        last[-1].start()
    return passing, direct, last


def ring_finish(axis, src, land, copies):
    _, direct, last = copies
    for copy in direct + last:
        copy.wait_recv()
    mine = place(axis)
    return [
        src[mine, h].astype(F32) + land[0, h].astype(F32) + land[1, h].astype(F32) for h in range(2)
    ]


def ring_done(copies):
    for group in copies:
        for copy in group:
            copy.wait_send()


RING = 9


def ring_scratch(unit, second):
    return [
        pltpu.VMEM((2,) + unit, BF16),
        pltpu.VMEM((2, 2) + unit, BF16),
        pltpu.VMEM((SIDE, 2) + second, BF16),
        pltpu.VMEM((2,) + second, BF16),
        pltpu.VMEM((2, 2) + second, BF16),
        pltpu.SemaphoreType.DMA((3, 2)),
        pltpu.SemaphoreType.DMA((3, 2)),
        pltpu.SemaphoreType.DMA((3, 2)),
        pltpu.SemaphoreType.DMA((3, 2)),
    ]


def plane_start(src, rings):
    started = []
    for q, (relay, land, _, _, _, send, recv, _, _) in enumerate(rings):
        started.append(ring_start(q, src[q], relay, land, send, recv))
    return started


def plane_middle(src, rings, copies):
    passed = []
    for q, (relay, land, _, _, _, send, recv, _, _) in enumerate(rings):
        passed.append(ring_middle(q, src[q], relay, land, send, recv, copies[q]))
    return passed


def plane_turn(src, rings, copies, split):
    started = []
    for q, (_, land, second, relay, land2, _, _, send, recv) in enumerate(rings):
        halves = ring_finish(q, src[q], land, copies[q])
        for o in range(SIDE):
            for h in range(2):
                second[o, h] = split(halves[o // 2][o % 2], h).astype(BF16)
        started.append(ring_start(1 - q, second, relay, land2, send, recv))
    return started


def plane_second_middle(rings, copies):
    passed = []
    for q, (_, _, second, relay, land2, _, _, send, recv) in enumerate(rings):
        passed.append(ring_middle(1 - q, second, relay, land2, send, recv, copies[q]))
    return passed


def plane_finish(rings, copies):
    return [ring_finish(1 - q, rings[q][2], rings[q][4], copies[q]) for q in range(2)]


def left_half(value, h):
    columns = value.shape[1] // 2
    return value[:, h * columns : (h + 1) * columns]


def top_half(value, h):
    rows = value.shape[0] // 2
    return value[h * rows : (h + 1) * rows]


X_ROWS = (288, 256)


def tail(
    part_ref, small_in, dgate_ref, step_grad, u_hbm, xw_hbm, dsig_hbm,
    hin_ref, hgate_ref, gx_ref, gstep_ref, gdecay_ref, gbias_ref, gskip_ref,
    low_part, io_part, low_land, io_land, low_all, io_all, wide, sum_send, sum_recv, all_send, all_recv,
    small_land, small_back, small_all, s_send, s_recv, t_send, t_recv,
    gate_land, in_out, in_land, hand_send, hand_recv, proj, proj_t, x_grad0, x_grad1,
    u_ref, xw_ref, dsig_ref, load_sem, *scratch,
):
    rings = [scratch[k * RING : (k + 1) * RING] for k in range(4)]
    step_ring, x_ring = rings[:2], rings[2:]
    step_grad = [step_grad.at[q] for q in range(2)]
    x_grad = [x_grad0, x_grad1]
    section = lax.axis_index("section")
    me = lax.axis_index("ctx")
    partners = others("ctx", CTX) + others("ch", CH) + [{"section": 1 - section}]
    greet(partners)
    loads = [
        pltpu.make_async_copy(src, dst, load_sem.at[k])
        for k, (src, dst) in enumerate(((u_hbm, u_ref), (xw_hbm, xw_ref), (dsig_hbm, dsig_ref)))
    ]
    for load in loads:
        load.start()
    prepare(part_ref, low_part, io_part)
    met(partners)
    gate_copy = remote(dgate_ref, gate_land, hand_send.at[0], hand_recv.at[0], {"section": 1 - section})
    in_copy = remote(in_out, in_land, hand_send.at[1], hand_recv.at[1], {"section": 1 - section})

    sums = sum_start(low_part, io_part, low_land, io_land, sum_send, sum_recv)
    first = plane_start(step_grad, step_ring)

    @pl.when(section == 1)
    def _():
        gate_copy.start()

    small_there = spread_start(small_in, small_land, s_send, s_recv)
    shares = share_start(sums, part_ref, io_part, low_land, io_land, low_all, io_all, all_send, all_recv)
    first = plane_middle(step_grad, step_ring, first)
    for copy in small_there:
        copy.wait_recv()
    total = small_land[0]
    for c in range(1, CTX):
        total = total + small_land[c]
    small_all[me] = total
    small_home = []
    for d, to in enumerate(others("ctx", CTX)):
        small_home.append(remote(small_all.at[me], small_all.at[me], t_send.at[d], t_recv.at[d], to))
        small_home[-1].start()

    share_finish(shares, low_all, io_all, wide)
    proj[...] = wide[...].astype(BF16)
    proj_t[...] = wide[...].T.astype(BF16)

    for load in loads:
        load.wait()

    def product(c, _):
        columns = pl.ds(pl.multiple_of(c * TILE, TILE), TILE)
        grad = jnp.dot(
            proj_t[: R + 2 * N, :], u_ref[:, columns], preferred_element_type=F32
        ).astype(BF16)
        x, y_high = c // 2, lax.rem(c, 2)
        for e in range(2):
            x_grad0[x, y_high, e] = grad[: X_ROWS[0], lanes(e)]
            x_grad1[2 * y_high + e, x // 2, lax.rem(x, 2)] = grad[X_ROWS[0] :, lanes(e)]
        return 0

    lax.fori_loop(0, CTX // 2, product, 0)
    first_x = plane_start(x_grad, x_ring)

    @pl.when(section == 1)
    def _():
        def one(j, _):
            columns = pl.ds(pl.multiple_of(j * TILE, TILE), TILE)
            in_out[:, columns] = (
                dsig_ref[:, columns]
                + lax.dot_general(
                    proj[:, : R + 2 * N], xw_ref[:, columns], (((1,), (0,)), ((), ())),
                    preferred_element_type=F32,
                )
            ).astype(BF16)
            return 0

        lax.fori_loop(0, u_ref.shape[1] // TILE, one, 0)
        in_copy.start()
        hin_ref[...] = jnp.zeros_like(hin_ref)
        hgate_ref[...] = jnp.zeros_like(hgate_ref)

    turned = plane_turn(step_grad, step_ring, first, left_half)
    first_x = plane_middle(x_grad, x_ring, first_x)
    turned = plane_second_middle(step_ring, turned)
    for copy in small_home:
        copy.wait_recv()
    for c in range(CTX):
        gdecay_ref[:, lanes(c)] = small_all[c, :N]
        gbias_ref[:, lanes(c)] = small_all[c, N : N + 1]
        gskip_ref[:, lanes(c)] = small_all[c, N + 1 : N + 2]
    for q, halves in enumerate(plane_finish(step_ring, turned)):
        for h in range(2):
            gstep_ref[q * 16 : (q + 1) * 16, h * 1024 : (h + 1) * 1024] = halves[h]
    turned_x = plane_turn(x_grad, x_ring, first_x, top_half)

    @pl.when(section == 0)
    def _():
        gate_copy.wait_recv()
        in_copy.wait_recv()
        hgate_ref[...] = gate_land[...]
        hin_ref[...] = in_land[...]

    turned_x = plane_second_middle(x_ring, turned_x)
    for q, halves in enumerate(plane_finish(x_ring, turned_x)):
        for h in range(2):
            rows = X_ROWS[q] // 2
            gx_ref[q * X_ROWS[0] + h * rows : q * X_ROWS[0] + (h + 1) * rows, :] = halves[h]

    @pl.when(section == 1)
    def _():
        gate_copy.wait_send()
        in_copy.wait_send()

    for copy in sums + shares + small_there + small_home:
        copy.wait_send()
    for copies in first + turned + first_x + turned_x:
        ring_done(copies)


def run_tail(part, small, dgate, step_grad, u, xw, dsig):
    ch = u.shape[1]
    f = lambda *s: jax.ShapeDtypeStruct(s, F32)
    b = lambda *s: jax.ShapeDtypeStruct(s, BF16)
    return pl.pallas_call(
        tail,
        in_specs=in_vmem(4) + [pl.BlockSpec(memory_space=pl.ANY)] * 3,
        out_specs=in_vmem(7),
        out_shape=[
            b(TOK, ch), b(TOK, ch), f(R + 2 * N, LANE), f(32, ch), f(N, ch), f(1, ch), f(1, ch),
        ],
        scratch_shapes=sum_scratch(BF16)
        + [pltpu.VMEM((CTX, SMALL, LANE), F32)] * 3
        + [pltpu.SemaphoreType.DMA((CTX - 1,))] * 4
        + [pltpu.VMEM((TOK, ch), BF16)] * 3
        + [pltpu.SemaphoreType.DMA((2,))] * 2
        + [pltpu.VMEM((TOK, WIDE), BF16), pltpu.VMEM((WIDE, TOK), BF16)]
        + [pltpu.VMEM((SIDE, 2, 2, rows, LANE), BF16) for rows in X_ROWS]
        + [pltpu.VMEM(u.shape, BF16), pltpu.VMEM(xw.shape, BF16), pltpu.VMEM(dsig.shape, F32)]
        + [pltpu.SemaphoreType.DMA((3,))]
        + ring_scratch((2, 16, 2048), (16, 1024)) * 2
        + ring_scratch((2, X_ROWS[0], LANE), (X_ROWS[0] // 2, LANE))
        + ring_scratch((2, X_ROWS[1], LANE), (X_ROWS[1] // 2, LANE)),
        compiler_params=pltpu.CompilerParams(
            collective_id=2, has_side_effects=True, vmem_limit_bytes=VMEM_BYTES
        ),
        name="tail",
    )(part, small, dgate, step_grad, u, xw, dsig)


def finish(*refs):
    count = len(refs) // 2
    for k in range(count):
        refs[count + k][...] = refs[k][...]


def run_finish(*results):
    return pl.pallas_call(
        finish,
        in_specs=in_vmem(len(results)),
        out_specs=in_vmem(len(results)),
        out_shape=[jax.ShapeDtypeStruct(r.shape, r.dtype) for r in results],
        compiler_params=pltpu.CompilerParams(vmem_limit_bytes=VMEM_BYTES),
        name="finish",
    )(*results)


def body(mixer_input, gate_input, upstream_grad, x_weight, step_weight, step_bias, decay_log, skip_gain):
    u, z, g = mixer_input[0], gate_input[0], upstream_grad[0]
    weight_x, weight_step = jnp.swapaxes(x_weight[0], 0, 1), step_weight[0]
    dlog = decay_log[0]
    low, io = run_sum(u, weight_x)
    *kept, across = run_first(low, io, weight_step, step_bias, dlog, u, z, g)
    d_gate, d_signal, d_part, grad_step, small = run_second(
        low, io, weight_step, dlog, skip_gain, u, z, g, kept, across
    )
    handed_input, handed_gate, grad_x, grad_step, g_decay, g_bias, g_skip = run_finish(
        *run_tail(d_part, small, d_gate, grad_step, u, weight_x, d_signal)
    )
    return (
        handed_input[None], handed_gate[None], jnp.swapaxes(grad_x, 0, 1)[None], grad_step[None],
        g_bias, g_decay[None], g_skip,
    )


def solution(mesh):
    return jax.shard_map(
        body,
        mesh=mesh,
        in_specs=(
            P("section", "ctx", "ch"), P("section", "ctx", "ch"), P("section", "ctx", "ch"),
            P("section", "ch", None), P("section", None, "ch"), P("section", "ch"),
            P("section", None, "ch"), P("section", "ch"),
        ),
        out_specs=(
            P("section", "ctx", "ch"), P("section", "ctx", "ch"), P("section", ("ch", "ctx"), None),
            P("section", "ctx", "ch"), P("section", "ch"), P("section", None, "ch"), P("section", "ch"),
        ),
        check_vma=False,
    )
```

```python
import functools

import jax
import jax.numpy as jnp
from jax import lax
from jax.experimental import pallas as pl
from jax.experimental.pallas import tpu as pltpu
from jax.sharding import PartitionSpec as P

R = 512
N = 16
TOK = 192
STEPS = 24
ROWS = 8
TILE = 256
LANE = 128
HALVES = TILE // LANE
CHUNK = 4
VMEM_BYTES = 60 * 2**20
SIDE = 4
CTX = 16
CH = 8
PIECE = TOK // CH
WIDE = R + LANE
PACK = 40
SMALL = 24
MESH = pl.DeviceIdType.MESH
F32 = jnp.float32
BF16 = jnp.bfloat16


def every(i):
    return pl.ds(i, ROWS, stride=STEPS)


def lanes(k):
    return slice(k * LANE, (k + 1) * LANE)


def by_step(ref, value, by_token):
    for k in range(HALVES):
        by_token[k] = value[:, lanes(k)]
        for i in range(STEPS):
            ref[k, i] = by_token[k, every(i), :]


def from_step(ref, by_token):
    for k in range(HALVES):
        for i in range(STEPS):
            by_token[k, every(i), :] = ref[k, i]
    return jnp.concatenate([by_token[k] for k in range(HALVES)], axis=1)


def row_index():
    return lax.broadcasted_iota(jnp.int32, (ROWS, LANE), 0)


def spread_columns(io_ref, spread):
    def one(i, _):
        rows = io_ref[every(i), :]
        for n in range(2 * N):
            spread[i, n] = jnp.broadcast_to(rows[:, n : n + 1], (ROWS, LANE))
        return 0

    lax.fori_loop(0, STEPS, one, 0)


def inverse(value):
    rough = pl.reciprocal(value, approx=True)
    return rough * (2.0 - value * rough)


def scan_rows(decay, value, reverse):
    row = row_index()
    for k in (1, 2, 4):
        shift = ROWS - k if reverse else k
        inside = row < ROWS - k if reverse else row >= k
        value = value + decay * jnp.where(inside, pltpu.roll(value, shift, 0), 0.0)
        if k < 4:
            decay = decay * jnp.where(inside, pltpu.roll(decay, shift, 0), 1.0)
    return value


def first_pass(
    low_ref, io_ref, w_ref, bias_ref, dlog_ref, all_dlog_ref, u_ref, z_ref, g_ref,
    step_ref, token_ref, sig_ref, drive, seed, entry_ref, exit_ref, bsum_ref, across_ref,
    spread, by_drive, by_seed, by_step_size, rates,
    pack, landed, back, result, send, recv, back_send, back_recv,
):
    tile = pl.program_id(0)
    last = pl.num_programs(0) - 1
    me = lax.axis_index("ctx")
    @pl.when(tile == 0)
    def _():
        greet(others("ctx", CTX))
        spread_columns(io_ref, spread)

    pre = jnp.dot(low_ref[...], w_ref[...], preferred_element_type=F32) + bias_ref[...]
    small = jnp.exp(-jnp.abs(pre))
    above = inverse(1.0 + small)
    series = small * (1.0 - small * (0.5 - small * (1.0 / 3.0)))
    step = jnp.maximum(pre, 0.0) + jnp.where(small < 1e-3, series, jnp.log(1.0 + small))
    sig_ref[...] = jnp.where(pre >= 0.0, above, small * above)
    z = z_ref[...].astype(F32)
    token_ref[...] = step
    by_step(step_ref, step, by_step_size)
    by_step(drive, step * u_ref[...].astype(F32), by_drive)
    by_step(seed, g_ref[...].astype(F32) * z * inverse(1.0 + jnp.exp(-z)), by_seed)
    rates[...] = -jnp.exp(dlog_ref[...])
    row = row_index()

    total = jnp.zeros((ROWS, TILE), F32)
    for i in range(STEPS):
        total = total + jnp.concatenate([step_ref[k, i] for k in range(HALVES)], axis=1)
    bsum_ref[...] = total
    whole_sum = jnp.sum(total, axis=0, keepdims=True)
    for k in range(HALVES):
        pack[HALVES * tile + k, 2 * N :, :] = jnp.broadcast_to(whole_sum[:, lanes(k)], (PACK - 2 * N, LANE))

    for c in range(N // CHUNK):
        pairs = [(n, k) for n in range(c * CHUNK, (c + 1) * CHUNK) for k in range(HALVES)]
        rate = [jnp.broadcast_to(rates[n : n + 1, lanes(k)], (ROWS, LANE)) for n, k in pairs]

        def one(i, carry):
            state, decay, start = carry
            st = [step_ref[k, i] for k in range(HALVES)]
            dr = [drive[k, i] for k in range(HALVES)]
            sd = [seed[k, i] for k in range(HALVES)]
            new_state, new_decay, new_start = [], [], []
            for p, (n, k) in enumerate(pairs):
                a = jnp.exp(st[k] * rate[p])
                new_state.append(a * state[p] + dr[k] * spread[i, n])
                d = a * decay[p]
                new_decay.append(d)
                new_start.append(start[p] + d * (sd[k] * spread[i, N + n]))
            return tuple(new_state), tuple(new_decay), tuple(new_start)

        zero = tuple(jnp.zeros((ROWS, LANE), F32) for _ in pairs)
        ones = tuple(jnp.ones((ROWS, LANE), F32) for _ in pairs)
        state, decay, start = lax.fori_loop(0, STEPS, one, (zero, ones, zero), unroll=12)
        for p, (n, k) in enumerate(pairs):
            ends = scan_rows(decay[p], state[p], False)
            starts = scan_rows(decay[p], start[p], True)
            entry_ref[n, :, lanes(k)] = jnp.where(row >= 1, pltpu.roll(ends, 1, 0), 0.0)
            exit_ref[n, :, lanes(k)] = jnp.where(row < ROWS - 1, pltpu.roll(starts, ROWS - 1, 0), 0.0)
            pack[HALVES * tile + k, n : n + 1, :] = ends[ROWS - 1 :, :]
            pack[HALVES * tile + k, N + n : N + n + 1, :] = starts[:1, :]

    @pl.when(tile == 0)
    def _():
        met(others("ctx", CTX))

    def chunk_to(c):
        return remote(pack.at[c], landed.at[me], send.at[c], recv.at[me], {"ctx": c})

    def chunk_from(c):
        return remote(pack.at[c], landed.at[c], send.at[c], recv.at[c], {"ctx": c})

    def answers():
        return [
            remote(back.at[to["ctx"]], result.at[me], back_send.at[d], back_recv.at[d], to)
            for d, to in enumerate(others("ctx", CTX))
        ]

    for k in range(HALVES):
        c = HALVES * tile + k

        @pl.when(c != me)
        def _():
            chunk_to(c).start()

        @pl.when(c == me)
        def _():
            landed[me] = pack[me]

    @pl.when(tile == jnp.minimum(me // HALVES + 1, last))
    def _():
        for c in range(CTX):
            @pl.when(c != me)
            def _():
                chunk_from(c).wait_recv()

        mine = -jnp.exp(all_dlog_ref[:, pl.ds(pl.multiple_of(me * LANE, LANE), LANE)])
        state = jnp.zeros((N, LANE), F32)
        adjoint = jnp.zeros((N, LANE), F32)
        for c in range(CTX):
            r = CTX - 1 - c
            back[c, :N] = state
            back[r, N:] = adjoint
            state = jnp.exp(landed[c, 2 * N : 2 * N + 1] * mine) * state + landed[c, :N]
            adjoint = jnp.exp(landed[r, 2 * N : 2 * N + 1] * mine) * adjoint + landed[r, N : 2 * N]
        result[me] = back[me]
        for copy in answers():
            copy.start()

    @pl.when(tile == last)
    def _():
        for copy in answers():
            copy.wait_recv()
        across_ref[...] = result[...]
        for copy in answers():
            copy.wait_send()
        for c in range(CTX):
            @pl.when(c != me)
            def _():
                chunk_to(c).wait_send()


def sum_before(value, reverse):
    row = lax.broadcasted_iota(jnp.int32, value.shape, 0)
    held = value
    for k in (1, 2, 4):
        shift = ROWS - k if reverse else k
        inside = row < ROWS - k if reverse else row >= k
        held = held + jnp.where(inside, pltpu.roll(held, shift, 0), 0.0)
    return held - value


def second_pass(
    low_ref, io_ref, w_ref, dlog_ref, skip_ref, u_ref, z_ref, g_ref, step_ref, token_ref, sig_ref, drive, seed,
    entry_ref, exit_ref, bsum_ref, across_ref,
    dgate_ref, dsig_ref, part_ref, gstep_ref, small_ref,
    spread, sums, held, decays, scanned, grad_drive, grad_decay, by_scan, by_grad, by_decay, rates, by_token, low_t,
):
    tile = pl.program_id(0)

    @pl.when(tile == 0)
    def _():
        spread_columns(io_ref, spread)
        sums[...] = jnp.zeros_like(sums)
        part_ref[...] = jnp.zeros_like(part_ref)
        low_t[...] = low_ref[...].astype(F32).T.astype(BF16)

    rates[...] = -jnp.exp(dlog_ref[...])
    prior = sum_before(bsum_ref[...], False)
    later = sum_before(bsum_ref[...], True)

    def so_far(ref, c, i):
        if c == 0:
            return [jnp.zeros((ROWS, LANE), F32) for k in range(HALVES)]
        return [ref[k, i] for k in range(HALVES)]

    for c in range(N // CHUNK):
        numbers = range(c * CHUNK, (c + 1) * CHUNK)
        pairs = [(n, k) for n in numbers for k in range(HALVES)]
        rate = [jnp.broadcast_to(rates[n : n + 1, lanes(k)], (ROWS, LANE)) for n, k in pairs]

        def forward(i, state, c=c, numbers=numbers, rate=rate):
            st = [step_ref[k, i] for k in range(HALVES)]
            dr = [drive[k, i] for k in range(HALVES)]
            sd = [seed[k, i] for k in range(HALVES)]
            out = so_far(scanned, c, i)
            new = []
            for m, n in enumerate(numbers):
                b_in, b_out = spread[i, n], spread[i, N + n]
                d_out = sums[i, N + n]
                for k in range(HALVES):
                    p = m * HALVES + k
                    held[k, i, m] = state[p]
                    decay = jnp.exp(st[k] * rate[p])
                    decays[k, i, m] = decay
                    now = decay * state[p] + dr[k] * b_in
                    new.append(now)
                    out[k] = out[k] + b_out * now
                    d_out = d_out + sd[k] * now
                sums[i, N + n] = d_out
            for k in range(HALVES):
                scanned[k, i] = out[k]
            return tuple(new)

        state = tuple(
            entry_ref[n, :, lanes(k)]
            + jnp.exp(prior[:, lanes(k)] * rate[p]) * across_ref[k, n : n + 1, :]
            for p, (n, k) in enumerate(pairs)
        )
        lax.fori_loop(0, STEPS, forward, state, unroll=8)

        def backward(j, carry, c=c, numbers=numbers, rate=rate):
            incoming, total = carry
            i = STEPS - 1 - j
            st = [step_ref[k, i] for k in range(HALVES)]
            dr = [drive[k, i] for k in range(HALVES)]
            sd = [seed[k, i] for k in range(HALVES)]
            g_drive = so_far(grad_drive, c, i)
            g_decay = so_far(grad_decay, c, i)
            new_in, new_total = [], []
            for m, n in enumerate(numbers):
                b_in, b_out = spread[i, n], spread[i, N + n]
                d_in = sums[i, n]
                for k in range(HALVES):
                    p = m * HALVES + k
                    adjoint = b_out * sd[k] + incoming[p]
                    passed = decays[k, i, m] * adjoint
                    pulled = passed * held[k, i, m]
                    new_in.append(passed)
                    new_total.append(total[p] + pulled * st[k])
                    g_decay[k] = g_decay[k] + pulled * rate[p]
                    g_drive[k] = g_drive[k] + adjoint * b_in
                    d_in = d_in + adjoint * dr[k]
                sums[i, n] = d_in
            for k in range(HALVES):
                grad_drive[k, i] = g_drive[k]
                grad_decay[k, i] = g_decay[k]
            return tuple(new_in), tuple(new_total)

        incoming = tuple(
            exit_ref[n, :, lanes(k)]
            + jnp.exp(later[:, lanes(k)] * rate[p]) * across_ref[k, N + n : N + n + 1, :]
            for p, (n, k) in enumerate(pairs)
        )
        zero = tuple(jnp.zeros((ROWS, LANE), F32) for _ in pairs)
        _, total = lax.fori_loop(0, STEPS, backward, (incoming, zero), unroll=8)
        for p, (n, k) in enumerate(pairs):
            small_ref[k, n : n + 1, :] = (
                jnp.sum(total[p], axis=0, keepdims=True) * rates[n : n + 1, lanes(k)]
            )

    u = u_ref[...].astype(F32)
    z = z_ref[...].astype(F32)
    g = g_ref[...].astype(F32)
    gate_sig = inverse(1.0 + jnp.exp(-z))
    seeds = g * z * gate_sig
    skip = skip_ref[...]
    from_drive = from_step(grad_drive, by_grad)
    mixed = from_step(scanned, by_scan) + skip * u
    dgate_ref[...] = (g * mixed * gate_sig * (1.0 + z * (1.0 - gate_sig))).astype(BF16)
    dsig_ref[...] = from_drive * token_ref[...] + skip * seeds
    d_pre = (from_drive * u + from_step(grad_decay, by_decay)) * sig_ref[...]
    pre = d_pre.astype(BF16)
    bias_row = jnp.sum(d_pre, axis=0, keepdims=True)
    skip_row = jnp.sum(seeds * u, axis=0, keepdims=True)
    for k in range(HALVES):
        small_ref[k, N : N + 1, :] = bias_row[:, lanes(k)]
        small_ref[k, N + 1 : N + 2, :] = skip_row[:, lanes(k)]
        small_ref[k, N + 2 :, :] = jnp.zeros((SMALL - N - 2, LANE), F32)
    part_ref[:, :R] += lax.dot_general(
        pre, w_ref[...], (((1,), (1,)), ((), ())), preferred_element_type=F32
    )
    grad = jnp.dot(low_t[...], pre, preferred_element_type=F32).astype(BF16)
    for x in range(SIDE):
        for y in range(SIDE):
            at = (x * SIDE + y) * 2 * 16
            gstep_ref[0, x, y // 2, y % 2] = grad[at : at + 16]
            gstep_ref[1, y, x // 2, x % 2] = grad[at + 16 : at + 32]

    @pl.when(tile == pl.num_programs(0) - 1)
    def _():
        column = lax.broadcasted_iota(jnp.int32, (ROWS, LANE), 1)

        def one(i, _):
            rows = jnp.zeros((ROWS, LANE), F32)
            for n in range(2 * N):
                rows = jnp.where(column == n, jnp.sum(sums[i, n], axis=1, keepdims=True), rows)
            by_token[every(i), :] = rows
            return 0

        lax.fori_loop(0, STEPS, one, 0)
        part_ref[:, R:] = by_token[...]


def whole(*shape):
    return pl.BlockSpec(shape, lambda j: (0,) * len(shape))


def tiled(*lead):
    return pl.BlockSpec(lead + (TILE,), lambda j: (0,) * len(lead) + (j,))


def stacked(*rows):
    return pl.BlockSpec((HALVES,) + rows + (LANE,), lambda j: (j,) + (0,) * (len(rows) + 1))


def run_first(low, io, weight, bias, dlog, u, z, g):
    ch = u.shape[1]
    f = lambda *s: jax.ShapeDtypeStruct(s, F32)
    return pl.pallas_call(
        first_pass,
        grid=(ch // TILE,),
        in_specs=[
            whole(TOK, R), whole(TOK, io.shape[1]), tiled(R), tiled(1), tiled(N), whole(N, ch),
            tiled(TOK), tiled(TOK), tiled(TOK),
        ],
        out_specs=[
            stacked(STEPS, ROWS), tiled(TOK), tiled(TOK), stacked(STEPS, ROWS), stacked(STEPS, ROWS),
            tiled(N, ROWS), tiled(N, ROWS), tiled(ROWS), whole(CTX, 2 * N, LANE),
        ],
        out_shape=[
            f(ch // LANE, STEPS, ROWS, LANE), f(TOK, ch), f(TOK, ch), f(ch // LANE, STEPS, ROWS, LANE),
            f(ch // LANE, STEPS, ROWS, LANE),
            f(N, ROWS, ch), f(N, ROWS, ch),
            f(ROWS, ch), f(CTX, 2 * N, LANE),
        ],
        scratch_shapes=[
            pltpu.VMEM((STEPS, 2 * N, ROWS, LANE), F32),
            pltpu.VMEM((HALVES, TOK, LANE), F32),
            pltpu.VMEM((HALVES, TOK, LANE), F32),
            pltpu.VMEM((HALVES, TOK, LANE), F32),
            pltpu.VMEM((N, TILE), F32),
            pltpu.VMEM((CTX, PACK, LANE), F32),
            pltpu.VMEM((CTX, PACK, LANE), F32),
            pltpu.VMEM((CTX, 2 * N, LANE), F32),
            pltpu.VMEM((CTX, 2 * N, LANE), F32),
            pltpu.SemaphoreType.DMA((CTX,)),
            pltpu.SemaphoreType.DMA((CTX,)),
            pltpu.SemaphoreType.DMA((CTX - 1,)),
            pltpu.SemaphoreType.DMA((CTX - 1,)),
        ],
        compiler_params=pltpu.CompilerParams(
            collective_id=1, has_side_effects=True, vmem_limit_bytes=VMEM_BYTES
        ),
        name="first_pass",
    )(low, io, weight, bias, dlog, dlog, u, z, g)


def run_second(low, io, weight, dlog, skip, u, z, g, kept, across):
    ch = u.shape[1]
    f = lambda *s: jax.ShapeDtypeStruct(s, F32)
    return pl.pallas_call(
        second_pass,
        grid=(ch // TILE,),
        in_specs=[
            whole(TOK, R), whole(TOK, io.shape[1]), tiled(R), tiled(N), tiled(1),
            tiled(TOK), tiled(TOK), tiled(TOK), stacked(STEPS, ROWS), tiled(TOK), tiled(TOK),
            stacked(STEPS, ROWS), stacked(STEPS, ROWS), tiled(N, ROWS), tiled(N, ROWS), tiled(ROWS), stacked(2 * N),
        ],
        out_specs=[
            tiled(TOK), tiled(TOK), whole(TOK, WIDE), tiled(2, SIDE, 2, 2, 16), stacked(SMALL),
        ],
        out_shape=[
            jax.ShapeDtypeStruct((TOK, ch), BF16), f(TOK, ch), f(TOK, WIDE),
            jax.ShapeDtypeStruct((2, SIDE, 2, 2, 16, ch), BF16), f(ch // LANE, SMALL, LANE),
        ],
        scratch_shapes=[
            pltpu.VMEM((STEPS, 2 * N, ROWS, LANE), F32),
            pltpu.VMEM((STEPS, 2 * N, ROWS, LANE), F32),
            pltpu.VMEM((HALVES, STEPS, CHUNK, ROWS, LANE), F32),
            pltpu.VMEM((HALVES, STEPS, CHUNK, ROWS, LANE), F32),
        ]
        + [pltpu.VMEM((HALVES, STEPS, ROWS, LANE), F32)] * 3
        + [pltpu.VMEM((HALVES, TOK, LANE), F32)] * 3
        + [pltpu.VMEM((N, TILE), F32), pltpu.VMEM((TOK, LANE), F32), pltpu.VMEM((R, TOK), BF16)],
        compiler_params=pltpu.CompilerParams(vmem_limit_bytes=VMEM_BYTES),
        name="second_pass",
    )(low, io, weight, dlog, skip, u, z, g, *kept, across)


def greet(partners):
    for partner in partners:
        pl.semaphore_signal(
            pltpu.get_barrier_semaphore(), inc=1, device_id=partner, device_id_type=MESH
        )


def met(partners):
    pl.semaphore_wait(pltpu.get_barrier_semaphore(), len(partners))


def remote(src, dst, send, recv, to):
    return pltpu.make_async_remote_copy(
        src_ref=src, dst_ref=dst, send_sem=send, recv_sem=recv, device_id=to, device_id_type=MESH
    )


def others(axis, count):
    me = lax.axis_index(axis)
    return [{axis: lax.rem(me + d, count)} for d in range(1, count)]


def token_rows(owner):
    return pl.ds(pl.multiple_of(owner * PIECE, 8), PIECE)


def fold(rows):
    return rows[:ROWS] + pltpu.roll(rows[ROWS : 2 * ROWS], 2 * N, 1) + pltpu.roll(rows[2 * ROWS :], 4 * N, 1)


def unfold(folded):
    used = lax.broadcasted_iota(jnp.int32, (ROWS, LANE), 1) < 2 * N
    parts = [folded, pltpu.roll(folded, LANE - 2 * N, 1), pltpu.roll(folded, LANE - 4 * N, 1)]
    return jnp.concatenate([jnp.where(used, part, 0.0) for part in parts], axis=0)


def over(rows):
    return jnp.concatenate([rows[:, : R // 2], rows[:, R // 2 : R]], axis=0)


def prepare(part_ref, low_part, io_part):
    for p in range(CH):
        rows = part_ref[p * PIECE : (p + 1) * PIECE, :]
        low_part[p] = over(rows).astype(low_part.dtype)
        io_part[p] = fold(rows[:, R:])


def sum_start(low_part, io_part, low_land, io_land, send, recv):
    copies = []
    for d, to in enumerate(others("ch", CH)):
        copies.append(remote(low_part.at[to["ch"]], low_land.at[d], send.at[0, d], recv.at[0, d], to))
        copies.append(remote(io_part.at[to["ch"]], io_land.at[d], send.at[1, d], recv.at[1, d], to))
    for copy in copies:
        copy.start()
    return copies


def share_start(sums, part_ref, io_part, low_land, io_land, low_all, io_all, send, recv):
    me = lax.axis_index("ch")
    for copy in sums:
        copy.wait_recv()
    low = over(part_ref[token_rows(me), :])
    io = io_part[me]
    for d in range(CH - 1):
        low = low + low_land[d].astype(F32)
        io = io + io_land[d]
    low_all[me] = low.astype(BF16)
    io_all[me] = io
    copies = []
    for d, to in enumerate(others("ch", CH)):
        copies.append(remote(low_all.at[me], low_all.at[me], send.at[0, d], recv.at[0, d], to))
        copies.append(remote(io_all.at[me], io_all.at[me], send.at[1, d], recv.at[1, d], to))
    for copy in copies:
        copy.start()
    return copies


def share_finish(copies, low_all, io_all, wide):
    for copy in copies:
        copy.wait_recv()
    for p in range(CH):
        both = low_all[p].astype(F32)
        rows = slice(p * PIECE, (p + 1) * PIECE)
        wide[rows, : R // 2] = both[:PIECE]
        wide[rows, R // 2 : R] = both[PIECE:]
        wide[rows, R:] = unfold(io_all[p])


def sum_scratch(sent):
    return [
        pltpu.VMEM((CH, 2 * PIECE, R // 2), sent),
        pltpu.VMEM((CH, ROWS, LANE), F32),
        pltpu.VMEM((CH - 1, 2 * PIECE, R // 2), sent),
        pltpu.VMEM((CH - 1, ROWS, LANE), F32),
        pltpu.VMEM((CH, 2 * PIECE, R // 2), BF16),
        pltpu.VMEM((CH, ROWS, LANE), F32),
        pltpu.VMEM((TOK, WIDE), F32),
        pltpu.SemaphoreType.DMA((2, CH - 1)),
        pltpu.SemaphoreType.DMA((2, CH - 1)),
        pltpu.SemaphoreType.DMA((2, CH - 1)),
        pltpu.SemaphoreType.DMA((2, CH - 1)),
    ]


LOADS = 4


def sum_projected(u_hbm, xt_hbm, low_ref, io_ref, part_ref, u_ref, xt_ref, load_sem, *scratch):
    low_part, io_part, low_land, io_land, low_all, io_all, wide, sum_send, sum_recv, all_send, all_recv = scratch
    loads = []
    wide_piece = u_ref.shape[1] // LOADS
    for k in range(LOADS):
        columns = slice(k * wide_piece, (k + 1) * wide_piece)
        for m, (src, dst) in enumerate(((u_hbm, u_ref), (xt_hbm, xt_ref))):
            loads.append(
                pltpu.make_async_copy(src.at[:, columns], dst.at[:, columns], load_sem.at[m, k])
            )
            loads[-1].start()
    greet(others("ch", CH))
    total = jnp.zeros((TOK, R + 2 * N), F32)
    for k in range(LOADS):
        columns = slice(k * wide_piece, (k + 1) * wide_piece)
        loads[2 * k].wait()
        loads[2 * k + 1].wait()
        total = total + lax.dot_general(
            u_ref[:, columns], xt_ref[:, columns], (((1,), (1,)), ((), ())), preferred_element_type=F32
        )
    part_ref[:, R:] = jnp.zeros((TOK, LANE), F32)
    part_ref[:, : R + 2 * N] = total
    prepare(part_ref, low_part, io_part)
    met(others("ch", CH))
    sums = sum_start(low_part, io_part, low_land, io_land, sum_send, sum_recv)
    shares = share_start(sums, part_ref, io_part, low_land, io_land, low_all, io_all, all_send, all_recv)
    share_finish(shares, low_all, io_all, wide)
    low_ref[...] = wide[:, :R].astype(BF16)
    io_ref[...] = wide[:, R:]
    for copy in sums + shares:
        copy.wait_send()


def in_vmem(count):
    return [pl.BlockSpec(memory_space=pltpu.VMEM)] * count


def run_sum(u, xt):
    return pl.pallas_call(
        sum_projected,
        in_specs=[pl.BlockSpec(memory_space=pl.ANY)] * 2,
        out_specs=in_vmem(2),
        out_shape=[jax.ShapeDtypeStruct((TOK, R), BF16), jax.ShapeDtypeStruct((TOK, LANE), F32)],
        scratch_shapes=[
            pltpu.VMEM((TOK, WIDE), F32), pltpu.VMEM(u.shape, BF16), pltpu.VMEM(xt.shape, BF16),
            pltpu.SemaphoreType.DMA((2, LOADS)),
        ]
        + sum_scratch(F32),
        compiler_params=pltpu.CompilerParams(
            collective_id=0, has_side_effects=True, vmem_limit_bytes=VMEM_BYTES
        ),
        name="sum_projected",
    )(u, xt)


def spread_start(src, dst, send, recv):
    me = lax.axis_index("ctx")
    copies = []
    for d, to in enumerate(others("ctx", CTX)):
        copies.append(remote(src.at[to["ctx"]], dst.at[me], send.at[d], recv.at[d], to))
        copies[-1].start()
    dst[me] = src[me]
    return copies


def neighbour(axis, d):
    me = lax.axis_index("ctx")
    x, y = me // SIDE, lax.rem(me, SIDE)
    if axis == 0:
        return {"ctx": lax.rem(x + d + SIDE, SIDE) * SIDE + y}
    return {"ctx": x * SIDE + lax.rem(y + d + SIDE, SIDE)}


def place(axis, d=0):
    me = lax.axis_index("ctx")
    at = me // SIDE if axis == 0 else lax.rem(me, SIDE)
    return lax.rem(at + d + SIDE, SIDE)


WAYS = ((0, 1, 0), (1, -1, 1))


def ring_start(axis, src, relay, land, send, recv):
    passing, direct = [], []
    for way, d, half in WAYS:
        to = neighbour(axis, d)
        passing.append(remote(src.at[place(axis, 2), half], relay.at[way], send.at[0, way], recv.at[0, way], to))
        direct.append(
            remote(src.at[place(axis, d), 1 - half], land.at[way, 1 - half], send.at[1, way], recv.at[1, way], to)
        )
        passing[-1].start()
    for copy in direct:
        copy.start()
    return passing, direct


def ring_middle(axis, src, relay, land, send, recv, copies):
    passing, direct = copies
    last = []
    for way, d, half in WAYS:
        passing[way].wait_recv()
        mine = src[place(axis, d), half]
        relay[way] = (relay[way].astype(F32) + mine.astype(F32)).astype(BF16)
        last.append(
            remote(relay.at[way], land.at[way, half], send.at[2, way], recv.at[2, way], neighbour(axis, d))
        )
        last[-1].start()
    return passing, direct, last


def ring_finish(axis, src, land, copies):
    _, direct, last = copies
    for copy in direct + last:
        copy.wait_recv()
    mine = place(axis)
    return [
        src[mine, h].astype(F32) + land[0, h].astype(F32) + land[1, h].astype(F32) for h in range(2)
    ]


def ring_done(copies):
    for group in copies:
        for copy in group:
            copy.wait_send()


RING = 9


def ring_scratch(unit, second):
    return [
        pltpu.VMEM((2,) + unit, BF16),
        pltpu.VMEM((2, 2) + unit, BF16),
        pltpu.VMEM((SIDE, 2) + second, BF16),
        pltpu.VMEM((2,) + second, BF16),
        pltpu.VMEM((2, 2) + second, BF16),
        pltpu.SemaphoreType.DMA((3, 2)),
        pltpu.SemaphoreType.DMA((3, 2)),
        pltpu.SemaphoreType.DMA((3, 2)),
        pltpu.SemaphoreType.DMA((3, 2)),
    ]


def plane_start(src, rings):
    started = []
    for q, (relay, land, _, _, _, send, recv, _, _) in enumerate(rings):
        started.append(ring_start(q, src[q], relay, land, send, recv))
    return started


def plane_middle(src, rings, copies):
    passed = []
    for q, (relay, land, _, _, _, send, recv, _, _) in enumerate(rings):
        passed.append(ring_middle(q, src[q], relay, land, send, recv, copies[q]))
    return passed


def plane_turn(src, rings, copies, split):
    started = []
    for q, (_, land, second, relay, land2, _, _, send, recv) in enumerate(rings):
        halves = ring_finish(q, src[q], land, copies[q])
        for o in range(SIDE):
            for h in range(2):
                second[o, h] = split(halves[o // 2][o % 2], h).astype(BF16)
        started.append(ring_start(1 - q, second, relay, land2, send, recv))
    return started


def plane_second_middle(rings, copies):
    passed = []
    for q, (_, _, second, relay, land2, _, _, send, recv) in enumerate(rings):
        passed.append(ring_middle(1 - q, second, relay, land2, send, recv, copies[q]))
    return passed


def plane_finish(rings, copies):
    return [ring_finish(1 - q, rings[q][2], rings[q][4], copies[q]) for q in range(2)]


def left_half(value, h):
    columns = value.shape[1] // 2
    return value[:, h * columns : (h + 1) * columns]


def top_half(value, h):
    rows = value.shape[0] // 2
    return value[h * rows : (h + 1) * rows]


X_ROWS = (288, 256)


def tail(
    part_ref, small_in, dgate_hbm, grad_hbm, u_hbm, xw_hbm, dsig_hbm,
    hin_ref, hgate_ref, gx_ref, gstep_ref, gdecay_ref, gbias_ref, gskip_ref,
    low_part, io_part, low_land, io_land, low_all, io_all, wide, sum_send, sum_recv, all_send, all_recv,
    small_land, small_back, small_all, s_send, s_recv, t_send, t_recv,
    gate_land, in_out, in_land, hand_send, hand_recv, proj, proj_t, x_grad0, x_grad1,
    u_ref, xw_ref, dsig_ref, step_grad, load_sem, *scratch,
):
    rings = [scratch[k * RING : (k + 1) * RING] for k in range(4)]
    step_ring, x_ring = rings[:2], rings[2:]
    grad_load = pltpu.make_async_copy(grad_hbm, step_grad, load_sem.at[3])
    step_grad = [step_grad.at[q] for q in range(2)]
    x_grad = [x_grad0, x_grad1]
    section = lax.axis_index("section")
    me = lax.axis_index("ctx")
    partners = others("ctx", CTX) + others("ch", CH) + [{"section": 1 - section}]
    grad_load.start()
    greet(partners)
    loads = [
        pltpu.make_async_copy(src, dst, load_sem.at[k])
        for k, (src, dst) in enumerate(((u_hbm, u_ref), (xw_hbm, xw_ref), (dsig_hbm, dsig_ref)))
    ]
    for load in loads:
        load.start()
    prepare(part_ref, low_part, io_part)
    met(partners)
    gate_copy = remote(dgate_hbm, gate_land, hand_send.at[0], hand_recv.at[0], {"section": 1 - section})
    in_copy = remote(in_out, in_land, hand_send.at[1], hand_recv.at[1], {"section": 1 - section})

    sums = sum_start(low_part, io_part, low_land, io_land, sum_send, sum_recv)
    grad_load.wait()
    first = plane_start(step_grad, step_ring)

    @pl.when(section == 1)
    def _():
        gate_copy.start()

    small_there = spread_start(small_in, small_land, s_send, s_recv)
    shares = share_start(sums, part_ref, io_part, low_land, io_land, low_all, io_all, all_send, all_recv)
    first = plane_middle(step_grad, step_ring, first)
    for copy in small_there:
        copy.wait_recv()
    total = small_land[0]
    for c in range(1, CTX):
        total = total + small_land[c]
    small_all[me] = total
    small_home = []
    for d, to in enumerate(others("ctx", CTX)):
        small_home.append(remote(small_all.at[me], small_all.at[me], t_send.at[d], t_recv.at[d], to))
        small_home[-1].start()

    share_finish(shares, low_all, io_all, wide)
    proj[...] = wide[...].astype(BF16)
    proj_t[...] = wide[...].T.astype(BF16)

    for load in loads:
        load.wait()

    def product(c, _):
        columns = pl.ds(pl.multiple_of(c * TILE, TILE), TILE)
        grad = jnp.dot(
            proj_t[: R + 2 * N, :], u_ref[:, columns], preferred_element_type=F32
        ).astype(BF16)
        x, y_high = c // 2, lax.rem(c, 2)
        for e in range(2):
            x_grad0[x, y_high, e] = grad[: X_ROWS[0], lanes(e)]
            x_grad1[2 * y_high + e, x // 2, lax.rem(x, 2)] = grad[X_ROWS[0] :, lanes(e)]
        return 0

    lax.fori_loop(0, CTX // 2, product, 0)
    first_x = plane_start(x_grad, x_ring)

    @pl.when(section == 1)
    def _():
        def one(j, _):
            columns = pl.ds(pl.multiple_of(j * TILE, TILE), TILE)
            in_out[:, columns] = (
                dsig_ref[:, columns]
                + lax.dot_general(
                    proj[:, : R + 2 * N], xw_ref[:, columns], (((1,), (0,)), ((), ())),
                    preferred_element_type=F32,
                )
            ).astype(BF16)
            return 0

        lax.fori_loop(0, u_ref.shape[1] // TILE, one, 0)
        in_copy.start()
        hin_ref[...] = jnp.zeros_like(hin_ref)
        hgate_ref[...] = jnp.zeros_like(hgate_ref)

    turned = plane_turn(step_grad, step_ring, first, left_half)
    first_x = plane_middle(x_grad, x_ring, first_x)
    turned = plane_second_middle(step_ring, turned)
    for copy in small_home:
        copy.wait_recv()
    for c in range(CTX):
        gdecay_ref[:, lanes(c)] = small_all[c, :N]
        gbias_ref[:, lanes(c)] = small_all[c, N : N + 1]
        gskip_ref[:, lanes(c)] = small_all[c, N + 1 : N + 2]
    for q, halves in enumerate(plane_finish(step_ring, turned)):
        for h in range(2):
            gstep_ref[q * 16 : (q + 1) * 16, h * 1024 : (h + 1) * 1024] = halves[h]
    turned_x = plane_turn(x_grad, x_ring, first_x, top_half)

    @pl.when(section == 0)
    def _():
        gate_copy.wait_recv()
        in_copy.wait_recv()
        hgate_ref[...] = gate_land[...]
        hin_ref[...] = in_land[...]

    turned_x = plane_second_middle(x_ring, turned_x)
    for q, halves in enumerate(plane_finish(x_ring, turned_x)):
        for h in range(2):
            rows = X_ROWS[q] // 2
            gx_ref[q * X_ROWS[0] + h * rows : q * X_ROWS[0] + (h + 1) * rows, :] = halves[h]

    @pl.when(section == 1)
    def _():
        gate_copy.wait_send()
        in_copy.wait_send()

    for copy in sums + shares + small_there + small_home:
        copy.wait_send()
    for copies in first + turned + first_x + turned_x:
        ring_done(copies)


def run_tail(part, small, dgate, step_grad, u, xw, dsig):
    ch = u.shape[1]
    f = lambda *s: jax.ShapeDtypeStruct(s, F32)
    b = lambda *s: jax.ShapeDtypeStruct(s, BF16)
    return pl.pallas_call(
        tail,
        in_specs=in_vmem(2) + [pl.BlockSpec(memory_space=pl.ANY)] * 5,
        out_specs=in_vmem(7),
        out_shape=[
            b(TOK, ch), b(TOK, ch), f(R + 2 * N, LANE), f(32, ch), f(N, ch), f(1, ch), f(1, ch),
        ],
        scratch_shapes=sum_scratch(BF16)
        + [pltpu.VMEM((CTX, SMALL, LANE), F32)] * 3
        + [pltpu.SemaphoreType.DMA((CTX - 1,))] * 4
        + [pltpu.VMEM((TOK, ch), BF16)] * 3
        + [pltpu.SemaphoreType.DMA((2,))] * 2
        + [pltpu.VMEM((TOK, WIDE), BF16), pltpu.VMEM((WIDE, TOK), BF16)]
        + [pltpu.VMEM((SIDE, 2, 2, rows, LANE), BF16) for rows in X_ROWS]
        + [pltpu.VMEM(u.shape, BF16), pltpu.VMEM(xw.shape, BF16), pltpu.VMEM(dsig.shape, F32)]
        + [pltpu.VMEM(step_grad.shape, BF16), pltpu.SemaphoreType.DMA((4,))]
        + ring_scratch((2, 16, 2048), (16, 1024)) * 2
        + ring_scratch((2, X_ROWS[0], LANE), (X_ROWS[0] // 2, LANE))
        + ring_scratch((2, X_ROWS[1], LANE), (X_ROWS[1] // 2, LANE)),
        compiler_params=pltpu.CompilerParams(
            collective_id=2, has_side_effects=True, vmem_limit_bytes=VMEM_BYTES
        ),
        name="tail",
    )(part, small, dgate, step_grad, u, xw, dsig)


def finish(*refs):
    count = len(refs) // 2
    for k in range(count):
        refs[count + k][...] = refs[k][...]


def run_finish(*results):
    return pl.pallas_call(
        finish,
        in_specs=in_vmem(len(results)),
        out_specs=in_vmem(len(results)),
        out_shape=[jax.ShapeDtypeStruct(r.shape, r.dtype) for r in results],
        compiler_params=pltpu.CompilerParams(vmem_limit_bytes=VMEM_BYTES),
        name="finish",
    )(*results)


def body(mixer_input, gate_input, upstream_grad, x_weight, step_weight, step_bias, decay_log, skip_gain):
    u, z, g = mixer_input[0], gate_input[0], upstream_grad[0]
    weight_x, weight_step = jnp.swapaxes(x_weight[0], 0, 1), step_weight[0]
    dlog = decay_log[0]
    low, io = run_sum(u, weight_x)
    *kept, across = run_first(low, io, weight_step, step_bias, dlog, u, z, g)
    d_gate, d_signal, d_part, grad_step, small = run_second(
        low, io, weight_step, dlog, skip_gain, u, z, g, kept, across
    )
    handed_input, handed_gate, grad_x, grad_step, g_decay, g_bias, g_skip = run_finish(
        *run_tail(d_part, small, d_gate, grad_step, u, weight_x, d_signal)
    )
    return (
        handed_input[None], handed_gate[None], jnp.swapaxes(grad_x, 0, 1)[None], grad_step[None],
        g_bias, g_decay[None], g_skip,
    )


def solution(mesh):
    return jax.shard_map(
        body,
        mesh=mesh,
        in_specs=(
            P("section", "ctx", "ch"), P("section", "ctx", "ch"), P("section", "ctx", "ch"),
            P("section", "ch", None), P("section", None, "ch"), P("section", "ch"),
            P("section", None, "ch"), P("section", "ch"),
        ),
        out_specs=(
            P("section", "ctx", "ch"), P("section", "ctx", "ch"), P("section", ("ch", "ctx"), None),
            P("section", "ctx", "ch"), P("section", "ch"), P("section", None, "ch"), P("section", "ch"),
        ),
        check_vma=False,
    )
```

```python
import functools

import jax
import jax.numpy as jnp
from jax import lax
from jax.experimental import pallas as pl
from jax.experimental.pallas import tpu as pltpu
from jax.sharding import PartitionSpec as P

R = 512
N = 16
TOK = 192
STEPS = 24
ROWS = 8
TILE = 256
LANE = 128
HALVES = TILE // LANE
CHUNK = 4
VMEM_BYTES = 60 * 2**20
SIDE = 4
CTX = 16
CH = 8
PIECE = TOK // CH
WIDE = R + LANE
PACK = 40
SMALL = 24
MESH = pl.DeviceIdType.MESH
F32 = jnp.float32
BF16 = jnp.bfloat16


def every(i):
    return pl.ds(i, ROWS, stride=STEPS)


def lanes(k):
    return slice(k * LANE, (k + 1) * LANE)


def by_step(ref, value, by_token):
    for k in range(HALVES):
        by_token[k] = value[:, lanes(k)]
        for i in range(STEPS):
            ref[k, i] = by_token[k, every(i), :]


def from_step(ref, by_token):
    for k in range(HALVES):
        for i in range(STEPS):
            by_token[k, every(i), :] = ref[k, i]
    return jnp.concatenate([by_token[k] for k in range(HALVES)], axis=1)


def spread_columns(io_ref, spread):
    def one(i, _):
        rows = io_ref[every(i), :]
        for n in range(2 * N):
            spread[i, n] = jnp.broadcast_to(rows[:, n : n + 1], (ROWS, LANE))
        return 0

    lax.fori_loop(0, STEPS, one, 0)


def inverse(value):
    rough = pl.reciprocal(value, approx=True)
    return rough * (2.0 - value * rough)


def block_rows(s):
    return pl.ds(s, N, stride=ROWS)


def scan_blocks(decays, values, out_ref, k, reverse):
    state = jnp.zeros((N, LANE), F32)
    for s in reversed(range(ROWS)) if reverse else range(ROWS):
        out_ref[k, block_rows(s), :] = state
        state = decays[k, block_rows(s), :] * state + values[k, block_rows(s), :]
    return state


def first_pass(
    low_ref, io_ref, w_ref, bias_ref, dlog_ref, all_dlog_ref, u_ref, z_ref, g_ref,
    step_ref, token_ref, sig_ref, drive, seed, entry_ref, exit_ref, bsum_ref, across_ref,
    spread, by_drive, by_seed, by_step_size, rates,
    pack, landed, back, result, send, recv, back_send, back_recv,
    block_decay, block_end, block_start,
):
    tile = pl.program_id(0)
    last = pl.num_programs(0) - 1
    me = lax.axis_index("ctx")
    @pl.when(tile == 0)
    def _():
        greet(others("ctx", CTX))
        spread_columns(io_ref, spread)

    pre = jnp.dot(low_ref[...], w_ref[...], preferred_element_type=F32) + bias_ref[...]
    small = jnp.exp(-jnp.abs(pre))
    above = inverse(1.0 + small)
    series = small * (1.0 - small * (0.5 - small * (1.0 / 3.0)))
    step = jnp.maximum(pre, 0.0) + jnp.where(small < 1e-3, series, jnp.log(1.0 + small))
    sig_ref[...] = jnp.where(pre >= 0.0, above, small * above)
    z = z_ref[...].astype(F32)
    token_ref[...] = step
    by_step(step_ref, step, by_step_size)
    by_step(drive, step * u_ref[...].astype(F32), by_drive)
    by_step(seed, g_ref[...].astype(F32) * z * inverse(1.0 + jnp.exp(-z)), by_seed)
    rates[...] = -jnp.exp(dlog_ref[...])
    total = jnp.zeros((ROWS, TILE), F32)
    for i in range(STEPS):
        total = total + jnp.concatenate([step_ref[k, i] for k in range(HALVES)], axis=1)
    bsum_ref[...] = total
    whole_sum = jnp.sum(total, axis=0, keepdims=True)
    for k in range(HALVES):
        pack[HALVES * tile + k, 2 * N :, :] = jnp.broadcast_to(whole_sum[:, lanes(k)], (PACK - 2 * N, LANE))

    for c in range(N // CHUNK):
        pairs = [(n, k) for n in range(c * CHUNK, (c + 1) * CHUNK) for k in range(HALVES)]
        rate = [jnp.broadcast_to(rates[n : n + 1, lanes(k)], (ROWS, LANE)) for n, k in pairs]

        def one(i, carry):
            state, decay, start = carry
            st = [step_ref[k, i] for k in range(HALVES)]
            dr = [drive[k, i] for k in range(HALVES)]
            sd = [seed[k, i] for k in range(HALVES)]
            new_state, new_decay, new_start = [], [], []
            for p, (n, k) in enumerate(pairs):
                a = jnp.exp(st[k] * rate[p])
                new_state.append(a * state[p] + dr[k] * spread[i, n])
                d = a * decay[p]
                new_decay.append(d)
                new_start.append(start[p] + d * (sd[k] * spread[i, N + n]))
            return tuple(new_state), tuple(new_decay), tuple(new_start)

        zero = tuple(jnp.zeros((ROWS, LANE), F32) for _ in pairs)
        ones = tuple(jnp.ones((ROWS, LANE), F32) for _ in pairs)
        state, decay, start = lax.fori_loop(0, STEPS, one, (zero, ones, zero), unroll=STEPS)
        for p, (n, k) in enumerate(pairs):
            at = slice(n * ROWS, (n + 1) * ROWS)
            block_decay[k, at, :] = decay[p]
            block_end[k, at, :] = state[p]
            block_start[k, at, :] = start[p]

    for k in range(HALVES):
        pack[HALVES * tile + k, :N, :] = scan_blocks(block_decay, block_end, entry_ref, k, False)
        pack[HALVES * tile + k, N : 2 * N, :] = scan_blocks(block_decay, block_start, exit_ref, k, True)

    @pl.when(tile == 0)
    def _():
        met(others("ctx", CTX))

    def chunk_to(c):
        return remote(pack.at[c], landed.at[me], send.at[c], recv.at[me], {"ctx": c})

    def chunk_from(c):
        return remote(pack.at[c], landed.at[c], send.at[c], recv.at[c], {"ctx": c})

    def answers():
        return [
            remote(back.at[to["ctx"]], result.at[me], back_send.at[d], back_recv.at[d], to)
            for d, to in enumerate(others("ctx", CTX))
        ]

    for k in range(HALVES):
        c = HALVES * tile + k

        @pl.when(c != me)
        def _():
            chunk_to(c).start()

        @pl.when(c == me)
        def _():
            landed[me] = pack[me]

    @pl.when(tile == jnp.minimum(me // HALVES + 1, last))
    def _():
        for c in range(CTX):
            @pl.when(c != me)
            def _():
                chunk_from(c).wait_recv()

        mine = -jnp.exp(all_dlog_ref[:, pl.ds(pl.multiple_of(me * LANE, LANE), LANE)])
        state = jnp.zeros((N, LANE), F32)
        adjoint = jnp.zeros((N, LANE), F32)
        for c in range(CTX):
            r = CTX - 1 - c
            back[c, :N] = state
            back[r, N:] = adjoint
            state = jnp.exp(landed[c, 2 * N : 2 * N + 1] * mine) * state + landed[c, :N]
            adjoint = jnp.exp(landed[r, 2 * N : 2 * N + 1] * mine) * adjoint + landed[r, N : 2 * N]
        result[me] = back[me]
        for copy in answers():
            copy.start()

    @pl.when(tile == last)
    def _():
        for copy in answers():
            copy.wait_recv()
        across_ref[...] = result[...]
        for copy in answers():
            copy.wait_send()
        for c in range(CTX):
            @pl.when(c != me)
            def _():
                chunk_to(c).wait_send()


def sum_before(value, reverse):
    row = lax.broadcasted_iota(jnp.int32, value.shape, 0)
    held = value
    for k in (1, 2, 4):
        shift = ROWS - k if reverse else k
        inside = row < ROWS - k if reverse else row >= k
        held = held + jnp.where(inside, pltpu.roll(held, shift, 0), 0.0)
    return held - value


def second_pass(
    low_ref, io_ref, w_ref, dlog_ref, skip_ref, u_ref, z_ref, g_ref, step_ref, token_ref, sig_ref, drive, seed,
    entry_ref, exit_ref, bsum_ref, across_ref,
    dgate_ref, dsig_ref, part_ref, gstep_ref, small_ref,
    spread, sums, held, decays, scanned, grad_drive, grad_decay, by_scan, by_grad, by_decay, rates, by_token, low_t,
):
    tile = pl.program_id(0)

    @pl.when(tile == 0)
    def _():
        spread_columns(io_ref, spread)
        sums[...] = jnp.zeros_like(sums)
        part_ref[...] = jnp.zeros_like(part_ref)
        low_t[...] = low_ref[...].astype(F32).T.astype(BF16)

    rates[...] = -jnp.exp(dlog_ref[...])
    prior = sum_before(bsum_ref[...], False)
    later = sum_before(bsum_ref[...], True)

    def so_far(ref, c, i):
        if c == 0:
            return [jnp.zeros((ROWS, LANE), F32) for k in range(HALVES)]
        return [ref[k, i] for k in range(HALVES)]

    for c in range(N // CHUNK):
        numbers = range(c * CHUNK, (c + 1) * CHUNK)
        pairs = [(n, k) for n in numbers for k in range(HALVES)]
        rate = [jnp.broadcast_to(rates[n : n + 1, lanes(k)], (ROWS, LANE)) for n, k in pairs]

        def forward(i, state, c=c, numbers=numbers, rate=rate):
            st = [step_ref[k, i] for k in range(HALVES)]
            dr = [drive[k, i] for k in range(HALVES)]
            sd = [seed[k, i] for k in range(HALVES)]
            out = so_far(scanned, c, i)
            new = []
            for m, n in enumerate(numbers):
                b_in, b_out = spread[i, n], spread[i, N + n]
                d_out = sums[i, N + n]
                for k in range(HALVES):
                    p = m * HALVES + k
                    held[k, i, m] = state[p]
                    decay = jnp.exp(st[k] * rate[p])
                    decays[k, i, m] = decay
                    now = decay * state[p] + dr[k] * b_in
                    new.append(now)
                    out[k] = out[k] + b_out * now
                    d_out = d_out + sd[k] * now
                sums[i, N + n] = d_out
            for k in range(HALVES):
                scanned[k, i] = out[k]
            return tuple(new)

        state = tuple(
            entry_ref[k, n * ROWS : (n + 1) * ROWS, :]
            + jnp.exp(prior[:, lanes(k)] * rate[p]) * across_ref[k, n : n + 1, :]
            for p, (n, k) in enumerate(pairs)
        )
        lax.fori_loop(0, STEPS, forward, state, unroll=STEPS)

        def backward(j, carry, c=c, numbers=numbers, rate=rate):
            incoming, total = carry
            i = STEPS - 1 - j
            st = [step_ref[k, i] for k in range(HALVES)]
            dr = [drive[k, i] for k in range(HALVES)]
            sd = [seed[k, i] for k in range(HALVES)]
            g_drive = so_far(grad_drive, c, i)
            g_decay = so_far(grad_decay, c, i)
            new_in, new_total = [], []
            for m, n in enumerate(numbers):
                b_in, b_out = spread[i, n], spread[i, N + n]
                d_in = sums[i, n]
                for k in range(HALVES):
                    p = m * HALVES + k
                    adjoint = b_out * sd[k] + incoming[p]
                    passed = decays[k, i, m] * adjoint
                    pulled = passed * held[k, i, m]
                    new_in.append(passed)
                    new_total.append(total[p] + pulled * st[k])
                    g_decay[k] = g_decay[k] + pulled * rate[p]
                    g_drive[k] = g_drive[k] + adjoint * b_in
                    d_in = d_in + adjoint * dr[k]
                sums[i, n] = d_in
            for k in range(HALVES):
                grad_drive[k, i] = g_drive[k]
                grad_decay[k, i] = g_decay[k]
            return tuple(new_in), tuple(new_total)

        incoming = tuple(
            exit_ref[k, n * ROWS : (n + 1) * ROWS, :]
            + jnp.exp(later[:, lanes(k)] * rate[p]) * across_ref[k, N + n : N + n + 1, :]
            for p, (n, k) in enumerate(pairs)
        )
        zero = tuple(jnp.zeros((ROWS, LANE), F32) for _ in pairs)
        _, total = lax.fori_loop(0, STEPS, backward, (incoming, zero), unroll=STEPS)
        for p, (n, k) in enumerate(pairs):
            small_ref[k, n : n + 1, :] = (
                jnp.sum(total[p], axis=0, keepdims=True) * rates[n : n + 1, lanes(k)]
            )

    u = u_ref[...].astype(F32)
    z = z_ref[...].astype(F32)
    g = g_ref[...].astype(F32)
    gate_sig = inverse(1.0 + jnp.exp(-z))
    seeds = g * z * gate_sig
    skip = skip_ref[...]
    from_drive = from_step(grad_drive, by_grad)
    mixed = from_step(scanned, by_scan) + skip * u
    dgate_ref[...] = (g * mixed * gate_sig * (1.0 + z * (1.0 - gate_sig))).astype(BF16)
    dsig_ref[...] = from_drive * token_ref[...] + skip * seeds
    d_pre = (from_drive * u + from_step(grad_decay, by_decay)) * sig_ref[...]
    pre = d_pre.astype(BF16)
    bias_row = jnp.sum(d_pre, axis=0, keepdims=True)
    skip_row = jnp.sum(seeds * u, axis=0, keepdims=True)
    for k in range(HALVES):
        small_ref[k, N : N + 1, :] = bias_row[:, lanes(k)]
        small_ref[k, N + 1 : N + 2, :] = skip_row[:, lanes(k)]
        small_ref[k, N + 2 :, :] = jnp.zeros((SMALL - N - 2, LANE), F32)
    part_ref[:, :R] += lax.dot_general(
        pre, w_ref[...], (((1,), (1,)), ((), ())), preferred_element_type=F32
    )
    grad = jnp.dot(low_t[...], pre, preferred_element_type=F32).astype(BF16)
    for x in range(SIDE):
        for y in range(SIDE):
            at = (x * SIDE + y) * 2 * 16
            gstep_ref[0, x, y // 2, y % 2] = grad[at : at + 16]
            gstep_ref[1, y, x // 2, x % 2] = grad[at + 16 : at + 32]

    @pl.when(tile == pl.num_programs(0) - 1)
    def _():
        column = lax.broadcasted_iota(jnp.int32, (ROWS, LANE), 1)

        def one(i, _):
            rows = jnp.zeros((ROWS, LANE), F32)
            for n in range(2 * N):
                rows = jnp.where(column == n, jnp.sum(sums[i, n], axis=1, keepdims=True), rows)
            by_token[every(i), :] = rows
            return 0

        lax.fori_loop(0, STEPS, one, 0)
        part_ref[:, R:] = by_token[...]


def whole(*shape):
    return pl.BlockSpec(shape, lambda j: (0,) * len(shape))


def tiled(*lead):
    return pl.BlockSpec(lead + (TILE,), lambda j: (0,) * len(lead) + (j,))


def stacked(*rows):
    return pl.BlockSpec((HALVES,) + rows + (LANE,), lambda j: (j,) + (0,) * (len(rows) + 1))


def run_first(low, io, weight, bias, dlog, u, z, g):
    ch = u.shape[1]
    f = lambda *s: jax.ShapeDtypeStruct(s, F32)
    return pl.pallas_call(
        first_pass,
        grid=(ch // TILE,),
        in_specs=[
            whole(TOK, R), whole(TOK, io.shape[1]), tiled(R), tiled(1), tiled(N), whole(N, ch),
            tiled(TOK), tiled(TOK), tiled(TOK),
        ],
        out_specs=[
            stacked(STEPS, ROWS), tiled(TOK), tiled(TOK), stacked(STEPS, ROWS), stacked(STEPS, ROWS),
            stacked(N * ROWS), stacked(N * ROWS), tiled(ROWS), whole(CTX, 2 * N, LANE),
        ],
        out_shape=[
            f(ch // LANE, STEPS, ROWS, LANE), f(TOK, ch), f(TOK, ch), f(ch // LANE, STEPS, ROWS, LANE),
            f(ch // LANE, STEPS, ROWS, LANE),
            f(ch // LANE, N * ROWS, LANE), f(ch // LANE, N * ROWS, LANE),
            f(ROWS, ch), f(CTX, 2 * N, LANE),
        ],
        scratch_shapes=[
            pltpu.VMEM((STEPS, 2 * N, ROWS, LANE), F32),
            pltpu.VMEM((HALVES, TOK, LANE), F32),
            pltpu.VMEM((HALVES, TOK, LANE), F32),
            pltpu.VMEM((HALVES, TOK, LANE), F32),
            pltpu.VMEM((N, TILE), F32),
            pltpu.VMEM((CTX, PACK, LANE), F32),
            pltpu.VMEM((CTX, PACK, LANE), F32),
            pltpu.VMEM((CTX, 2 * N, LANE), F32),
            pltpu.VMEM((CTX, 2 * N, LANE), F32),
            pltpu.SemaphoreType.DMA((CTX,)),
            pltpu.SemaphoreType.DMA((CTX,)),
            pltpu.SemaphoreType.DMA((CTX - 1,)),
            pltpu.SemaphoreType.DMA((CTX - 1,)),
        ]
        + [pltpu.VMEM((HALVES, N * ROWS, LANE), F32)] * 3,
        compiler_params=pltpu.CompilerParams(
            collective_id=1, has_side_effects=True, vmem_limit_bytes=VMEM_BYTES
        ),
        name="first_pass",
    )(low, io, weight, bias, dlog, dlog, u, z, g)


def run_second(low, io, weight, dlog, skip, u, z, g, kept, across):
    ch = u.shape[1]
    f = lambda *s: jax.ShapeDtypeStruct(s, F32)
    return pl.pallas_call(
        second_pass,
        grid=(ch // TILE,),
        in_specs=[
            whole(TOK, R), whole(TOK, io.shape[1]), tiled(R), tiled(N), tiled(1),
            tiled(TOK), tiled(TOK), tiled(TOK), stacked(STEPS, ROWS), tiled(TOK), tiled(TOK),
            stacked(STEPS, ROWS), stacked(STEPS, ROWS), stacked(N * ROWS), stacked(N * ROWS), tiled(ROWS), stacked(2 * N),
        ],
        out_specs=[
            tiled(TOK), tiled(TOK), whole(TOK, WIDE), tiled(2, SIDE, 2, 2, 16), stacked(SMALL),
        ],
        out_shape=[
            jax.ShapeDtypeStruct((TOK, ch), BF16), f(TOK, ch), f(TOK, WIDE),
            jax.ShapeDtypeStruct((2, SIDE, 2, 2, 16, ch), BF16), f(ch // LANE, SMALL, LANE),
        ],
        scratch_shapes=[
            pltpu.VMEM((STEPS, 2 * N, ROWS, LANE), F32),
            pltpu.VMEM((STEPS, 2 * N, ROWS, LANE), F32),
            pltpu.VMEM((HALVES, STEPS, CHUNK, ROWS, LANE), F32),
            pltpu.VMEM((HALVES, STEPS, CHUNK, ROWS, LANE), F32),
        ]
        + [pltpu.VMEM((HALVES, STEPS, ROWS, LANE), F32)] * 3
        + [pltpu.VMEM((HALVES, TOK, LANE), F32)] * 3
        + [pltpu.VMEM((N, TILE), F32), pltpu.VMEM((TOK, LANE), F32), pltpu.VMEM((R, TOK), BF16)],
        compiler_params=pltpu.CompilerParams(vmem_limit_bytes=VMEM_BYTES),
        name="second_pass",
    )(low, io, weight, dlog, skip, u, z, g, *kept, across)


def greet(partners):
    for partner in partners:
        pl.semaphore_signal(
            pltpu.get_barrier_semaphore(), inc=1, device_id=partner, device_id_type=MESH
        )


def met(partners):
    pl.semaphore_wait(pltpu.get_barrier_semaphore(), len(partners))


def remote(src, dst, send, recv, to):
    return pltpu.make_async_remote_copy(
        src_ref=src, dst_ref=dst, send_sem=send, recv_sem=recv, device_id=to, device_id_type=MESH
    )


def others(axis, count):
    me = lax.axis_index(axis)
    return [{axis: lax.rem(me + d, count)} for d in range(1, count)]


def token_rows(owner):
    return pl.ds(pl.multiple_of(owner * PIECE, 8), PIECE)


def fold(rows):
    return rows[:ROWS] + pltpu.roll(rows[ROWS : 2 * ROWS], 2 * N, 1) + pltpu.roll(rows[2 * ROWS :], 4 * N, 1)


def unfold(folded):
    used = lax.broadcasted_iota(jnp.int32, (ROWS, LANE), 1) < 2 * N
    parts = [folded, pltpu.roll(folded, LANE - 2 * N, 1), pltpu.roll(folded, LANE - 4 * N, 1)]
    return jnp.concatenate([jnp.where(used, part, 0.0) for part in parts], axis=0)


def over(rows):
    return jnp.concatenate([rows[:, : R // 2], rows[:, R // 2 : R]], axis=0)


def prepare(part_ref, low_part, io_part):
    for p in range(CH):
        rows = part_ref[p * PIECE : (p + 1) * PIECE, :]
        low_part[p] = over(rows).astype(low_part.dtype)
        io_part[p] = fold(rows[:, R:])


def sum_start(low_part, io_part, low_land, io_land, send, recv):
    copies = []
    for d, to in enumerate(others("ch", CH)):
        copies.append(remote(low_part.at[to["ch"]], low_land.at[d], send.at[0, d], recv.at[0, d], to))
        copies.append(remote(io_part.at[to["ch"]], io_land.at[d], send.at[1, d], recv.at[1, d], to))
    for copy in copies:
        copy.start()
    return copies


def share_start(sums, part_ref, io_part, low_land, io_land, low_all, io_all, send, recv):
    me = lax.axis_index("ch")
    for copy in sums:
        copy.wait_recv()
    low = over(part_ref[token_rows(me), :])
    io = io_part[me]
    for d in range(CH - 1):
        low = low + low_land[d].astype(F32)
        io = io + io_land[d]
    low_all[me] = low.astype(BF16)
    io_all[me] = io
    copies = []
    for d, to in enumerate(others("ch", CH)):
        copies.append(remote(low_all.at[me], low_all.at[me], send.at[0, d], recv.at[0, d], to))
        copies.append(remote(io_all.at[me], io_all.at[me], send.at[1, d], recv.at[1, d], to))
    for copy in copies:
        copy.start()
    return copies


def share_finish(copies, low_all, io_all, wide):
    for copy in copies:
        copy.wait_recv()
    for p in range(CH):
        both = low_all[p].astype(F32)
        rows = slice(p * PIECE, (p + 1) * PIECE)
        wide[rows, : R // 2] = both[:PIECE]
        wide[rows, R // 2 : R] = both[PIECE:]
        wide[rows, R:] = unfold(io_all[p])


def sum_scratch(sent):
    return [
        pltpu.VMEM((CH, 2 * PIECE, R // 2), sent),
        pltpu.VMEM((CH, ROWS, LANE), F32),
        pltpu.VMEM((CH - 1, 2 * PIECE, R // 2), sent),
        pltpu.VMEM((CH - 1, ROWS, LANE), F32),
        pltpu.VMEM((CH, 2 * PIECE, R // 2), BF16),
        pltpu.VMEM((CH, ROWS, LANE), F32),
        pltpu.VMEM((TOK, WIDE), F32),
        pltpu.SemaphoreType.DMA((2, CH - 1)),
        pltpu.SemaphoreType.DMA((2, CH - 1)),
        pltpu.SemaphoreType.DMA((2, CH - 1)),
        pltpu.SemaphoreType.DMA((2, CH - 1)),
    ]


LOADS = 4


def sum_projected(u_hbm, xt_hbm, low_ref, io_ref, part_ref, u_ref, xt_ref, load_sem, *scratch):
    low_part, io_part, low_land, io_land, low_all, io_all, wide, sum_send, sum_recv, all_send, all_recv = scratch
    loads = []
    wide_piece = u_ref.shape[1] // LOADS
    for k in range(LOADS):
        columns = slice(k * wide_piece, (k + 1) * wide_piece)
        for m, (src, dst) in enumerate(((u_hbm, u_ref), (xt_hbm, xt_ref))):
            loads.append(
                pltpu.make_async_copy(src.at[:, columns], dst.at[:, columns], load_sem.at[m, k])
            )
            loads[-1].start()
    greet(others("ch", CH))
    total = jnp.zeros((TOK, R + 2 * N), F32)
    for k in range(LOADS):
        columns = slice(k * wide_piece, (k + 1) * wide_piece)
        loads[2 * k].wait()
        loads[2 * k + 1].wait()
        total = total + lax.dot_general(
            u_ref[:, columns], xt_ref[:, columns], (((1,), (1,)), ((), ())), preferred_element_type=F32
        )
    part_ref[:, R:] = jnp.zeros((TOK, LANE), F32)
    part_ref[:, : R + 2 * N] = total
    prepare(part_ref, low_part, io_part)
    met(others("ch", CH))
    sums = sum_start(low_part, io_part, low_land, io_land, sum_send, sum_recv)
    shares = share_start(sums, part_ref, io_part, low_land, io_land, low_all, io_all, all_send, all_recv)
    share_finish(shares, low_all, io_all, wide)
    low_ref[...] = wide[:, :R].astype(BF16)
    io_ref[...] = wide[:, R:]
    for copy in sums + shares:
        copy.wait_send()


def in_vmem(count):
    return [pl.BlockSpec(memory_space=pltpu.VMEM)] * count


def run_sum(u, xt):
    return pl.pallas_call(
        sum_projected,
        in_specs=[pl.BlockSpec(memory_space=pl.ANY)] * 2,
        out_specs=in_vmem(2),
        out_shape=[jax.ShapeDtypeStruct((TOK, R), BF16), jax.ShapeDtypeStruct((TOK, LANE), F32)],
        scratch_shapes=[
            pltpu.VMEM((TOK, WIDE), F32), pltpu.VMEM(u.shape, BF16), pltpu.VMEM(xt.shape, BF16),
            pltpu.SemaphoreType.DMA((2, LOADS)),
        ]
        + sum_scratch(F32),
        compiler_params=pltpu.CompilerParams(
            collective_id=0, has_side_effects=True, vmem_limit_bytes=VMEM_BYTES
        ),
        name="sum_projected",
    )(u, xt)


def spread_start(src, dst, send, recv):
    me = lax.axis_index("ctx")
    copies = []
    for d, to in enumerate(others("ctx", CTX)):
        copies.append(remote(src.at[to["ctx"]], dst.at[me], send.at[d], recv.at[d], to))
        copies[-1].start()
    dst[me] = src[me]
    return copies


def neighbour(axis, d):
    me = lax.axis_index("ctx")
    x, y = me // SIDE, lax.rem(me, SIDE)
    if axis == 0:
        return {"ctx": lax.rem(x + d + SIDE, SIDE) * SIDE + y}
    return {"ctx": x * SIDE + lax.rem(y + d + SIDE, SIDE)}


def place(axis, d=0):
    me = lax.axis_index("ctx")
    at = me // SIDE if axis == 0 else lax.rem(me, SIDE)
    return lax.rem(at + d + SIDE, SIDE)


WAYS = ((0, 1, 0), (1, -1, 1))


def ring_start(axis, src, relay, land, send, recv):
    passing, direct = [], []
    for way, d, half in WAYS:
        to = neighbour(axis, d)
        passing.append(remote(src.at[place(axis, 2), half], relay.at[way], send.at[0, way], recv.at[0, way], to))
        direct.append(
            remote(src.at[place(axis, d), 1 - half], land.at[way, 1 - half], send.at[1, way], recv.at[1, way], to)
        )
        passing[-1].start()
    for copy in direct:
        copy.start()
    return passing, direct


def ring_middle(axis, src, relay, land, send, recv, copies):
    passing, direct = copies
    last = []
    for way, d, half in WAYS:
        passing[way].wait_recv()
        mine = src[place(axis, d), half]
        relay[way] = (relay[way].astype(F32) + mine.astype(F32)).astype(BF16)
        last.append(
            remote(relay.at[way], land.at[way, half], send.at[2, way], recv.at[2, way], neighbour(axis, d))
        )
        last[-1].start()
    return passing, direct, last


def ring_finish(axis, src, land, copies):
    _, direct, last = copies
    for copy in direct + last:
        copy.wait_recv()
    mine = place(axis)
    return [
        src[mine, h].astype(F32) + land[0, h].astype(F32) + land[1, h].astype(F32) for h in range(2)
    ]


def ring_done(copies):
    for group in copies:
        for copy in group:
            copy.wait_send()


RING = 9


def ring_scratch(unit, second):
    return [
        pltpu.VMEM((2,) + unit, BF16),
        pltpu.VMEM((2, 2) + unit, BF16),
        pltpu.VMEM((SIDE, 2) + second, BF16),
        pltpu.VMEM((2,) + second, BF16),
        pltpu.VMEM((2, 2) + second, BF16),
        pltpu.SemaphoreType.DMA((3, 2)),
        pltpu.SemaphoreType.DMA((3, 2)),
        pltpu.SemaphoreType.DMA((3, 2)),
        pltpu.SemaphoreType.DMA((3, 2)),
    ]


def plane_start(src, rings):
    started = []
    for q, (relay, land, _, _, _, send, recv, _, _) in enumerate(rings):
        started.append(ring_start(q, src[q], relay, land, send, recv))
    return started


def plane_middle(src, rings, copies):
    passed = []
    for q, (relay, land, _, _, _, send, recv, _, _) in enumerate(rings):
        passed.append(ring_middle(q, src[q], relay, land, send, recv, copies[q]))
    return passed


def plane_turn(src, rings, copies, split):
    started = []
    for q, (_, land, second, relay, land2, _, _, send, recv) in enumerate(rings):
        halves = ring_finish(q, src[q], land, copies[q])
        for o in range(SIDE):
            for h in range(2):
                second[o, h] = split(halves[o // 2][o % 2], h).astype(BF16)
        started.append(ring_start(1 - q, second, relay, land2, send, recv))
    return started


def plane_second_middle(rings, copies):
    passed = []
    for q, (_, _, second, relay, land2, _, _, send, recv) in enumerate(rings):
        passed.append(ring_middle(1 - q, second, relay, land2, send, recv, copies[q]))
    return passed


def plane_finish(rings, copies):
    return [ring_finish(1 - q, rings[q][2], rings[q][4], copies[q]) for q in range(2)]


def left_half(value, h):
    columns = value.shape[1] // 2
    return value[:, h * columns : (h + 1) * columns]


def top_half(value, h):
    rows = value.shape[0] // 2
    return value[h * rows : (h + 1) * rows]


X_ROWS = (288, 256)


def tail(
    part_ref, small_in, dgate_hbm, grad_hbm, u_hbm, xw_hbm, dsig_hbm,
    hin_ref, hgate_ref, gx_ref, gstep_ref, gdecay_ref, gbias_ref, gskip_ref,
    low_part, io_part, low_land, io_land, low_all, io_all, wide, sum_send, sum_recv, all_send, all_recv,
    small_land, small_back, small_all, s_send, s_recv, t_send, t_recv,
    gate_land, in_out, in_land, hand_send, hand_recv, proj, proj_t, x_grad0, x_grad1,
    u_ref, xw_ref, dsig_ref, step_grad, load_sem, *scratch,
):
    rings = [scratch[k * RING : (k + 1) * RING] for k in range(4)]
    step_ring, x_ring = rings[:2], rings[2:]
    grad_load = pltpu.make_async_copy(grad_hbm, step_grad, load_sem.at[3])
    step_grad = [step_grad.at[q] for q in range(2)]
    x_grad = [x_grad0, x_grad1]
    section = lax.axis_index("section")
    me = lax.axis_index("ctx")
    partners = others("ctx", CTX) + others("ch", CH) + [{"section": 1 - section}]
    grad_load.start()
    greet(partners)
    loads = [
        pltpu.make_async_copy(src, dst, load_sem.at[k])
        for k, (src, dst) in enumerate(((u_hbm, u_ref), (xw_hbm, xw_ref), (dsig_hbm, dsig_ref)))
    ]
    for load in loads:
        load.start()
    prepare(part_ref, low_part, io_part)
    met(partners)
    gate_copy = remote(dgate_hbm, gate_land, hand_send.at[0], hand_recv.at[0], {"section": 1 - section})
    in_copy = remote(in_out, in_land, hand_send.at[1], hand_recv.at[1], {"section": 1 - section})

    sums = sum_start(low_part, io_part, low_land, io_land, sum_send, sum_recv)
    grad_load.wait()
    first = plane_start(step_grad, step_ring)

    @pl.when(section == 1)
    def _():
        gate_copy.start()

    shares = share_start(sums, part_ref, io_part, low_land, io_land, low_all, io_all, all_send, all_recv)
    small_there = spread_start(small_in, small_land, s_send, s_recv)
    first = plane_middle(step_grad, step_ring, first)
    share_finish(shares, low_all, io_all, wide)
    proj[...] = wide[...].astype(BF16)
    proj_t[...] = wide[...].T.astype(BF16)

    for load in loads:
        load.wait()

    def product(c, _):
        columns = pl.ds(pl.multiple_of(c * TILE, TILE), TILE)
        grad = jnp.dot(
            proj_t[: R + 2 * N, :], u_ref[:, columns], preferred_element_type=F32
        ).astype(BF16)
        x, y_high = c // 2, lax.rem(c, 2)
        for e in range(2):
            x_grad0[x, y_high, e] = grad[: X_ROWS[0], lanes(e)]
            x_grad1[2 * y_high + e, x // 2, lax.rem(x, 2)] = grad[X_ROWS[0] :, lanes(e)]
        return 0

    lax.fori_loop(0, CTX // 2, product, 0)
    first_x = plane_start(x_grad, x_ring)

    @pl.when(section == 1)
    def _():
        def one(j, _):
            columns = pl.ds(pl.multiple_of(j * TILE, TILE), TILE)
            in_out[:, columns] = (
                dsig_ref[:, columns]
                + lax.dot_general(
                    proj[:, : R + 2 * N], xw_ref[:, columns], (((1,), (0,)), ((), ())),
                    preferred_element_type=F32,
                )
            ).astype(BF16)
            return 0

        lax.fori_loop(0, u_ref.shape[1] // TILE, one, 0)
        in_copy.start()
        hin_ref[...] = jnp.zeros_like(hin_ref)
        hgate_ref[...] = jnp.zeros_like(hgate_ref)

    first_x = plane_middle(x_grad, x_ring, first_x)
    turned = plane_turn(step_grad, step_ring, first, left_half)
    for copy in small_there:
        copy.wait_recv()
    total = small_land[0]
    for c in range(1, CTX):
        total = total + small_land[c]
    small_all[me] = total
    small_home = []
    for d, to in enumerate(others("ctx", CTX)):
        small_home.append(remote(small_all.at[me], small_all.at[me], t_send.at[d], t_recv.at[d], to))
        small_home[-1].start()
    turned_x = plane_turn(x_grad, x_ring, first_x, top_half)
    turned = plane_second_middle(step_ring, turned)
    turned_x = plane_second_middle(x_ring, turned_x)
    for copy in small_home:
        copy.wait_recv()
    for c in range(CTX):
        gdecay_ref[:, lanes(c)] = small_all[c, :N]
        gbias_ref[:, lanes(c)] = small_all[c, N : N + 1]
        gskip_ref[:, lanes(c)] = small_all[c, N + 1 : N + 2]
    for q, halves in enumerate(plane_finish(step_ring, turned)):
        for h in range(2):
            gstep_ref[q * 16 : (q + 1) * 16, h * 1024 : (h + 1) * 1024] = halves[h]

    @pl.when(section == 0)
    def _():
        gate_copy.wait_recv()
        in_copy.wait_recv()
        hgate_ref[...] = gate_land[...]
        hin_ref[...] = in_land[...]

    for q, halves in enumerate(plane_finish(x_ring, turned_x)):
        for h in range(2):
            rows = X_ROWS[q] // 2
            gx_ref[q * X_ROWS[0] + h * rows : q * X_ROWS[0] + (h + 1) * rows, :] = halves[h]

    @pl.when(section == 1)
    def _():
        gate_copy.wait_send()
        in_copy.wait_send()

    for copy in sums + shares + small_there + small_home:
        copy.wait_send()
    for copies in first + turned + first_x + turned_x:
        ring_done(copies)


def run_tail(part, small, dgate, step_grad, u, xw, dsig):
    ch = u.shape[1]
    f = lambda *s: jax.ShapeDtypeStruct(s, F32)
    b = lambda *s: jax.ShapeDtypeStruct(s, BF16)
    return pl.pallas_call(
        tail,
        in_specs=in_vmem(2) + [pl.BlockSpec(memory_space=pl.ANY)] * 5,
        out_specs=in_vmem(7),
        out_shape=[
            b(TOK, ch), b(TOK, ch), f(R + 2 * N, LANE), f(32, ch), f(N, ch), f(1, ch), f(1, ch),
        ],
        scratch_shapes=sum_scratch(BF16)
        + [pltpu.VMEM((CTX, SMALL, LANE), F32)] * 3
        + [pltpu.SemaphoreType.DMA((CTX - 1,))] * 4
        + [pltpu.VMEM((TOK, ch), BF16)] * 3
        + [pltpu.SemaphoreType.DMA((2,))] * 2
        + [pltpu.VMEM((TOK, WIDE), BF16), pltpu.VMEM((WIDE, TOK), BF16)]
        + [pltpu.VMEM((SIDE, 2, 2, rows, LANE), BF16) for rows in X_ROWS]
        + [pltpu.VMEM(u.shape, BF16), pltpu.VMEM(xw.shape, BF16), pltpu.VMEM(dsig.shape, F32)]
        + [pltpu.VMEM(step_grad.shape, BF16), pltpu.SemaphoreType.DMA((4,))]
        + ring_scratch((2, 16, 2048), (16, 1024)) * 2
        + ring_scratch((2, X_ROWS[0], LANE), (X_ROWS[0] // 2, LANE))
        + ring_scratch((2, X_ROWS[1], LANE), (X_ROWS[1] // 2, LANE)),
        compiler_params=pltpu.CompilerParams(
            collective_id=2, has_side_effects=True, vmem_limit_bytes=VMEM_BYTES
        ),
        name="tail",
    )(part, small, dgate, step_grad, u, xw, dsig)


def finish(*refs):
    count = len(refs) // 2
    for k in range(count):
        refs[count + k][...] = refs[k][...]


def run_finish(*results):
    return pl.pallas_call(
        finish,
        in_specs=in_vmem(len(results)),
        out_specs=in_vmem(len(results)),
        out_shape=[jax.ShapeDtypeStruct(r.shape, r.dtype) for r in results],
        compiler_params=pltpu.CompilerParams(vmem_limit_bytes=VMEM_BYTES),
        name="finish",
    )(*results)


def body(mixer_input, gate_input, upstream_grad, x_weight, step_weight, step_bias, decay_log, skip_gain):
    u, z, g = mixer_input[0], gate_input[0], upstream_grad[0]
    weight_x, weight_step = jnp.swapaxes(x_weight[0], 0, 1), step_weight[0]
    dlog = decay_log[0]
    low, io = run_sum(u, weight_x)
    *kept, across = run_first(low, io, weight_step, step_bias, dlog, u, z, g)
    d_gate, d_signal, d_part, grad_step, small = run_second(
        low, io, weight_step, dlog, skip_gain, u, z, g, kept, across
    )
    handed_input, handed_gate, grad_x, grad_step, g_decay, g_bias, g_skip = run_finish(
        *run_tail(d_part, small, d_gate, grad_step, u, weight_x, d_signal)
    )
    return (
        handed_input[None], handed_gate[None], jnp.swapaxes(grad_x, 0, 1)[None], grad_step[None],
        g_bias, g_decay[None], g_skip,
    )


def solution(mesh):
    return jax.shard_map(
        body,
        mesh=mesh,
        in_specs=(
            P("section", "ctx", "ch"), P("section", "ctx", "ch"), P("section", "ctx", "ch"),
            P("section", "ch", None), P("section", None, "ch"), P("section", "ch"),
            P("section", None, "ch"), P("section", "ch"),
        ),
        out_specs=(
            P("section", "ctx", "ch"), P("section", "ctx", "ch"), P("section", ("ch", "ctx"), None),
            P("section", "ctx", "ch"), P("section", "ch"), P("section", None, "ch"), P("section", "ch"),
        ),
        check_vma=False,
    )
```

```python
import functools

import jax
import jax.numpy as jnp
from jax import lax
from jax.experimental import pallas as pl
from jax.experimental.pallas import tpu as pltpu
from jax.sharding import PartitionSpec as P

R = 512
N = 16
TOK = 192
STEPS = 24
ROWS = 8
TILE = 256
LANE = 128
HALVES = TILE // LANE
CHUNK = 4
VMEM_BYTES = 60 * 2**20
SIDE = 4
CTX = 16
CH = 8
PIECE = TOK // CH
WIDE = R + LANE
PACK = 40
SMALL = 24
MESH = pl.DeviceIdType.MESH
F32 = jnp.float32
BF16 = jnp.bfloat16


def every(i):
    return pl.ds(i, ROWS, stride=STEPS)


def lanes(k):
    return slice(k * LANE, (k + 1) * LANE)


def by_step(ref, value, by_token):
    for k in range(HALVES):
        by_token[k] = value[:, lanes(k)]
        for i in range(STEPS):
            ref[k, i] = by_token[k, every(i), :]


def from_step(ref, by_token):
    for k in range(HALVES):
        for i in range(STEPS):
            by_token[k, every(i), :] = ref[k, i]
    return jnp.concatenate([by_token[k] for k in range(HALVES)], axis=1)


def spread_columns(io_ref, spread):
    def one(i, _):
        rows = io_ref[every(i), :]
        for n in range(2 * N):
            spread[i, n] = jnp.broadcast_to(rows[:, n : n + 1], (ROWS, LANE))
        return 0

    lax.fori_loop(0, STEPS, one, 0)


def inverse(value):
    rough = pl.reciprocal(value, approx=True)
    return rough * (2.0 - value * rough)


def block_rows(s):
    return pl.ds(s, N, stride=ROWS)


def scan_blocks(decays, values, out_ref, k, reverse):
    state = jnp.zeros((N, LANE), F32)
    for s in reversed(range(ROWS)) if reverse else range(ROWS):
        out_ref[k, block_rows(s), :] = state
        state = decays[k, block_rows(s), :] * state + values[k, block_rows(s), :]
    return state


def owner_of(tile, k):
    x, y = tile // SIDE, tile % SIDE
    return (x + 2 * k) * SIDE + (y + 2 * k) % SIDE


def chunk_of(me):
    x, y = me // SIDE, lax.rem(me, SIDE)
    k = x // 2
    return 2 * ((x - 2 * k) * SIDE + lax.rem(y + 2 * k, SIDE)) + k


def first_pass(
    low_ref, io_ref, w_ref, bias_ref, dlog_ref, all_dlog_ref, u_ref, z_ref, g_ref,
    step_ref, token_ref, sig_ref, drive, seed, entry_ref, exit_ref, bsum_ref, across_ref,
    spread, by_drive, by_seed, by_step_size, rates,
    pack, landed, back, result, send, recv, back_send, back_recv,
    block_decay, block_end, block_start,
):
    tile = pl.program_id(0)
    last = pl.num_programs(0) - 1
    me = lax.axis_index("ctx")
    @pl.when(tile == 0)
    def _():
        greet(others("ctx", CTX))
        spread_columns(io_ref, spread)

    pre = jnp.dot(low_ref[...], w_ref[...], preferred_element_type=F32) + bias_ref[...]
    small = jnp.exp(-jnp.abs(pre))
    above = inverse(1.0 + small)
    series = small * (1.0 - small * (0.5 - small * (1.0 / 3.0)))
    step = jnp.maximum(pre, 0.0) + jnp.where(small < 1e-3, series, jnp.log(1.0 + small))
    sig_ref[...] = jnp.where(pre >= 0.0, above, small * above)
    z = z_ref[...].astype(F32)
    token_ref[...] = step
    by_step(step_ref, step, by_step_size)
    by_step(drive, step * u_ref[...].astype(F32), by_drive)
    by_step(seed, g_ref[...].astype(F32) * z * inverse(1.0 + jnp.exp(-z)), by_seed)
    rates[...] = -jnp.exp(dlog_ref[...])
    total = jnp.zeros((ROWS, TILE), F32)
    for i in range(STEPS):
        total = total + jnp.concatenate([step_ref[k, i] for k in range(HALVES)], axis=1)
    bsum_ref[...] = total
    whole_sum = jnp.sum(total, axis=0, keepdims=True)
    for k in range(HALVES):
        pack[HALVES * tile + k, 2 * N :, :] = jnp.broadcast_to(whole_sum[:, lanes(k)], (PACK - 2 * N, LANE))

    for c in range(N // CHUNK):
        pairs = [(n, k) for n in range(c * CHUNK, (c + 1) * CHUNK) for k in range(HALVES)]
        rate = [jnp.broadcast_to(rates[n : n + 1, lanes(k)], (ROWS, LANE)) for n, k in pairs]

        def one(i, carry):
            state, decay, start = carry
            st = [step_ref[k, i] for k in range(HALVES)]
            dr = [drive[k, i] for k in range(HALVES)]
            sd = [seed[k, i] for k in range(HALVES)]
            new_state, new_decay, new_start = [], [], []
            for p, (n, k) in enumerate(pairs):
                a = jnp.exp(st[k] * rate[p])
                new_state.append(a * state[p] + dr[k] * spread[i, n])
                d = a * decay[p]
                new_decay.append(d)
                new_start.append(start[p] + d * (sd[k] * spread[i, N + n]))
            return tuple(new_state), tuple(new_decay), tuple(new_start)

        zero = tuple(jnp.zeros((ROWS, LANE), F32) for _ in pairs)
        ones = tuple(jnp.ones((ROWS, LANE), F32) for _ in pairs)
        state, decay, start = lax.fori_loop(0, STEPS, one, (zero, ones, zero), unroll=STEPS)
        for p, (n, k) in enumerate(pairs):
            at = slice(n * ROWS, (n + 1) * ROWS)
            block_decay[k, at, :] = decay[p]
            block_end[k, at, :] = state[p]
            block_start[k, at, :] = start[p]

    for k in range(HALVES):
        pack[HALVES * tile + k, :N, :] = scan_blocks(block_decay, block_end, entry_ref, k, False)
        pack[HALVES * tile + k, N : 2 * N, :] = scan_blocks(block_decay, block_start, exit_ref, k, True)

    @pl.when(tile == 0)
    def _():
        met(others("ctx", CTX))

    own = chunk_of(me)

    def chunk_to(c, owner):
        return remote(pack.at[c], landed.at[me], send.at[c], recv.at[me], {"ctx": owner})

    def chunk_from(c):
        return remote(pack.at[c], landed.at[c], send.at[c], recv.at[c], {"ctx": c})

    def answers():
        return [
            remote(back.at[to["ctx"]], result.at[own], back_send.at[d], back_recv.at[d], to)
            for d, to in enumerate(others("ctx", CTX))
        ]

    for k in range(HALVES):
        c = HALVES * tile + k
        owner = owner_of(tile, k)

        @pl.when(owner != me)
        def _():
            chunk_to(c, owner).start()

        @pl.when(owner == me)
        def _():
            landed[me] = pack[c]

    @pl.when(tile == jnp.minimum(own // HALVES + 1, last))
    def _():
        for c in range(CTX):
            @pl.when(c != me)
            def _():
                chunk_from(c).wait_recv()

        mine = -jnp.exp(all_dlog_ref[:, pl.ds(pl.multiple_of(own * LANE, LANE), LANE)])
        state = jnp.zeros((N, LANE), F32)
        adjoint = jnp.zeros((N, LANE), F32)
        for c in range(CTX):
            r = CTX - 1 - c
            back[c, :N] = state
            back[r, N:] = adjoint
            state = jnp.exp(landed[c, 2 * N : 2 * N + 1] * mine) * state + landed[c, :N]
            adjoint = jnp.exp(landed[r, 2 * N : 2 * N + 1] * mine) * adjoint + landed[r, N : 2 * N]
        result[own] = back[me]
        for copy in answers():
            copy.start()

    @pl.when(tile == last)
    def _():
        for copy in answers():
            copy.wait_recv()
        across_ref[...] = result[...]
        for copy in answers():
            copy.wait_send()
        for c in range(CTX):
            owner = owner_of(c // HALVES, c % HALVES)

            @pl.when(owner != me)
            def _():
                chunk_to(c, owner).wait_send()


def sum_before(value, reverse):
    row = lax.broadcasted_iota(jnp.int32, value.shape, 0)
    held = value
    for k in (1, 2, 4):
        shift = ROWS - k if reverse else k
        inside = row < ROWS - k if reverse else row >= k
        held = held + jnp.where(inside, pltpu.roll(held, shift, 0), 0.0)
    return held - value


def second_pass(
    low_ref, io_ref, w_ref, dlog_ref, skip_ref, u_ref, z_ref, g_ref, step_ref, token_ref, sig_ref, drive, seed,
    entry_ref, exit_ref, bsum_ref, across_ref,
    dgate_ref, dsig_ref, part_ref, gstep_ref, small_ref,
    spread, sums, held, decays, scanned, grad_drive, grad_decay, by_scan, by_grad, by_decay, rates, by_token, low_t,
):
    tile = pl.program_id(0)

    @pl.when(tile == 0)
    def _():
        spread_columns(io_ref, spread)
        sums[...] = jnp.zeros_like(sums)
        part_ref[...] = jnp.zeros_like(part_ref)
        low_t[...] = low_ref[...].astype(F32).T.astype(BF16)

    rates[...] = -jnp.exp(dlog_ref[...])
    prior = sum_before(bsum_ref[...], False)
    later = sum_before(bsum_ref[...], True)

    def so_far(ref, c, i):
        if c == 0:
            return [jnp.zeros((ROWS, LANE), F32) for k in range(HALVES)]
        return [ref[k, i] for k in range(HALVES)]

    for c in range(N // CHUNK):
        numbers = range(c * CHUNK, (c + 1) * CHUNK)
        pairs = [(n, k) for n in numbers for k in range(HALVES)]
        rate = [jnp.broadcast_to(rates[n : n + 1, lanes(k)], (ROWS, LANE)) for n, k in pairs]

        def forward(i, state, c=c, numbers=numbers, rate=rate):
            st = [step_ref[k, i] for k in range(HALVES)]
            dr = [drive[k, i] for k in range(HALVES)]
            sd = [seed[k, i] for k in range(HALVES)]
            out = so_far(scanned, c, i)
            new = []
            for m, n in enumerate(numbers):
                b_in, b_out = spread[i, n], spread[i, N + n]
                d_out = sums[i, N + n]
                for k in range(HALVES):
                    p = m * HALVES + k
                    held[k, i, m] = state[p]
                    decay = jnp.exp(st[k] * rate[p])
                    decays[k, i, m] = decay
                    now = decay * state[p] + dr[k] * b_in
                    new.append(now)
                    out[k] = out[k] + b_out * now
                    d_out = d_out + sd[k] * now
                sums[i, N + n] = d_out
            for k in range(HALVES):
                scanned[k, i] = out[k]
            return tuple(new)

        state = tuple(
            entry_ref[k, n * ROWS : (n + 1) * ROWS, :]
            + jnp.exp(prior[:, lanes(k)] * rate[p]) * across_ref[k, n : n + 1, :]
            for p, (n, k) in enumerate(pairs)
        )
        lax.fori_loop(0, STEPS, forward, state, unroll=STEPS)

        def backward(j, carry, c=c, numbers=numbers, rate=rate):
            incoming, total = carry
            i = STEPS - 1 - j
            st = [step_ref[k, i] for k in range(HALVES)]
            dr = [drive[k, i] for k in range(HALVES)]
            sd = [seed[k, i] for k in range(HALVES)]
            g_drive = so_far(grad_drive, c, i)
            g_decay = so_far(grad_decay, c, i)
            new_in, new_total = [], []
            for m, n in enumerate(numbers):
                b_in, b_out = spread[i, n], spread[i, N + n]
                d_in = sums[i, n]
                for k in range(HALVES):
                    p = m * HALVES + k
                    adjoint = b_out * sd[k] + incoming[p]
                    passed = decays[k, i, m] * adjoint
                    pulled = passed * held[k, i, m]
                    new_in.append(passed)
                    new_total.append(total[p] + pulled * st[k])
                    g_decay[k] = g_decay[k] + pulled * rate[p]
                    g_drive[k] = g_drive[k] + adjoint * b_in
                    d_in = d_in + adjoint * dr[k]
                sums[i, n] = d_in
            for k in range(HALVES):
                grad_drive[k, i] = g_drive[k]
                grad_decay[k, i] = g_decay[k]
            return tuple(new_in), tuple(new_total)

        incoming = tuple(
            exit_ref[k, n * ROWS : (n + 1) * ROWS, :]
            + jnp.exp(later[:, lanes(k)] * rate[p]) * across_ref[k, N + n : N + n + 1, :]
            for p, (n, k) in enumerate(pairs)
        )
        zero = tuple(jnp.zeros((ROWS, LANE), F32) for _ in pairs)
        _, total = lax.fori_loop(0, STEPS, backward, (incoming, zero), unroll=STEPS)
        for p, (n, k) in enumerate(pairs):
            small_ref[k, n : n + 1, :] = (
                jnp.sum(total[p], axis=0, keepdims=True) * rates[n : n + 1, lanes(k)]
            )

    u = u_ref[...].astype(F32)
    z = z_ref[...].astype(F32)
    g = g_ref[...].astype(F32)
    gate_sig = inverse(1.0 + jnp.exp(-z))
    seeds = g * z * gate_sig
    skip = skip_ref[...]
    from_drive = from_step(grad_drive, by_grad)
    mixed = from_step(scanned, by_scan) + skip * u
    dgate_ref[...] = (g * mixed * gate_sig * (1.0 + z * (1.0 - gate_sig))).astype(BF16)
    dsig_ref[...] = from_drive * token_ref[...] + skip * seeds
    d_pre = (from_drive * u + from_step(grad_decay, by_decay)) * sig_ref[...]
    pre = d_pre.astype(BF16)
    bias_row = jnp.sum(d_pre, axis=0, keepdims=True)
    skip_row = jnp.sum(seeds * u, axis=0, keepdims=True)
    for k in range(HALVES):
        small_ref[k, N : N + 1, :] = bias_row[:, lanes(k)]
        small_ref[k, N + 1 : N + 2, :] = skip_row[:, lanes(k)]
        small_ref[k, N + 2 :, :] = jnp.zeros((SMALL - N - 2, LANE), F32)
    part_ref[:, :R] += lax.dot_general(
        pre, w_ref[...], (((1,), (1,)), ((), ())), preferred_element_type=F32
    )
    grad = jnp.dot(low_t[...], pre, preferred_element_type=F32).astype(BF16)
    for x in range(SIDE):
        for y in range(SIDE):
            at = (x * SIDE + y) * 2 * 16
            gstep_ref[0, x, y // 2, y % 2] = grad[at : at + 16]
            gstep_ref[1, y, x // 2, x % 2] = grad[at + 16 : at + 32]

    @pl.when(tile == pl.num_programs(0) - 1)
    def _():
        column = lax.broadcasted_iota(jnp.int32, (ROWS, LANE), 1)

        def one(i, _):
            rows = jnp.zeros((ROWS, LANE), F32)
            for n in range(2 * N):
                rows = jnp.where(column == n, jnp.sum(sums[i, n], axis=1, keepdims=True), rows)
            by_token[every(i), :] = rows
            return 0

        lax.fori_loop(0, STEPS, one, 0)
        part_ref[:, R:] = by_token[...]


def whole(*shape):
    return pl.BlockSpec(shape, lambda j: (0,) * len(shape))


def tiled(*lead):
    return pl.BlockSpec(lead + (TILE,), lambda j: (0,) * len(lead) + (j,))


def stacked(*rows):
    return pl.BlockSpec((HALVES,) + rows + (LANE,), lambda j: (j,) + (0,) * (len(rows) + 1))


def run_first(low, io, weight, bias, dlog, u, z, g):
    ch = u.shape[1]
    f = lambda *s: jax.ShapeDtypeStruct(s, F32)
    return pl.pallas_call(
        first_pass,
        grid=(ch // TILE,),
        in_specs=[
            whole(TOK, R), whole(TOK, io.shape[1]), tiled(R), tiled(1), tiled(N), whole(N, ch),
            tiled(TOK), tiled(TOK), tiled(TOK),
        ],
        out_specs=[
            stacked(STEPS, ROWS), tiled(TOK), tiled(TOK), stacked(STEPS, ROWS), stacked(STEPS, ROWS),
            stacked(N * ROWS), stacked(N * ROWS), tiled(ROWS), whole(CTX, 2 * N, LANE),
        ],
        out_shape=[
            f(ch // LANE, STEPS, ROWS, LANE), f(TOK, ch), f(TOK, ch), f(ch // LANE, STEPS, ROWS, LANE),
            f(ch // LANE, STEPS, ROWS, LANE),
            f(ch // LANE, N * ROWS, LANE), f(ch // LANE, N * ROWS, LANE),
            f(ROWS, ch), f(CTX, 2 * N, LANE),
        ],
        scratch_shapes=[
            pltpu.VMEM((STEPS, 2 * N, ROWS, LANE), F32),
            pltpu.VMEM((HALVES, TOK, LANE), F32),
            pltpu.VMEM((HALVES, TOK, LANE), F32),
            pltpu.VMEM((HALVES, TOK, LANE), F32),
            pltpu.VMEM((N, TILE), F32),
            pltpu.VMEM((CTX, PACK, LANE), F32),
            pltpu.VMEM((CTX, PACK, LANE), F32),
            pltpu.VMEM((CTX, 2 * N, LANE), F32),
            pltpu.VMEM((CTX, 2 * N, LANE), F32),
            pltpu.SemaphoreType.DMA((CTX,)),
            pltpu.SemaphoreType.DMA((CTX,)),
            pltpu.SemaphoreType.DMA((CTX - 1,)),
            pltpu.SemaphoreType.DMA((CTX - 1,)),
        ]
        + [pltpu.VMEM((HALVES, N * ROWS, LANE), F32)] * 3,
        compiler_params=pltpu.CompilerParams(
            collective_id=1, has_side_effects=True, vmem_limit_bytes=VMEM_BYTES
        ),
        name="first_pass",
    )(low, io, weight, bias, dlog, dlog, u, z, g)


def run_second(low, io, weight, dlog, skip, u, z, g, kept, across):
    ch = u.shape[1]
    f = lambda *s: jax.ShapeDtypeStruct(s, F32)
    return pl.pallas_call(
        second_pass,
        grid=(ch // TILE,),
        in_specs=[
            whole(TOK, R), whole(TOK, io.shape[1]), tiled(R), tiled(N), tiled(1),
            tiled(TOK), tiled(TOK), tiled(TOK), stacked(STEPS, ROWS), tiled(TOK), tiled(TOK),
            stacked(STEPS, ROWS), stacked(STEPS, ROWS), stacked(N * ROWS), stacked(N * ROWS), tiled(ROWS), stacked(2 * N),
        ],
        out_specs=[
            tiled(TOK), tiled(TOK), whole(TOK, WIDE), tiled(2, SIDE, 2, 2, 16), stacked(SMALL),
        ],
        out_shape=[
            jax.ShapeDtypeStruct((TOK, ch), BF16), f(TOK, ch), f(TOK, WIDE),
            jax.ShapeDtypeStruct((2, SIDE, 2, 2, 16, ch), BF16), f(ch // LANE, SMALL, LANE),
        ],
        scratch_shapes=[
            pltpu.VMEM((STEPS, 2 * N, ROWS, LANE), F32),
            pltpu.VMEM((STEPS, 2 * N, ROWS, LANE), F32),
            pltpu.VMEM((HALVES, STEPS, CHUNK, ROWS, LANE), F32),
            pltpu.VMEM((HALVES, STEPS, CHUNK, ROWS, LANE), F32),
        ]
        + [pltpu.VMEM((HALVES, STEPS, ROWS, LANE), F32)] * 3
        + [pltpu.VMEM((HALVES, TOK, LANE), F32)] * 3
        + [pltpu.VMEM((N, TILE), F32), pltpu.VMEM((TOK, LANE), F32), pltpu.VMEM((R, TOK), BF16)],
        compiler_params=pltpu.CompilerParams(vmem_limit_bytes=VMEM_BYTES),
        name="second_pass",
    )(low, io, weight, dlog, skip, u, z, g, *kept, across)


def greet(partners):
    for partner in partners:
        pl.semaphore_signal(
            pltpu.get_barrier_semaphore(), inc=1, device_id=partner, device_id_type=MESH
        )


def met(partners):
    pl.semaphore_wait(pltpu.get_barrier_semaphore(), len(partners))


def remote(src, dst, send, recv, to):
    return pltpu.make_async_remote_copy(
        src_ref=src, dst_ref=dst, send_sem=send, recv_sem=recv, device_id=to, device_id_type=MESH
    )


def others(axis, count):
    me = lax.axis_index(axis)
    return [{axis: lax.rem(me + d, count)} for d in range(1, count)]


def token_rows(owner):
    return pl.ds(pl.multiple_of(owner * PIECE, 8), PIECE)


def fold(rows):
    return rows[:ROWS] + pltpu.roll(rows[ROWS : 2 * ROWS], 2 * N, 1) + pltpu.roll(rows[2 * ROWS :], 4 * N, 1)


def unfold(folded):
    used = lax.broadcasted_iota(jnp.int32, (ROWS, LANE), 1) < 2 * N
    parts = [folded, pltpu.roll(folded, LANE - 2 * N, 1), pltpu.roll(folded, LANE - 4 * N, 1)]
    return jnp.concatenate([jnp.where(used, part, 0.0) for part in parts], axis=0)


def over(rows):
    return jnp.concatenate([rows[:, : R // 2], rows[:, R // 2 : R]], axis=0)


def prepare(part_ref, low_part, io_part):
    for p in range(CH):
        rows = part_ref[p * PIECE : (p + 1) * PIECE, :]
        low_part[p] = over(rows).astype(low_part.dtype)
        io_part[p] = fold(rows[:, R:])


def sum_start(low_part, io_part, low_land, io_land, send, recv):
    copies = []
    for d, to in enumerate(others("ch", CH)):
        copies.append(remote(low_part.at[to["ch"]], low_land.at[d], send.at[0, d], recv.at[0, d], to))
        copies.append(remote(io_part.at[to["ch"]], io_land.at[d], send.at[1, d], recv.at[1, d], to))
    for copy in copies:
        copy.start()
    return copies


def share_start(sums, part_ref, io_part, low_land, io_land, low_all, io_all, send, recv):
    me = lax.axis_index("ch")
    for copy in sums:
        copy.wait_recv()
    low = over(part_ref[token_rows(me), :])
    io = io_part[me]
    for d in range(CH - 1):
        low = low + low_land[d].astype(F32)
        io = io + io_land[d]
    low_all[me] = low.astype(BF16)
    io_all[me] = io
    copies = []
    for d, to in enumerate(others("ch", CH)):
        copies.append(remote(low_all.at[me], low_all.at[me], send.at[0, d], recv.at[0, d], to))
        copies.append(remote(io_all.at[me], io_all.at[me], send.at[1, d], recv.at[1, d], to))
    for copy in copies:
        copy.start()
    return copies


def share_finish(copies, low_all, io_all, wide):
    for copy in copies:
        copy.wait_recv()
    for p in range(CH):
        both = low_all[p].astype(F32)
        rows = slice(p * PIECE, (p + 1) * PIECE)
        wide[rows, : R // 2] = both[:PIECE]
        wide[rows, R // 2 : R] = both[PIECE:]
        wide[rows, R:] = unfold(io_all[p])


def sum_scratch(sent):
    return [
        pltpu.VMEM((CH, 2 * PIECE, R // 2), sent),
        pltpu.VMEM((CH, ROWS, LANE), F32),
        pltpu.VMEM((CH - 1, 2 * PIECE, R // 2), sent),
        pltpu.VMEM((CH - 1, ROWS, LANE), F32),
        pltpu.VMEM((CH, 2 * PIECE, R // 2), BF16),
        pltpu.VMEM((CH, ROWS, LANE), F32),
        pltpu.VMEM((TOK, WIDE), F32),
        pltpu.SemaphoreType.DMA((2, CH - 1)),
        pltpu.SemaphoreType.DMA((2, CH - 1)),
        pltpu.SemaphoreType.DMA((2, CH - 1)),
        pltpu.SemaphoreType.DMA((2, CH - 1)),
    ]


LOADS = 4


def sum_projected(u_hbm, xt_hbm, low_ref, io_ref, part_ref, u_ref, xt_ref, load_sem, *scratch):
    low_part, io_part, low_land, io_land, low_all, io_all, wide, sum_send, sum_recv, all_send, all_recv = scratch
    loads = []
    wide_piece = u_ref.shape[1] // LOADS
    for k in range(LOADS):
        columns = slice(k * wide_piece, (k + 1) * wide_piece)
        for m, (src, dst) in enumerate(((u_hbm, u_ref), (xt_hbm, xt_ref))):
            loads.append(
                pltpu.make_async_copy(src.at[:, columns], dst.at[:, columns], load_sem.at[m, k])
            )
            loads[-1].start()
    greet(others("ch", CH))
    total = jnp.zeros((TOK, R + 2 * N), F32)
    for k in range(LOADS):
        columns = slice(k * wide_piece, (k + 1) * wide_piece)
        loads[2 * k].wait()
        loads[2 * k + 1].wait()
        total = total + lax.dot_general(
            u_ref[:, columns], xt_ref[:, columns], (((1,), (1,)), ((), ())), preferred_element_type=F32
        )
    part_ref[:, R:] = jnp.zeros((TOK, LANE), F32)
    part_ref[:, : R + 2 * N] = total
    prepare(part_ref, low_part, io_part)
    met(others("ch", CH))
    sums = sum_start(low_part, io_part, low_land, io_land, sum_send, sum_recv)
    shares = share_start(sums, part_ref, io_part, low_land, io_land, low_all, io_all, all_send, all_recv)
    share_finish(shares, low_all, io_all, wide)
    low_ref[...] = wide[:, :R].astype(BF16)
    io_ref[...] = wide[:, R:]
    for copy in sums + shares:
        copy.wait_send()


def in_vmem(count):
    return [pl.BlockSpec(memory_space=pltpu.VMEM)] * count


def run_sum(u, xt):
    return pl.pallas_call(
        sum_projected,
        in_specs=[pl.BlockSpec(memory_space=pl.ANY)] * 2,
        out_specs=in_vmem(2),
        out_shape=[jax.ShapeDtypeStruct((TOK, R), BF16), jax.ShapeDtypeStruct((TOK, LANE), F32)],
        scratch_shapes=[
            pltpu.VMEM((TOK, WIDE), F32), pltpu.VMEM(u.shape, BF16), pltpu.VMEM(xt.shape, BF16),
            pltpu.SemaphoreType.DMA((2, LOADS)),
        ]
        + sum_scratch(F32),
        compiler_params=pltpu.CompilerParams(
            collective_id=0, has_side_effects=True, vmem_limit_bytes=VMEM_BYTES
        ),
        name="sum_projected",
    )(u, xt)


def spread_start(src, dst, send, recv):
    me = lax.axis_index("ctx")
    copies = []
    for d, to in enumerate(others("ctx", CTX)):
        copies.append(remote(src.at[to["ctx"]], dst.at[me], send.at[d], recv.at[d], to))
        copies[-1].start()
    dst[me] = src[me]
    return copies


def neighbour(axis, d):
    me = lax.axis_index("ctx")
    x, y = me // SIDE, lax.rem(me, SIDE)
    if axis == 0:
        return {"ctx": lax.rem(x + d + SIDE, SIDE) * SIDE + y}
    return {"ctx": x * SIDE + lax.rem(y + d + SIDE, SIDE)}


def place(axis, d=0):
    me = lax.axis_index("ctx")
    at = me // SIDE if axis == 0 else lax.rem(me, SIDE)
    return lax.rem(at + d + SIDE, SIDE)


WAYS = ((0, 1, 0), (1, -1, 1))


def ring_start(axis, src, relay, land, send, recv):
    passing, direct = [], []
    for way, d, half in WAYS:
        to = neighbour(axis, d)
        passing.append(remote(src.at[place(axis, 2), half], relay.at[way], send.at[0, way], recv.at[0, way], to))
        direct.append(
            remote(src.at[place(axis, d), 1 - half], land.at[way, 1 - half], send.at[1, way], recv.at[1, way], to)
        )
        passing[-1].start()
    for copy in direct:
        copy.start()
    return passing, direct


def ring_middle(axis, src, relay, land, send, recv, copies):
    passing, direct = copies
    last = []
    for way, d, half in WAYS:
        passing[way].wait_recv()
        mine = src[place(axis, d), half]
        relay[way] = (relay[way].astype(F32) + mine.astype(F32)).astype(BF16)
        last.append(
            remote(relay.at[way], land.at[way, half], send.at[2, way], recv.at[2, way], neighbour(axis, d))
        )
        last[-1].start()
    return passing, direct, last


def ring_finish(axis, src, land, copies):
    _, direct, last = copies
    for copy in direct + last:
        copy.wait_recv()
    mine = place(axis)
    return [
        src[mine, h].astype(F32) + land[0, h].astype(F32) + land[1, h].astype(F32) for h in range(2)
    ]


def ring_done(copies):
    for group in copies:
        for copy in group:
            copy.wait_send()


RING = 9


def ring_scratch(unit, second):
    return [
        pltpu.VMEM((2,) + unit, BF16),
        pltpu.VMEM((2, 2) + unit, BF16),
        pltpu.VMEM((SIDE, 2) + second, BF16),
        pltpu.VMEM((2,) + second, BF16),
        pltpu.VMEM((2, 2) + second, BF16),
        pltpu.SemaphoreType.DMA((3, 2)),
        pltpu.SemaphoreType.DMA((3, 2)),
        pltpu.SemaphoreType.DMA((3, 2)),
        pltpu.SemaphoreType.DMA((3, 2)),
    ]


def plane_start(src, rings):
    started = []
    for q, (relay, land, _, _, _, send, recv, _, _) in enumerate(rings):
        started.append(ring_start(q, src[q], relay, land, send, recv))
    return started


def plane_middle(src, rings, copies):
    passed = []
    for q, (relay, land, _, _, _, send, recv, _, _) in enumerate(rings):
        passed.append(ring_middle(q, src[q], relay, land, send, recv, copies[q]))
    return passed


def plane_turn(src, rings, copies, split):
    started = []
    for q, (_, land, second, relay, land2, _, _, send, recv) in enumerate(rings):
        halves = ring_finish(q, src[q], land, copies[q])
        for o in range(SIDE):
            for h in range(2):
                second[o, h] = split(halves[o // 2][o % 2], h).astype(BF16)
        started.append(ring_start(1 - q, second, relay, land2, send, recv))
    return started


def plane_second_middle(rings, copies):
    passed = []
    for q, (_, _, second, relay, land2, _, _, send, recv) in enumerate(rings):
        passed.append(ring_middle(1 - q, second, relay, land2, send, recv, copies[q]))
    return passed


def plane_finish(rings, copies):
    return [ring_finish(1 - q, rings[q][2], rings[q][4], copies[q]) for q in range(2)]


def left_half(value, h):
    columns = value.shape[1] // 2
    return value[:, h * columns : (h + 1) * columns]


def top_half(value, h):
    rows = value.shape[0] // 2
    return value[h * rows : (h + 1) * rows]


X_ROWS = (288, 256)


def tail(
    part_ref, small_in, dgate_hbm, grad_hbm, u_hbm, xw_hbm, dsig_hbm,
    hin_ref, hgate_ref, gx_ref, gstep_ref, gdecay_ref, gbias_ref, gskip_ref,
    low_part, io_part, low_land, io_land, low_all, io_all, wide, sum_send, sum_recv, all_send, all_recv,
    small_land, small_back, small_all, s_send, s_recv, t_send, t_recv,
    gate_land, in_out, in_land, hand_send, hand_recv, proj, proj_t, x_grad0, x_grad1,
    u_ref, xw_ref, dsig_ref, step_grad, load_sem, *scratch,
):
    rings = [scratch[k * RING : (k + 1) * RING] for k in range(4)]
    step_ring, x_ring = rings[:2], rings[2:]
    grad_load = pltpu.make_async_copy(grad_hbm, step_grad, load_sem.at[3])
    step_grad = [step_grad.at[q] for q in range(2)]
    x_grad = [x_grad0, x_grad1]
    section = lax.axis_index("section")
    me = lax.axis_index("ctx")
    partners = others("ctx", CTX) + others("ch", CH) + [{"section": 1 - section}]
    grad_load.start()
    greet(partners)
    loads = [
        pltpu.make_async_copy(src, dst, load_sem.at[k])
        for k, (src, dst) in enumerate(((u_hbm, u_ref), (xw_hbm, xw_ref), (dsig_hbm, dsig_ref)))
    ]
    for load in loads:
        load.start()
    prepare(part_ref, low_part, io_part)
    met(partners)
    gate_copy = remote(dgate_hbm, gate_land, hand_send.at[0], hand_recv.at[0], {"section": 1 - section})
    in_copy = remote(in_out, in_land, hand_send.at[1], hand_recv.at[1], {"section": 1 - section})

    sums = sum_start(low_part, io_part, low_land, io_land, sum_send, sum_recv)
    grad_load.wait()
    first = plane_start(step_grad, step_ring)

    @pl.when(section == 1)
    def _():
        gate_copy.start()

    shares = share_start(sums, part_ref, io_part, low_land, io_land, low_all, io_all, all_send, all_recv)
    small_there = spread_start(small_in, small_land, s_send, s_recv)
    first = plane_middle(step_grad, step_ring, first)
    share_finish(shares, low_all, io_all, wide)
    proj[...] = wide[...].astype(BF16)
    proj_t[...] = wide[...].T.astype(BF16)

    for load in loads:
        load.wait()

    def product(c, _):
        columns = pl.ds(pl.multiple_of(c * TILE, TILE), TILE)
        grad = jnp.dot(
            proj_t[: R + 2 * N, :], u_ref[:, columns], preferred_element_type=F32
        ).astype(BF16)
        x, y_high = c // 2, lax.rem(c, 2)
        for e in range(2):
            x_grad0[x, y_high, e] = grad[: X_ROWS[0], lanes(e)]
            x_grad1[2 * y_high + e, x // 2, lax.rem(x, 2)] = grad[X_ROWS[0] :, lanes(e)]
        return 0

    lax.fori_loop(0, CTX // 2, product, 0)
    first_x = plane_start(x_grad, x_ring)

    @pl.when(section == 1)
    def _():
        def one(j, _):
            columns = pl.ds(pl.multiple_of(j * TILE, TILE), TILE)
            in_out[:, columns] = (
                dsig_ref[:, columns]
                + lax.dot_general(
                    proj[:, : R + 2 * N], xw_ref[:, columns], (((1,), (0,)), ((), ())),
                    preferred_element_type=F32,
                )
            ).astype(BF16)
            return 0

        lax.fori_loop(0, u_ref.shape[1] // TILE, one, 0)
        in_copy.start()
        hin_ref[...] = jnp.zeros_like(hin_ref)
        hgate_ref[...] = jnp.zeros_like(hgate_ref)

    first_x = plane_middle(x_grad, x_ring, first_x)
    turned = plane_turn(step_grad, step_ring, first, left_half)
    for copy in small_there:
        copy.wait_recv()
    total = small_land[0]
    for c in range(1, CTX):
        total = total + small_land[c]
    small_all[me] = total
    small_home = []
    for d, to in enumerate(others("ctx", CTX)):
        small_home.append(remote(small_all.at[me], small_all.at[me], t_send.at[d], t_recv.at[d], to))
        small_home[-1].start()
    turned_x = plane_turn(x_grad, x_ring, first_x, top_half)
    turned = plane_second_middle(step_ring, turned)
    turned_x = plane_second_middle(x_ring, turned_x)
    for copy in small_home:
        copy.wait_recv()
    for c in range(CTX):
        gdecay_ref[:, lanes(c)] = small_all[c, :N]
        gbias_ref[:, lanes(c)] = small_all[c, N : N + 1]
        gskip_ref[:, lanes(c)] = small_all[c, N + 1 : N + 2]
    for q, halves in enumerate(plane_finish(step_ring, turned)):
        for h in range(2):
            gstep_ref[q * 16 : (q + 1) * 16, h * 1024 : (h + 1) * 1024] = halves[h]

    @pl.when(section == 0)
    def _():
        gate_copy.wait_recv()
        in_copy.wait_recv()
        hgate_ref[...] = gate_land[...]
        hin_ref[...] = in_land[...]

    for q, halves in enumerate(plane_finish(x_ring, turned_x)):
        for h in range(2):
            rows = X_ROWS[q] // 2
            gx_ref[q * X_ROWS[0] + h * rows : q * X_ROWS[0] + (h + 1) * rows, :] = halves[h]

    @pl.when(section == 1)
    def _():
        gate_copy.wait_send()
        in_copy.wait_send()

    for copy in sums + shares + small_there + small_home:
        copy.wait_send()
    for copies in first + turned + first_x + turned_x:
        ring_done(copies)


def run_tail(part, small, dgate, step_grad, u, xw, dsig):
    ch = u.shape[1]
    f = lambda *s: jax.ShapeDtypeStruct(s, F32)
    b = lambda *s: jax.ShapeDtypeStruct(s, BF16)
    return pl.pallas_call(
        tail,
        in_specs=in_vmem(2) + [pl.BlockSpec(memory_space=pl.ANY)] * 5,
        out_specs=in_vmem(7),
        out_shape=[
            b(TOK, ch), b(TOK, ch), f(R + 2 * N, LANE), f(32, ch), f(N, ch), f(1, ch), f(1, ch),
        ],
        scratch_shapes=sum_scratch(BF16)
        + [pltpu.VMEM((CTX, SMALL, LANE), F32)] * 3
        + [pltpu.SemaphoreType.DMA((CTX - 1,))] * 4
        + [pltpu.VMEM((TOK, ch), BF16)] * 3
        + [pltpu.SemaphoreType.DMA((2,))] * 2
        + [pltpu.VMEM((TOK, WIDE), BF16), pltpu.VMEM((WIDE, TOK), BF16)]
        + [pltpu.VMEM((SIDE, 2, 2, rows, LANE), BF16) for rows in X_ROWS]
        + [pltpu.VMEM(u.shape, BF16), pltpu.VMEM(xw.shape, BF16), pltpu.VMEM(dsig.shape, F32)]
        + [pltpu.VMEM(step_grad.shape, BF16), pltpu.SemaphoreType.DMA((4,))]
        + ring_scratch((2, 16, 2048), (16, 1024)) * 2
        + ring_scratch((2, X_ROWS[0], LANE), (X_ROWS[0] // 2, LANE))
        + ring_scratch((2, X_ROWS[1], LANE), (X_ROWS[1] // 2, LANE)),
        compiler_params=pltpu.CompilerParams(
            collective_id=2, has_side_effects=True, vmem_limit_bytes=VMEM_BYTES
        ),
        name="tail",
    )(part, small, dgate, step_grad, u, xw, dsig)


def finish(*refs):
    count = len(refs) // 2
    for k in range(count):
        refs[count + k][...] = refs[k][...]


def run_finish(*results):
    def rows(r):
        return pl.BlockSpec((r.shape[0] // SIDE, r.shape[1]), lambda j: (j, 0))

    def columns(r):
        return pl.BlockSpec((r.shape[0], r.shape[1] // SIDE), lambda j: (0, j))

    specs = [rows(r) for r in results[:4]] + [columns(r) for r in results[4:]]
    return pl.pallas_call(
        finish,
        grid=(SIDE,),
        in_specs=specs,
        out_specs=specs,
        out_shape=[jax.ShapeDtypeStruct(r.shape, r.dtype) for r in results],
        compiler_params=pltpu.CompilerParams(vmem_limit_bytes=VMEM_BYTES),
        name="finish",
    )(*results)


def body(mixer_input, gate_input, upstream_grad, x_weight, step_weight, step_bias, decay_log, skip_gain):
    u, z, g = mixer_input[0], gate_input[0], upstream_grad[0]
    weight_x, weight_step = jnp.swapaxes(x_weight[0], 0, 1), step_weight[0]
    dlog = decay_log[0]
    low, io = run_sum(u, weight_x)
    *kept, across = run_first(low, io, weight_step, step_bias, dlog, u, z, g)
    d_gate, d_signal, d_part, grad_step, small = run_second(
        low, io, weight_step, dlog, skip_gain, u, z, g, kept, across
    )
    handed_input, handed_gate, grad_x, grad_step, g_decay, g_bias, g_skip = run_finish(
        *run_tail(d_part, small, d_gate, grad_step, u, weight_x, d_signal)
    )
    return (
        handed_input[None], handed_gate[None], jnp.swapaxes(grad_x, 0, 1)[None], grad_step[None],
        g_bias, g_decay[None], g_skip,
    )


def solution(mesh):
    return jax.shard_map(
        body,
        mesh=mesh,
        in_specs=(
            P("section", "ctx", "ch"), P("section", "ctx", "ch"), P("section", "ctx", "ch"),
            P("section", "ch", None), P("section", None, "ch"), P("section", "ch"),
            P("section", None, "ch"), P("section", "ch"),
        ),
        out_specs=(
            P("section", "ctx", "ch"), P("section", "ctx", "ch"), P("section", ("ch", "ctx"), None),
            P("section", "ctx", "ch"), P("section", "ch"), P("section", None, "ch"), P("section", "ch"),
        ),
        check_vma=False,
    )
```

```python
import functools

import jax
import jax.numpy as jnp
from jax import lax
from jax.experimental import pallas as pl
from jax.experimental.pallas import tpu as pltpu
from jax.sharding import PartitionSpec as P

R = 512
N = 16
TOK = 192
STEPS = 24
ROWS = 8
TILE = 256
LANE = 128
HALVES = TILE // LANE
CHUNK = 4
VMEM_BYTES = 60 * 2**20
SIDE = 4
CTX = 16
CH = 8
PIECE = TOK // CH
WIDE = R + LANE
PACK = 40
SMALL = 24
MESH = pl.DeviceIdType.MESH
F32 = jnp.float32
BF16 = jnp.bfloat16


def every(i):
    return pl.ds(i, ROWS, stride=STEPS)


def lanes(k):
    return slice(k * LANE, (k + 1) * LANE)


def by_step(ref, value, by_token):
    for k in range(HALVES):
        by_token[k] = value[:, lanes(k)]
        for i in range(STEPS):
            ref[k, i] = by_token[k, every(i), :]


def from_step(ref, by_token):
    for k in range(HALVES):
        for i in range(STEPS):
            by_token[k, every(i), :] = ref[k, i]
    return jnp.concatenate([by_token[k] for k in range(HALVES)], axis=1)


def spread_columns(io_ref, spread):
    def one(i, _):
        rows = io_ref[every(i), :]
        for n in range(2 * N):
            spread[i, n] = jnp.broadcast_to(rows[:, n : n + 1], (ROWS, LANE))
        return 0

    lax.fori_loop(0, STEPS, one, 0)


def inverse(value):
    rough = pl.reciprocal(value, approx=True)
    return rough * (2.0 - value * rough)


def block_rows(s):
    return pl.ds(s, N, stride=ROWS)


def scan_blocks(decays, values, out_ref, k, reverse):
    state = jnp.zeros((N, LANE), F32)
    for s in reversed(range(ROWS)) if reverse else range(ROWS):
        out_ref[k, block_rows(s), :] = state
        state = decays[k, block_rows(s), :] * state + values[k, block_rows(s), :]
    return state


def first_pass(
    low_ref, io_ref, w_ref, bias_ref, dlog_ref, all_dlog_ref, u_ref, z_ref, g_ref,
    step_ref, token_ref, sig_ref, drive, seed, entry_ref, exit_ref, bsum_ref, across_ref,
    spread, by_drive, by_seed, by_step_size, rates,
    pack, landed, back, result, send, recv, back_send, back_recv,
    block_decay, block_end, block_start,
):
    tile = pl.program_id(0)
    last = pl.num_programs(0) - 1
    me = lax.axis_index("ctx")
    @pl.when(tile == 0)
    def _():
        greet(others("ctx", CTX))
        spread_columns(io_ref, spread)

    pre = jnp.dot(low_ref[...], w_ref[...], preferred_element_type=F32) + bias_ref[...]
    small = jnp.exp(-jnp.abs(pre))
    above = inverse(1.0 + small)
    series = small * (1.0 - small * (0.5 - small * (1.0 / 3.0)))
    step = jnp.maximum(pre, 0.0) + jnp.where(small < 1e-3, series, jnp.log(1.0 + small))
    sig_ref[...] = jnp.where(pre >= 0.0, above, small * above)
    z = z_ref[...].astype(F32)
    token_ref[...] = step
    by_step(step_ref, step, by_step_size)
    by_step(drive, step * u_ref[...].astype(F32), by_drive)
    by_step(seed, g_ref[...].astype(F32) * z * inverse(1.0 + jnp.exp(-z)), by_seed)
    rates[...] = -jnp.exp(dlog_ref[...])
    total = jnp.zeros((ROWS, TILE), F32)
    for i in range(STEPS):
        total = total + jnp.concatenate([step_ref[k, i] for k in range(HALVES)], axis=1)
    bsum_ref[...] = total
    whole_sum = jnp.sum(total, axis=0, keepdims=True)
    for k in range(HALVES):
        pack[HALVES * tile + k, 2 * N :, :] = jnp.broadcast_to(whole_sum[:, lanes(k)], (PACK - 2 * N, LANE))

    for c in range(N // CHUNK):
        pairs = [(n, k) for n in range(c * CHUNK, (c + 1) * CHUNK) for k in range(HALVES)]
        rate = [jnp.broadcast_to(rates[n : n + 1, lanes(k)], (ROWS, LANE)) for n, k in pairs]

        def one(i, carry):
            state, decay, start = carry
            st = [step_ref[k, i] for k in range(HALVES)]
            dr = [drive[k, i] for k in range(HALVES)]
            sd = [seed[k, i] for k in range(HALVES)]
            new_state, new_decay, new_start = [], [], []
            for p, (n, k) in enumerate(pairs):
                a = jnp.exp(st[k] * rate[p])
                new_state.append(a * state[p] + dr[k] * spread[i, n])
                d = a * decay[p]
                new_decay.append(d)
                new_start.append(start[p] + d * (sd[k] * spread[i, N + n]))
            return tuple(new_state), tuple(new_decay), tuple(new_start)

        zero = tuple(jnp.zeros((ROWS, LANE), F32) for _ in pairs)
        ones = tuple(jnp.ones((ROWS, LANE), F32) for _ in pairs)
        state, decay, start = lax.fori_loop(0, STEPS, one, (zero, ones, zero), unroll=STEPS)
        for p, (n, k) in enumerate(pairs):
            at = slice(n * ROWS, (n + 1) * ROWS)
            block_decay[k, at, :] = decay[p]
            block_end[k, at, :] = state[p]
            block_start[k, at, :] = start[p]

    for k in range(HALVES):
        pack[HALVES * tile + k, :N, :] = scan_blocks(block_decay, block_end, entry_ref, k, False)
        pack[HALVES * tile + k, N : 2 * N, :] = scan_blocks(block_decay, block_start, exit_ref, k, True)

    @pl.when(tile == 0)
    def _():
        met(others("ctx", CTX))

    def chunk_to(c):
        return remote(pack.at[c], landed.at[me], send.at[c], recv.at[me], {"ctx": c})

    def chunk_from(c):
        return remote(pack.at[c], landed.at[c], send.at[c], recv.at[c], {"ctx": c})

    def answers():
        return [
            remote(back.at[to["ctx"]], result.at[me], back_send.at[d], back_recv.at[d], to)
            for d, to in enumerate(others("ctx", CTX))
        ]

    for k in range(HALVES):
        c = HALVES * tile + k

        @pl.when(c != me)
        def _():
            chunk_to(c).start()

        @pl.when(c == me)
        def _():
            landed[me] = pack[me]

    @pl.when(tile == jnp.minimum(me // HALVES + 1, last))
    def _():
        for c in range(CTX):
            @pl.when(c != me)
            def _():
                chunk_from(c).wait_recv()

        mine = -jnp.exp(all_dlog_ref[:, pl.ds(pl.multiple_of(me * LANE, LANE), LANE)])
        state = jnp.zeros((N, LANE), F32)
        adjoint = jnp.zeros((N, LANE), F32)
        for c in range(CTX):
            r = CTX - 1 - c
            back[c, :N] = state
            back[r, N:] = adjoint
            state = jnp.exp(landed[c, 2 * N : 2 * N + 1] * mine) * state + landed[c, :N]
            adjoint = jnp.exp(landed[r, 2 * N : 2 * N + 1] * mine) * adjoint + landed[r, N : 2 * N]
        result[me] = back[me]
        for copy in answers():
            copy.start()

    @pl.when(tile == last)
    def _():
        for copy in answers():
            copy.wait_recv()
        across_ref[...] = result[...]
        for copy in answers():
            copy.wait_send()
        for c in range(CTX):
            @pl.when(c != me)
            def _():
                chunk_to(c).wait_send()


def sum_before(value, reverse):
    row = lax.broadcasted_iota(jnp.int32, value.shape, 0)
    held = value
    for k in (1, 2, 4):
        shift = ROWS - k if reverse else k
        inside = row < ROWS - k if reverse else row >= k
        held = held + jnp.where(inside, pltpu.roll(held, shift, 0), 0.0)
    return held - value


def second_pass(
    low_ref, io_ref, w_ref, dlog_ref, skip_ref, u_ref, z_ref, g_ref, step_ref, token_ref, sig_ref, drive, seed,
    entry_ref, exit_ref, bsum_ref, across_ref,
    dgate_ref, dsig_ref, part_ref, gstep_ref, small_ref,
    spread, sums, held, decays, scanned, grad_drive, grad_decay, by_scan, by_grad, by_decay, rates, by_token, low_t,
):
    tile = pl.program_id(0)

    @pl.when(tile == 0)
    def _():
        spread_columns(io_ref, spread)
        sums[...] = jnp.zeros_like(sums)
        part_ref[...] = jnp.zeros_like(part_ref)
        low_t[...] = low_ref[...].astype(F32).T.astype(BF16)

    rates[...] = -jnp.exp(dlog_ref[...])
    prior = sum_before(bsum_ref[...], False)
    later = sum_before(bsum_ref[...], True)

    def so_far(ref, c, i):
        if c == 0:
            return [jnp.zeros((ROWS, LANE), F32) for k in range(HALVES)]
        return [ref[k, i] for k in range(HALVES)]

    for c in range(N // CHUNK):
        numbers = range(c * CHUNK, (c + 1) * CHUNK)
        pairs = [(n, k) for n in numbers for k in range(HALVES)]
        rate = [jnp.broadcast_to(rates[n : n + 1, lanes(k)], (ROWS, LANE)) for n, k in pairs]

        def forward(i, state, c=c, numbers=numbers, rate=rate):
            st = [step_ref[k, i] for k in range(HALVES)]
            dr = [drive[k, i] for k in range(HALVES)]
            sd = [seed[k, i] for k in range(HALVES)]
            out = so_far(scanned, c, i)
            new = []
            for m, n in enumerate(numbers):
                b_in, b_out = spread[i, n], spread[i, N + n]
                d_out = sums[i, N + n]
                for k in range(HALVES):
                    p = m * HALVES + k
                    held[k, i, m] = state[p]
                    decay = jnp.exp(st[k] * rate[p])
                    decays[k, i, m] = decay
                    now = decay * state[p] + dr[k] * b_in
                    new.append(now)
                    out[k] = out[k] + b_out * now
                    d_out = d_out + sd[k] * now
                sums[i, N + n] = d_out
            for k in range(HALVES):
                scanned[k, i] = out[k]
            return tuple(new)

        state = tuple(
            entry_ref[k, n * ROWS : (n + 1) * ROWS, :]
            + jnp.exp(prior[:, lanes(k)] * rate[p]) * across_ref[k, n : n + 1, :]
            for p, (n, k) in enumerate(pairs)
        )
        lax.fori_loop(0, STEPS, forward, state, unroll=STEPS)

        def backward(j, carry, c=c, numbers=numbers, rate=rate):
            incoming, total = carry
            i = STEPS - 1 - j
            st = [step_ref[k, i] for k in range(HALVES)]
            dr = [drive[k, i] for k in range(HALVES)]
            sd = [seed[k, i] for k in range(HALVES)]
            g_drive = so_far(grad_drive, c, i)
            g_decay = so_far(grad_decay, c, i)
            new_in, new_total = [], []
            for m, n in enumerate(numbers):
                b_in, b_out = spread[i, n], spread[i, N + n]
                d_in = sums[i, n]
                for k in range(HALVES):
                    p = m * HALVES + k
                    adjoint = b_out * sd[k] + incoming[p]
                    passed = decays[k, i, m] * adjoint
                    pulled = passed * held[k, i, m]
                    new_in.append(passed)
                    new_total.append(total[p] + pulled * st[k])
                    g_decay[k] = g_decay[k] + pulled * rate[p]
                    g_drive[k] = g_drive[k] + adjoint * b_in
                    d_in = d_in + adjoint * dr[k]
                sums[i, n] = d_in
            for k in range(HALVES):
                grad_drive[k, i] = g_drive[k]
                grad_decay[k, i] = g_decay[k]
            return tuple(new_in), tuple(new_total)

        incoming = tuple(
            exit_ref[k, n * ROWS : (n + 1) * ROWS, :]
            + jnp.exp(later[:, lanes(k)] * rate[p]) * across_ref[k, N + n : N + n + 1, :]
            for p, (n, k) in enumerate(pairs)
        )
        zero = tuple(jnp.zeros((ROWS, LANE), F32) for _ in pairs)
        _, total = lax.fori_loop(0, STEPS, backward, (incoming, zero), unroll=STEPS)
        for p, (n, k) in enumerate(pairs):
            small_ref[k, n : n + 1, :] = (
                jnp.sum(total[p], axis=0, keepdims=True) * rates[n : n + 1, lanes(k)]
            )

    u = u_ref[...].astype(F32)
    z = z_ref[...].astype(F32)
    g = g_ref[...].astype(F32)
    gate_sig = inverse(1.0 + jnp.exp(-z))
    seeds = g * z * gate_sig
    skip = skip_ref[...]
    from_drive = from_step(grad_drive, by_grad)
    mixed = from_step(scanned, by_scan) + skip * u
    dgate_ref[...] = (g * mixed * gate_sig * (1.0 + z * (1.0 - gate_sig))).astype(BF16)
    dsig_ref[...] = from_drive * token_ref[...] + skip * seeds
    d_pre = (from_drive * u + from_step(grad_decay, by_decay)) * sig_ref[...]
    pre = d_pre.astype(BF16)
    bias_row = jnp.sum(d_pre, axis=0, keepdims=True)
    skip_row = jnp.sum(seeds * u, axis=0, keepdims=True)
    for k in range(HALVES):
        small_ref[k, N : N + 1, :] = bias_row[:, lanes(k)]
        small_ref[k, N + 1 : N + 2, :] = skip_row[:, lanes(k)]
        small_ref[k, N + 2 :, :] = jnp.zeros((SMALL - N - 2, LANE), F32)
    part_ref[:, :R] += lax.dot_general(
        pre, w_ref[...], (((1,), (1,)), ((), ())), preferred_element_type=F32
    )
    grad = jnp.dot(low_t[...], pre, preferred_element_type=F32).astype(BF16)
    for x in range(SIDE):
        for y in range(SIDE):
            at = (x * SIDE + y) * 2 * 16
            gstep_ref[0, x, y // 2, y % 2] = grad[at : at + 16]
            gstep_ref[1, y, x // 2, x % 2] = grad[at + 16 : at + 32]

    @pl.when(tile == pl.num_programs(0) - 1)
    def _():
        column = lax.broadcasted_iota(jnp.int32, (ROWS, LANE), 1)

        def one(i, _):
            rows = jnp.zeros((ROWS, LANE), F32)
            for n in range(2 * N):
                rows = jnp.where(column == n, jnp.sum(sums[i, n], axis=1, keepdims=True), rows)
            by_token[every(i), :] = rows
            return 0

        lax.fori_loop(0, STEPS, one, 0)
        part_ref[:, R:] = by_token[...]


def whole(*shape):
    return pl.BlockSpec(shape, lambda j: (0,) * len(shape))


def tiled(*lead):
    return pl.BlockSpec(lead + (TILE,), lambda j: (0,) * len(lead) + (j,))


def stacked(*rows):
    return pl.BlockSpec((HALVES,) + rows + (LANE,), lambda j: (j,) + (0,) * (len(rows) + 1))


def run_first(low, io, weight, bias, dlog, u, z, g):
    ch = u.shape[1]
    f = lambda *s: jax.ShapeDtypeStruct(s, F32)
    return pl.pallas_call(
        first_pass,
        grid=(ch // TILE,),
        in_specs=[
            whole(TOK, R), whole(TOK, io.shape[1]), tiled(R), tiled(1), tiled(N), whole(N, ch),
            tiled(TOK), tiled(TOK), tiled(TOK),
        ],
        out_specs=[
            stacked(STEPS, ROWS), tiled(TOK), tiled(TOK), stacked(STEPS, ROWS), stacked(STEPS, ROWS),
            stacked(N * ROWS), stacked(N * ROWS), tiled(ROWS), whole(CTX, 2 * N, LANE),
        ],
        out_shape=[
            f(ch // LANE, STEPS, ROWS, LANE), f(TOK, ch), f(TOK, ch), f(ch // LANE, STEPS, ROWS, LANE),
            f(ch // LANE, STEPS, ROWS, LANE),
            f(ch // LANE, N * ROWS, LANE), f(ch // LANE, N * ROWS, LANE),
            f(ROWS, ch), f(CTX, 2 * N, LANE),
        ],
        scratch_shapes=[
            pltpu.VMEM((STEPS, 2 * N, ROWS, LANE), F32),
            pltpu.VMEM((HALVES, TOK, LANE), F32),
            pltpu.VMEM((HALVES, TOK, LANE), F32),
            pltpu.VMEM((HALVES, TOK, LANE), F32),
            pltpu.VMEM((N, TILE), F32),
            pltpu.VMEM((CTX, PACK, LANE), F32),
            pltpu.VMEM((CTX, PACK, LANE), F32),
            pltpu.VMEM((CTX, 2 * N, LANE), F32),
            pltpu.VMEM((CTX, 2 * N, LANE), F32),
            pltpu.SemaphoreType.DMA((CTX,)),
            pltpu.SemaphoreType.DMA((CTX,)),
            pltpu.SemaphoreType.DMA((CTX - 1,)),
            pltpu.SemaphoreType.DMA((CTX - 1,)),
        ]
        + [pltpu.VMEM((HALVES, N * ROWS, LANE), F32)] * 3,
        compiler_params=pltpu.CompilerParams(
            collective_id=1, has_side_effects=True, vmem_limit_bytes=VMEM_BYTES
        ),
        name="first_pass",
    )(low, io, weight, bias, dlog, dlog, u, z, g)


def run_second(low, io, weight, dlog, skip, u, z, g, kept, across):
    ch = u.shape[1]
    f = lambda *s: jax.ShapeDtypeStruct(s, F32)
    return pl.pallas_call(
        second_pass,
        grid=(ch // TILE,),
        in_specs=[
            whole(TOK, R), whole(TOK, io.shape[1]), tiled(R), tiled(N), tiled(1),
            tiled(TOK), tiled(TOK), tiled(TOK), stacked(STEPS, ROWS), tiled(TOK), tiled(TOK),
            stacked(STEPS, ROWS), stacked(STEPS, ROWS), stacked(N * ROWS), stacked(N * ROWS), tiled(ROWS), stacked(2 * N),
        ],
        out_specs=[
            tiled(TOK), tiled(TOK), whole(TOK, WIDE), tiled(2, SIDE, 2, 2, 16), stacked(SMALL),
        ],
        out_shape=[
            jax.ShapeDtypeStruct((TOK, ch), BF16), f(TOK, ch), f(TOK, WIDE),
            jax.ShapeDtypeStruct((2, SIDE, 2, 2, 16, ch), BF16), f(ch // LANE, SMALL, LANE),
        ],
        scratch_shapes=[
            pltpu.VMEM((STEPS, 2 * N, ROWS, LANE), F32),
            pltpu.VMEM((STEPS, 2 * N, ROWS, LANE), F32),
            pltpu.VMEM((HALVES, STEPS, CHUNK, ROWS, LANE), F32),
            pltpu.VMEM((HALVES, STEPS, CHUNK, ROWS, LANE), F32),
        ]
        + [pltpu.VMEM((HALVES, STEPS, ROWS, LANE), F32)] * 3
        + [pltpu.VMEM((HALVES, TOK, LANE), F32)] * 3
        + [pltpu.VMEM((N, TILE), F32), pltpu.VMEM((TOK, LANE), F32), pltpu.VMEM((R, TOK), BF16)],
        compiler_params=pltpu.CompilerParams(vmem_limit_bytes=VMEM_BYTES),
        name="second_pass",
    )(low, io, weight, dlog, skip, u, z, g, *kept, across)


def greet(partners):
    for partner in partners:
        pl.semaphore_signal(
            pltpu.get_barrier_semaphore(), inc=1, device_id=partner, device_id_type=MESH
        )


def met(partners):
    pl.semaphore_wait(pltpu.get_barrier_semaphore(), len(partners))


def remote(src, dst, send, recv, to):
    return pltpu.make_async_remote_copy(
        src_ref=src, dst_ref=dst, send_sem=send, recv_sem=recv, device_id=to, device_id_type=MESH
    )


def others(axis, count):
    me = lax.axis_index(axis)
    return [{axis: lax.rem(me + d, count)} for d in range(1, count)]


def token_rows(owner):
    return pl.ds(pl.multiple_of(owner * PIECE, 8), PIECE)


def fold(rows):
    return rows[:ROWS] + pltpu.roll(rows[ROWS : 2 * ROWS], 2 * N, 1) + pltpu.roll(rows[2 * ROWS :], 4 * N, 1)


def unfold(folded):
    used = lax.broadcasted_iota(jnp.int32, (ROWS, LANE), 1) < 2 * N
    parts = [folded, pltpu.roll(folded, LANE - 2 * N, 1), pltpu.roll(folded, LANE - 4 * N, 1)]
    return jnp.concatenate([jnp.where(used, part, 0.0) for part in parts], axis=0)


def over(rows):
    return jnp.concatenate([rows[:, : R // 2], rows[:, R // 2 : R]], axis=0)


def prepare(part_ref, low_part, io_part):
    for p in range(CH):
        rows = part_ref[p * PIECE : (p + 1) * PIECE, :]
        low_part[p] = over(rows).astype(low_part.dtype)
        io_part[p] = fold(rows[:, R:])


def sum_start(low_part, io_part, low_land, io_land, send, recv):
    copies = []
    for d, to in enumerate(others("ch", CH)):
        copies.append(remote(low_part.at[to["ch"]], low_land.at[d], send.at[0, d], recv.at[0, d], to))
        copies.append(remote(io_part.at[to["ch"]], io_land.at[d], send.at[1, d], recv.at[1, d], to))
    for copy in copies:
        copy.start()
    return copies


def share_start(sums, part_ref, io_part, low_land, io_land, low_all, io_all, send, recv):
    me = lax.axis_index("ch")
    for copy in sums:
        copy.wait_recv()
    low = over(part_ref[token_rows(me), :])
    io = io_part[me]
    for d in range(CH - 1):
        low = low + low_land[d].astype(F32)
        io = io + io_land[d]
    low_all[me] = low.astype(BF16)
    io_all[me] = io
    copies = []
    for d, to in enumerate(others("ch", CH)):
        copies.append(remote(low_all.at[me], low_all.at[me], send.at[0, d], recv.at[0, d], to))
        copies.append(remote(io_all.at[me], io_all.at[me], send.at[1, d], recv.at[1, d], to))
    for copy in copies:
        copy.start()
    return copies


def share_finish(copies, low_all, io_all, wide):
    for copy in copies:
        copy.wait_recv()
    for p in range(CH):
        both = low_all[p].astype(F32)
        rows = slice(p * PIECE, (p + 1) * PIECE)
        wide[rows, : R // 2] = both[:PIECE]
        wide[rows, R // 2 : R] = both[PIECE:]
        wide[rows, R:] = unfold(io_all[p])


def sum_scratch(sent):
    return [
        pltpu.VMEM((CH, 2 * PIECE, R // 2), sent),
        pltpu.VMEM((CH, ROWS, LANE), F32),
        pltpu.VMEM((CH - 1, 2 * PIECE, R // 2), sent),
        pltpu.VMEM((CH - 1, ROWS, LANE), F32),
        pltpu.VMEM((CH, 2 * PIECE, R // 2), BF16),
        pltpu.VMEM((CH, ROWS, LANE), F32),
        pltpu.VMEM((TOK, WIDE), F32),
        pltpu.SemaphoreType.DMA((2, CH - 1)),
        pltpu.SemaphoreType.DMA((2, CH - 1)),
        pltpu.SemaphoreType.DMA((2, CH - 1)),
        pltpu.SemaphoreType.DMA((2, CH - 1)),
    ]


LOADS = 4


def sum_projected(u_hbm, xt_hbm, low_ref, io_ref, part_ref, u_ref, xt_ref, load_sem, *scratch):
    low_part, io_part, low_land, io_land, low_all, io_all, wide, sum_send, sum_recv, all_send, all_recv = scratch
    loads = []
    wide_piece = u_ref.shape[1] // LOADS
    for k in range(LOADS):
        columns = slice(k * wide_piece, (k + 1) * wide_piece)
        for m, (src, dst) in enumerate(((u_hbm, u_ref), (xt_hbm, xt_ref))):
            loads.append(
                pltpu.make_async_copy(src.at[:, columns], dst.at[:, columns], load_sem.at[m, k])
            )
            loads[-1].start()
    greet(others("ch", CH))
    total = jnp.zeros((TOK, R + 2 * N), F32)
    for k in range(LOADS):
        columns = slice(k * wide_piece, (k + 1) * wide_piece)
        loads[2 * k].wait()
        loads[2 * k + 1].wait()
        total = total + lax.dot_general(
            u_ref[:, columns], xt_ref[:, columns], (((1,), (1,)), ((), ())), preferred_element_type=F32
        )
    part_ref[:, R:] = jnp.zeros((TOK, LANE), F32)
    part_ref[:, : R + 2 * N] = total
    prepare(part_ref, low_part, io_part)
    met(others("ch", CH))
    sums = sum_start(low_part, io_part, low_land, io_land, sum_send, sum_recv)
    shares = share_start(sums, part_ref, io_part, low_land, io_land, low_all, io_all, all_send, all_recv)
    share_finish(shares, low_all, io_all, wide)
    low_ref[...] = wide[:, :R].astype(BF16)
    io_ref[...] = wide[:, R:]
    for copy in sums + shares:
        copy.wait_send()


def in_vmem(count):
    return [pl.BlockSpec(memory_space=pltpu.VMEM)] * count


def run_sum(u, xt):
    return pl.pallas_call(
        sum_projected,
        in_specs=[pl.BlockSpec(memory_space=pl.ANY)] * 2,
        out_specs=in_vmem(2),
        out_shape=[jax.ShapeDtypeStruct((TOK, R), BF16), jax.ShapeDtypeStruct((TOK, LANE), F32)],
        scratch_shapes=[
            pltpu.VMEM((TOK, WIDE), F32), pltpu.VMEM(u.shape, BF16), pltpu.VMEM(xt.shape, BF16),
            pltpu.SemaphoreType.DMA((2, LOADS)),
        ]
        + sum_scratch(F32),
        compiler_params=pltpu.CompilerParams(
            collective_id=0, has_side_effects=True, vmem_limit_bytes=VMEM_BYTES
        ),
        name="sum_projected",
    )(u, xt)


def spread_start(src, dst, send, recv):
    me = lax.axis_index("ctx")
    copies = []
    for d, to in enumerate(others("ctx", CTX)):
        copies.append(remote(src.at[to["ctx"]], dst.at[me], send.at[d], recv.at[d], to))
        copies[-1].start()
    dst[me] = src[me]
    return copies


def neighbour(axis, d):
    me = lax.axis_index("ctx")
    x, y = me // SIDE, lax.rem(me, SIDE)
    if axis == 0:
        return {"ctx": lax.rem(x + d + SIDE, SIDE) * SIDE + y}
    return {"ctx": x * SIDE + lax.rem(y + d + SIDE, SIDE)}


def place(axis, d=0):
    me = lax.axis_index("ctx")
    at = me // SIDE if axis == 0 else lax.rem(me, SIDE)
    return lax.rem(at + d + SIDE, SIDE)


WAYS = ((0, 1, 0), (1, -1, 1))


def ring_start(axis, src, relay, land, send, recv):
    passing, direct = [], []
    for way, d, half in WAYS:
        to = neighbour(axis, d)
        passing.append(remote(src.at[place(axis, 2), half], relay.at[way], send.at[0, way], recv.at[0, way], to))
        direct.append(
            remote(src.at[place(axis, d), 1 - half], land.at[way, 1 - half], send.at[1, way], recv.at[1, way], to)
        )
        passing[-1].start()
    for copy in direct:
        copy.start()
    return passing, direct


def ring_middle(axis, src, relay, land, send, recv, copies):
    passing, direct = copies
    last = []
    for way, d, half in WAYS:
        passing[way].wait_recv()
        mine = src[place(axis, d), half]
        relay[way] = (relay[way].astype(F32) + mine.astype(F32)).astype(BF16)
        last.append(
            remote(relay.at[way], land.at[way, half], send.at[2, way], recv.at[2, way], neighbour(axis, d))
        )
        last[-1].start()
    return passing, direct, last


def ring_finish(axis, src, land, copies):
    _, direct, last = copies
    for copy in direct + last:
        copy.wait_recv()
    mine = place(axis)
    return [
        src[mine, h].astype(F32) + land[0, h].astype(F32) + land[1, h].astype(F32) for h in range(2)
    ]


def ring_done(copies):
    for group in copies:
        for copy in group:
            copy.wait_send()


RING = 9


def ring_scratch(unit, second):
    return [
        pltpu.VMEM((2,) + unit, BF16),
        pltpu.VMEM((2, 2) + unit, BF16),
        pltpu.VMEM((SIDE, 2) + second, BF16),
        pltpu.VMEM((2,) + second, BF16),
        pltpu.VMEM((2, 2) + second, BF16),
        pltpu.SemaphoreType.DMA((3, 2)),
        pltpu.SemaphoreType.DMA((3, 2)),
        pltpu.SemaphoreType.DMA((3, 2)),
        pltpu.SemaphoreType.DMA((3, 2)),
    ]


def plane_start(src, rings):
    started = []
    for q, (relay, land, _, _, _, send, recv, _, _) in enumerate(rings):
        started.append(ring_start(q, src[q], relay, land, send, recv))
    return started


def plane_middle(src, rings, copies):
    passed = []
    for q, (relay, land, _, _, _, send, recv, _, _) in enumerate(rings):
        passed.append(ring_middle(q, src[q], relay, land, send, recv, copies[q]))
    return passed


def plane_turn(src, rings, copies, split):
    started = []
    for q, (_, land, second, relay, land2, _, _, send, recv) in enumerate(rings):
        halves = ring_finish(q, src[q], land, copies[q])
        for o in range(SIDE):
            for h in range(2):
                second[o, h] = split(halves[o // 2][o % 2], h).astype(BF16)
        started.append(ring_start(1 - q, second, relay, land2, send, recv))
    return started


def plane_second_middle(rings, copies):
    passed = []
    for q, (_, _, second, relay, land2, _, _, send, recv) in enumerate(rings):
        passed.append(ring_middle(1 - q, second, relay, land2, send, recv, copies[q]))
    return passed


def plane_finish(rings, copies):
    return [ring_finish(1 - q, rings[q][2], rings[q][4], copies[q]) for q in range(2)]


def left_half(value, h):
    columns = value.shape[1] // 2
    return value[:, h * columns : (h + 1) * columns]


def top_half(value, h):
    rows = value.shape[0] // 2
    return value[h * rows : (h + 1) * rows]


X_ROWS = (288, 256)


def tail(
    part_ref, small_in, dgate_hbm, grad_hbm, u_hbm, xw_hbm, dsig_hbm,
    hin_ref, hgate_ref, gx_ref, gstep_ref, gdecay_ref, gbias_ref, gskip_ref,
    low_part, io_part, low_land, io_land, low_all, io_all, wide, sum_send, sum_recv, all_send, all_recv,
    small_land, small_back, small_all, s_send, s_recv, t_send, t_recv,
    gate_land, in_out, in_land, hand_send, hand_recv, proj, proj_t, x_grad0, x_grad1,
    u_ref, xw_ref, dsig_ref, step_grad, load_sem, *scratch,
):
    rings = [scratch[k * RING : (k + 1) * RING] for k in range(4)]
    step_ring, x_ring = rings[:2], rings[2:]
    grad_load = pltpu.make_async_copy(grad_hbm, step_grad, load_sem.at[3])
    step_grad = [step_grad.at[q] for q in range(2)]
    x_grad = [x_grad0, x_grad1]
    section = lax.axis_index("section")
    me = lax.axis_index("ctx")
    partners = others("ctx", CTX) + others("ch", CH) + [{"section": 1 - section}]
    grad_load.start()
    greet(partners)
    loads = [
        pltpu.make_async_copy(src, dst, load_sem.at[k])
        for k, (src, dst) in enumerate(((u_hbm, u_ref), (xw_hbm, xw_ref), (dsig_hbm, dsig_ref)))
    ]
    for load in loads:
        load.start()
    prepare(part_ref, low_part, io_part)
    met(partners)
    gate_copy = remote(dgate_hbm, gate_land, hand_send.at[0], hand_recv.at[0], {"section": 1 - section})
    in_copy = remote(in_out, in_land, hand_send.at[1], hand_recv.at[1], {"section": 1 - section})

    sums = sum_start(low_part, io_part, low_land, io_land, sum_send, sum_recv)
    grad_load.wait()
    first = plane_start(step_grad, step_ring)

    @pl.when(section == 1)
    def _():
        gate_copy.start()

    shares = share_start(sums, part_ref, io_part, low_land, io_land, low_all, io_all, all_send, all_recv)
    small_there = spread_start(small_in, small_land, s_send, s_recv)
    first = plane_middle(step_grad, step_ring, first)
    share_finish(shares, low_all, io_all, wide)
    proj[...] = wide[...].astype(BF16)
    proj_t[...] = wide[...].T.astype(BF16)

    for load in loads:
        load.wait()

    def product(c, _):
        columns = pl.ds(pl.multiple_of(c * TILE, TILE), TILE)
        grad = jnp.dot(
            proj_t[: R + 2 * N, :], u_ref[:, columns], preferred_element_type=F32
        ).astype(BF16)
        x, y_high = c // 2, lax.rem(c, 2)
        for e in range(2):
            x_grad0[x, y_high, e] = grad[: X_ROWS[0], lanes(e)]
            x_grad1[2 * y_high + e, x // 2, lax.rem(x, 2)] = grad[X_ROWS[0] :, lanes(e)]
        return 0

    lax.fori_loop(0, CTX // 2, product, 0)
    first_x = plane_start(x_grad, x_ring)

    @pl.when(section == 1)
    def _():
        def one(j, _):
            columns = pl.ds(pl.multiple_of(j * TILE, TILE), TILE)
            in_out[:, columns] = (
                dsig_ref[:, columns]
                + lax.dot_general(
                    proj[:, : R + 2 * N], xw_ref[:, columns], (((1,), (0,)), ((), ())),
                    preferred_element_type=F32,
                )
            ).astype(BF16)
            return 0

        lax.fori_loop(0, u_ref.shape[1] // TILE, one, 0)
        in_copy.start()
        hin_ref[...] = jnp.zeros_like(hin_ref)
        hgate_ref[...] = jnp.zeros_like(hgate_ref)

    first_x = plane_middle(x_grad, x_ring, first_x)
    turned = plane_turn(step_grad, step_ring, first, left_half)
    turned_x = plane_turn(x_grad, x_ring, first_x, top_half)
    for copy in small_there:
        copy.wait_recv()
    total = small_land[0]
    for c in range(1, CTX):
        total = total + small_land[c]
    small_all[me] = total
    small_home = []
    for d, to in enumerate(others("ctx", CTX)):
        small_home.append(remote(small_all.at[me], small_all.at[me], t_send.at[d], t_recv.at[d], to))
        small_home[-1].start()
    turned = plane_second_middle(step_ring, turned)
    turned_x = plane_second_middle(x_ring, turned_x)
    for copy in small_home:
        copy.wait_recv()
    for c in range(CTX):
        gdecay_ref[:, lanes(c)] = small_all[c, :N]
        gbias_ref[:, lanes(c)] = small_all[c, N : N + 1]
        gskip_ref[:, lanes(c)] = small_all[c, N + 1 : N + 2]
    for q, halves in enumerate(plane_finish(step_ring, turned)):
        for h in range(2):
            gstep_ref[q * 16 : (q + 1) * 16, h * 1024 : (h + 1) * 1024] = halves[h]

    @pl.when(section == 0)
    def _():
        gate_copy.wait_recv()
        in_copy.wait_recv()
        hgate_ref[...] = gate_land[...]
        hin_ref[...] = in_land[...]

    for q, halves in enumerate(plane_finish(x_ring, turned_x)):
        for h in range(2):
            rows = X_ROWS[q] // 2
            gx_ref[q * X_ROWS[0] + h * rows : q * X_ROWS[0] + (h + 1) * rows, :] = halves[h]

    @pl.when(section == 1)
    def _():
        gate_copy.wait_send()
        in_copy.wait_send()

    for copy in sums + shares + small_there + small_home:
        copy.wait_send()
    for copies in first + turned + first_x + turned_x:
        ring_done(copies)


def run_tail(part, small, dgate, step_grad, u, xw, dsig):
    ch = u.shape[1]
    f = lambda *s: jax.ShapeDtypeStruct(s, F32)
    b = lambda *s: jax.ShapeDtypeStruct(s, BF16)
    return pl.pallas_call(
        tail,
        in_specs=in_vmem(2) + [pl.BlockSpec(memory_space=pl.ANY)] * 5,
        out_specs=in_vmem(7),
        out_shape=[
            b(TOK, ch), b(TOK, ch), f(R + 2 * N, LANE), f(32, ch), f(N, ch), f(1, ch), f(1, ch),
        ],
        scratch_shapes=sum_scratch(BF16)
        + [pltpu.VMEM((CTX, SMALL, LANE), F32)] * 3
        + [pltpu.SemaphoreType.DMA((CTX - 1,))] * 4
        + [pltpu.VMEM((TOK, ch), BF16)] * 3
        + [pltpu.SemaphoreType.DMA((2,))] * 2
        + [pltpu.VMEM((TOK, WIDE), BF16), pltpu.VMEM((WIDE, TOK), BF16)]
        + [pltpu.VMEM((SIDE, 2, 2, rows, LANE), BF16) for rows in X_ROWS]
        + [pltpu.VMEM(u.shape, BF16), pltpu.VMEM(xw.shape, BF16), pltpu.VMEM(dsig.shape, F32)]
        + [pltpu.VMEM(step_grad.shape, BF16), pltpu.SemaphoreType.DMA((4,))]
        + ring_scratch((2, 16, 2048), (16, 1024)) * 2
        + ring_scratch((2, X_ROWS[0], LANE), (X_ROWS[0] // 2, LANE))
        + ring_scratch((2, X_ROWS[1], LANE), (X_ROWS[1] // 2, LANE)),
        compiler_params=pltpu.CompilerParams(
            collective_id=2, has_side_effects=True, vmem_limit_bytes=VMEM_BYTES
        ),
        name="tail",
    )(part, small, dgate, step_grad, u, xw, dsig)


def finish(*refs):
    count = len(refs) // 2
    for k in range(count):
        refs[count + k][...] = refs[k][...]


def run_finish(*results):
    return pl.pallas_call(
        finish,
        in_specs=in_vmem(len(results)),
        out_specs=in_vmem(len(results)),
        out_shape=[jax.ShapeDtypeStruct(r.shape, r.dtype) for r in results],
        compiler_params=pltpu.CompilerParams(vmem_limit_bytes=VMEM_BYTES),
        name="finish",
    )(*results)


def body(mixer_input, gate_input, upstream_grad, x_weight, step_weight, step_bias, decay_log, skip_gain):
    u, z, g = mixer_input[0], gate_input[0], upstream_grad[0]
    weight_x, weight_step = jnp.swapaxes(x_weight[0], 0, 1), step_weight[0]
    dlog = decay_log[0]
    low, io = run_sum(u, weight_x)
    *kept, across = run_first(low, io, weight_step, step_bias, dlog, u, z, g)
    d_gate, d_signal, d_part, grad_step, small = run_second(
        low, io, weight_step, dlog, skip_gain, u, z, g, kept, across
    )
    handed_input, handed_gate, grad_x, grad_step, g_decay, g_bias, g_skip = run_finish(
        *run_tail(d_part, small, d_gate, grad_step, u, weight_x, d_signal)
    )
    return (
        handed_input[None], handed_gate[None], jnp.swapaxes(grad_x, 0, 1)[None], grad_step[None],
        g_bias, g_decay[None], g_skip,
    )


def solution(mesh):
    return jax.shard_map(
        body,
        mesh=mesh,
        in_specs=(
            P("section", "ctx", "ch"), P("section", "ctx", "ch"), P("section", "ctx", "ch"),
            P("section", "ch", None), P("section", None, "ch"), P("section", "ch"),
            P("section", None, "ch"), P("section", "ch"),
        ),
        out_specs=(
            P("section", "ctx", "ch"), P("section", "ctx", "ch"), P("section", ("ch", "ctx"), None),
            P("section", "ctx", "ch"), P("section", "ch"), P("section", None, "ch"), P("section", "ch"),
        ),
        check_vma=False,
    )
```
